32 devices in a mesh: ctx: 2 (over core), dp: 16 (over z, y, x).
Axes of the slice: x: 2, y: 2, z: 4, core: 2. Of those that a mesh axis runs over, the one named last changes fastest.
Arguments:
- inputs: bfloat16 [16, 256, 2048], P('dp', 'ctx'), may hold values from -8 to 8
- values: bfloat16 [16, 256, 2048], P('dp', 'ctx'), may hold values from -6 to 6
- gating: bfloat16 [16, 256, 2048], P('dp', 'ctx'), may hold values from -6 to 6
- out_grad: bfloat16 [16, 256, 2048], P('dp', 'ctx'), may hold values from -6 to 6
- weight: bfloat16 [2048, 2048], P('dp'), may hold values from -0.125 to 0.125
- decay_rate: float32 [16, 2048], replicated, may hold values from 0.001953125 to 0.08
- mode_gain: float32 [16, 2048], replicated, may hold values from -1.75 to 1.75
Outputs:
- in_grad: float32 [16, 256, 2048], P('dp', 'ctx')
- gate_grad: float32 [16, 256, 2048], P('dp', 'ctx')
- weight_grad: float32 [2048, 2048], P('dp')
The draws below stay inside these ranges and needn't reach their ends.
All inputs are finite; a program needn't handle non-finite values.
Results may differ from the reference program's by a relative error of at most 0.003.
Values may be sent and summed in bfloat16 or wider, within the bound.
A program may use at most 128 MiB of HBM per device.

```python
import math
import jax
import jax.numpy as jnp
from jax import lax

D = 2048
C = 2048
MODES = 16
SEQ = 256
SEQS = 16


def spiked(values, own_key, source, target, parts, factor):
    def block_of(axis_at):
        return (jnp.arange(values.shape[axis_at]) // (values.shape[axis_at] // parts)).reshape((-1,) + (1,) * (values.ndim - 1 - axis_at))

    first = jax.random.permutation(own_key, parts)[block_of(target)]
    second = (block_of(target) + parts // 2) % parts
    return jnp.where((block_of(source) == first) | (block_of(source) == second), factor * values, values)


def steps_of(rng, dims, pieces, least, largest):
    level = 1.0
    for axis_at, blocks in pieces:
        steps = jax.random.uniform(jax.random.fold_in(jax.random.fold_in(rng, 6), axis_at), (blocks,), jnp.float32, least / len(pieces), largest / len(pieces))
        level = level * jnp.repeat(jnp.exp(steps), dims[axis_at] // blocks).reshape((-1,) + (1,) * (len(dims) - 1 - axis_at))
    return level


def scatter_about(rng, extent, width, bound, split=(), dtype=jnp.bfloat16):
    drawn = width * jax.random.normal(rng, extent, jnp.float32)
    if split:
        drawn = drawn * steps_of(rng, extent, split, -0.22, 0.18)
    return jnp.clip(drawn, -bound, bound).astype(dtype)


def gaussian_with(stream_key, dims, width, most, shards, heavy, dtype=jnp.bfloat16):
    values = width * jax.random.normal(stream_key, dims, jnp.float32)
    if shards:
        values = values * steps_of(stream_key, dims, shards, -0.22, 0.18)
    return jnp.clip(spiked(values, jax.random.fold_in(stream_key, 3), *heavy), -most, most).astype(dtype)


def setup_inputs(seed: int = 0) -> dict:
    streams_of = jax.random.split(jax.random.key(seed), 8)
    return {
        "inputs": gaussian_with(streams_of[0], (SEQS, SEQ, D), 1.0, 8.0, ((0, 16), (1, 2)), (0, 2, 16, 2.0)),
        "values": scatter_about(streams_of[1], (SEQS, SEQ, C), 1.0, 6.0, ((0, 16), (1, 2))),
        "gating": scatter_about(streams_of[2], (SEQS, SEQ, C), 1.0, 6.0, ((0, 16), (1, 2))),
        "out_grad": scatter_about(streams_of[3], (SEQS, SEQ, C), 1.0, 6.0, ((0, 16), (1, 2))),
        "weight": scatter_about(streams_of[4], (D, C), C ** -0.5, 0.125, ((0, 16),)),
        "decay_rate": jnp.clip(jnp.exp(jax.random.uniform(streams_of[5], (MODES, C), jnp.float32, math.log(0.001953125), math.log(0.08))), 0.001953125, 0.08),
        "mode_gain": scatter_about(streams_of[6], (MODES, C), 0.3, 1.75, (), jnp.float32),
    }


def modal_scan(series, lam, mode_coef, reverse):

    def advance(state, column):
        state = lam[None] * state + column[:, None, :]
        return (state, lax.optimization_barrier(jnp.sum(mode_coef[None] * state, axis=1)))
    initial = jnp.zeros((series.shape[0],) + lam.shape, jnp.float32)
    _, result = lax.scan(advance, initial, jnp.swapaxes(series, 0, 1), reverse=reverse)
    return jnp.swapaxes(result, 0, 1)

def reference(inputs, values, gating, out_grad, weight, decay_rate, mode_gain):
    lam = jnp.exp(-decay_rate)
    mode_coef = mode_gain * jnp.sqrt(-jnp.expm1(-2.0 * decay_rate))
    mixed = modal_scan(values.astype(jnp.float32), lam, mode_coef, False)
    gate_grad = out_grad.astype(jnp.float32) * mixed
    mix_grad = gating.astype(jnp.float32) * out_grad.astype(jnp.float32)
    val_grad = modal_scan(mix_grad, lam, mode_coef, True).astype(jnp.bfloat16)
    flat_grad = val_grad.reshape(-1, C).astype(jnp.float32)
    flat_in = inputs.reshape(-1, D).astype(jnp.float32)
    weight_full = weight.astype(jnp.float32)
    in_grad = lax.dot_general(flat_grad, weight_full, (((1,), (1,)), ((), ())), precision=lax.Precision.HIGHEST, preferred_element_type=jnp.float32)
    in_grad = in_grad.reshape(SEQS, SEQ, D)
    weight_grad = lax.dot_general(flat_in, flat_grad, (((0,), (0,)), ((), ())), precision=lax.Precision.HIGHEST, preferred_element_type=jnp.float32)
    weight_grad = weight_grad / jnp.sqrt(jnp.float32(SEQS * SEQ))
    return (in_grad, gate_grad, weight_grad)
```

```python
import functools
import math

import jax
import jax.numpy as jnp
from jax import lax
from jax.experimental import pallas as pl
from jax.experimental.pallas import tpu as pltpu
from jax.sharding import PartitionSpec as P

MESH = pl.DeviceIdType.MESH
F32 = jnp.float32
BF16 = jnp.bfloat16
LANES = 128
RUN = 16
RUNS = 8
ROWS = RUN * RUNS
NZ = 4

IN_COPY, BACK_COPY, FWD_COPY, VAL_COPY, IG_COPY, WG_COPY = range(6)
AG_Z, AG_X, AG_Y, AG_A, AG_B, RS_A, RS_B, RS_X, RS_Y, RS_Z = range(6, 46, 4)
COPIES = 46


def dot(lhs, rhs, lhs_dim, rhs_dim):
    return lax.dot_general(
        lhs, rhs, (((lhs_dim,), (rhs_dim,)), ((), ())), preferred_element_type=F32
    )


def lanes_of(tile):
    return pl.ds(pl.multiple_of(tile * LANES, LANES), LANES)


def run_rows(step):
    return pl.ds(step, RUNS, RUN)


def row_index():
    return lax.broadcasted_iota(jnp.int32, (RUNS, LANES), 0)


def shifted_runs(state, by, reverse):
    rows = row_index()
    if reverse:
        return jnp.where(rows < RUNS - by, pltpu.roll(state, RUNS - by, 0), 0.0)
    return jnp.where(rows >= by, pltpu.roll(state, by, 0), 0.0)


def spread(row):
    return jnp.broadcast_to(row, (RUNS, LANES))


def modes_of(decay_ref, coef_ref, tile):
    decay = decay_ref[:, lanes_of(tile)]
    lam = jnp.exp(-decay)
    coef = coef_ref[:, lanes_of(tile)]
    return decay, lam, coef


def run_states(series, decay, lam, states, ends, tile, reverse):
    order = range(RUN - 1, -1, -1) if reverse else range(RUN)
    steps = [series[tile, run_rows(step), :] for step in order]
    over_run = jnp.exp(-float(RUN) * decay)
    for mode in range(decay.shape[0]):
        rate = spread(lam[mode : mode + 1])
        state = steps[0]
        for column in steps[1:]:
            state = rate * state + column
        span = spread(over_run[mode : mode + 1])
        for by in (1, 2, 4):
            state = state + span * shifted_runs(state, by, reverse)
            span = span * span
        states[tile, mode] = state
        last = 0 if reverse else RUNS - 1
        ends[tile, mode : mode + 1, :] = state[last : last + 1]


def run_outputs(series, impulse, decay, lam, coef, states, incoming, enters, result, tile, reverse):
    order = list(range(RUN - 1, -1, -1) if reverse else range(RUN))
    steps = [series[tile, run_rows(step), :] for step in order]
    lags = [spread(impulse[tile, lag : lag + 1, :]) for lag in range(RUN)]
    ahead = row_index()
    ahead = (RUNS - 1 - ahead if reverse else ahead).astype(F32) * float(RUN)
    rates, carried = [], []
    for mode in range(decay.shape[0]):
        rate = spread(lam[mode : mode + 1])
        entry = jnp.where(enters, spread(incoming[tile, mode : mode + 1, :]), 0.0)
        prior = shifted_runs(states[tile, mode], 1, reverse)
        prior = prior + jnp.exp(-ahead * spread(decay[mode : mode + 1])) * entry
        rates.append(rate)
        carried.append(spread(coef[mode : mode + 1]) * rate * prior)
    for at, step in enumerate(order):
        terms = [lags[at - back] * steps[back] for back in range(at + 1)] + carried
        while len(terms) > 1:
            odd = terms[-1:] if len(terms) % 2 else []
            terms = [a + b for a, b in zip(terms[::2], terms[1::2])] + odd
        result[tile, run_rows(step), :] = terms[0]
        carried = [rate * item for rate, item in zip(rates, carried)]


def chip_kernel(
    scale,
    in_ref, values_ref, gating_ref, grad_ref, weight_ref, decay_ref, coef_ref,
    ig_ref, gate_ref, wg_ref,
    series_f, series_b, result, impulse, states_f, states_b,
    ends_f, ends_b, enter_f, enter_b,
    in_full, val_full, val_send, wfull,
    s1, r1a, r1b, s2x, s2y, r2x, r2y, s3, r3,
    ig_send, ig_recv, wg_send, wg_recv,
    send_sem, recv_sem,
):
    core = lax.axis_index("ctx")
    dp = lax.axis_index("dp")
    z, y, x = dp // 4, (dp // 2) % 2, dp % 2
    tiles = series_f.shape[0]
    half_tiles = tiles // 2
    half = half_tiles * LANES
    block = weight_ref.shape[0]
    mid = block // 2

    def chip(cz, cy, cx):
        return cz * 4 + cy * 2 + cx

    sibling = (1 - core, dp)
    x_dev = (core, chip(z, y, 1 - x))
    y_dev = (core, chip(z, 1 - y, x))

    def z_dev(hop):
        return (core, chip((z + hop) % NZ, y, x))

    def copy(src, dst, which, device):
        return pltpu.make_async_remote_copy(
            src_ref=src, dst_ref=dst, send_sem=send_sem.at[which], recv_sem=recv_sem.at[which],
            device_id=device, device_id_type=MESH,
        )

    barrier = pltpu.get_barrier_semaphore()
    partners = [sibling, x_dev, y_dev] + [z_dev(hop) for hop in range(1, NZ)]
    for device in partners:
        pl.semaphore_signal(barrier, inc=1, device_id=device, device_id_type=MESH)
    pl.semaphore_wait(barrier, len(partners))

    def wrows(index, start=0, size=block):
        return wfull.at[pl.ds(pl.multiple_of(index * block + start, mid), size), :]

    own_half = pl.ds(pl.multiple_of(core * half, half), half)
    other_half = pl.ds(pl.multiple_of((1 - core) * half, half), half)
    own_rows = pl.ds(pl.multiple_of(core * ROWS, ROWS), ROWS)

    wrows(dp)[...] = weight_ref[:, own_half]

    def ag_z(hop):
        return copy(wrows(dp), wrows(dp), AG_Z + hop, z_dev(hop))

    def ag_x(hop):
        rows = wrows(chip((z - hop + NZ) % NZ, y, x))
        return copy(rows, rows, AG_X + hop, x_dev)

    def ag_y(hop):
        rows = wrows(chip((z - hop + NZ) % NZ, y, x))
        return copy(rows, rows, AG_Y + hop, y_dev)

    def ag_a(hop):
        rows = wrows(chip((z - hop + NZ) % NZ, y, 1 - x), 0, mid)
        return copy(rows, rows, AG_A + hop, y_dev)

    def ag_b(hop):
        rows = wrows(chip((z - hop + NZ) % NZ, 1 - y, x), mid, mid)
        return copy(rows, rows, AG_B + hop, x_dev)

    for hop in (1, 3, 2):
        ag_z(hop).start()
    ag_x(0).start()
    ag_y(0).start()
    in_copy = copy(in_ref, in_full.at[own_rows, :], IN_COPY, sibling)
    in_copy.start()
    in_full[own_rows, :] = in_ref[...]

    def back_states(tile, carry):
        lanes = lanes_of(tile)
        series_b[tile] = gating_ref[:, lanes].astype(F32) * grad_ref[:, lanes].astype(F32)
        decay, lam, coef = modes_of(decay_ref, coef_ref, tile)
        power = coef
        for lag in range(RUN):
            impulse[tile, lag : lag + 1, :] = jnp.sum(power, axis=0, keepdims=True)
            power = power * lam
        run_states(series_b, decay, lam, states_b, ends_b, tile, True)
        return carry

    def fwd_states(tile, carry):
        series_f[tile] = values_ref[:, lanes_of(tile)].astype(F32)
        decay, lam, coef = modes_of(decay_ref, coef_ref, tile)
        run_states(series_f, decay, lam, states_f, ends_f, tile, False)
        return carry

    lax.fori_loop(0, tiles, back_states, 0)
    back_copy = copy(ends_b, enter_b, BACK_COPY, sibling)
    back_copy.start()
    lax.fori_loop(0, tiles, fwd_states, 0)
    fwd_copy = copy(ends_f, enter_f, FWD_COPY, sibling)
    fwd_copy.start()
    back_copy.wait_recv()

    def val_tile(tile):
        decay, lam, coef = modes_of(decay_ref, coef_ref, tile)
        run_outputs(
            series_b, impulse, decay, lam, coef, states_b, enter_b, core == 0, result, tile, True
        )
        return result[tile].astype(BF16)

    def val_other(tile, carry):
        val_send[:, lanes_of(tile)] = val_tile((1 - core) * half_tiles + tile)
        return carry

    def val_own(tile, carry):
        val_full[own_rows, lanes_of(tile)] = val_tile(core * half_tiles + tile)
        return carry

    lax.fori_loop(0, half_tiles, val_other, 0)
    val_copy = copy(val_send, val_full.at[own_rows, :], VAL_COPY, sibling)
    val_copy.start()
    lax.fori_loop(0, half_tiles, val_own, 0)
    in_copy.wait_recv()
    val_copy.wait_recv()

    def term(index):
        columns = pl.ds(pl.multiple_of(index * block, block), block)
        return dot(in_full[:, columns], val_full[...], 0, 0)

    def rs_a(hop):
        return copy(s1.at[hop, pl.ds(0, mid), :], r1a.at[hop], RS_A + hop, y_dev)

    def rs_b(hop):
        return copy(s1.at[hop, pl.ds(mid, mid), :], r1b.at[hop], RS_B + hop, x_dev)

    def rs_x(hop):
        return copy(s2x.at[hop], r2x.at[hop], RS_X + hop, x_dev)

    def rs_y(hop):
        return copy(s2y.at[hop], r2y.at[hop], RS_Y + hop, y_dev)

    def rs_z(hop):
        return copy(s3.at[hop], r3.at[hop], RS_Z + hop, z_dev(hop))

    def rs_first(hop, carry):
        s1[hop] = term(chip((z + hop) % NZ, 1 - y, 1 - x)).astype(BF16)
        rs_a(hop).start()
        rs_b(hop).start()
        return carry

    lax.fori_loop(0, NZ, rs_first, 0)

    def ag_second(hop, carry):
        ag_z(hop).wait_recv()
        ag_x(hop).start()
        ag_y(hop).start()
        return carry

    def rs_second(hop, carry):
        to_x = term(chip((z + hop) % NZ, y, 1 - x))
        rs_a(hop).wait_recv()
        s2x[hop, pl.ds(0, mid), :] = (to_x[:mid] + r1a[hop].astype(F32)).astype(BF16)
        s2x[hop, pl.ds(mid, mid), :] = to_x[mid:].astype(BF16)
        rs_x(hop).start()
        to_y = term(chip((z + hop) % NZ, 1 - y, x))
        rs_b(hop).wait_recv()
        s2y[hop, pl.ds(0, mid), :] = to_y[:mid].astype(BF16)
        s2y[hop, pl.ds(mid, mid), :] = (to_y[mid:] + r1b[hop].astype(F32)).astype(BF16)
        rs_y(hop).start()
        return carry

    lax.fori_loop(0, NZ, rs_second, 0)
    lax.fori_loop(1, NZ, ag_second, 0)

    fwd_copy.wait_recv()

    def gate_tile(tile, carry):
        decay, lam, coef = modes_of(decay_ref, coef_ref, tile)
        run_outputs(
            series_f, impulse, decay, lam, coef, states_f, enter_f, core == 1, result, tile, False
        )
        lanes = lanes_of(tile)
        gate_ref[:, lanes] = grad_ref[:, lanes].astype(F32) * result[tile]
        return carry

    lax.fori_loop(0, tiles, gate_tile, 0)

    def ag_third(hop, carry):
        ag_x(hop).wait_recv()
        ag_a(hop).start()
        ag_y(hop).wait_recv()
        ag_b(hop).start()
        return carry

    def own_sum(hop):
        total = term(chip((z + hop) % NZ, y, x))
        rs_x(hop).wait_recv()
        rs_y(hop).wait_recv()
        return total + r2x[hop].astype(F32) + r2y[hop].astype(F32)

    def rs_third(hop, carry):
        s3[hop] = own_sum(hop).astype(BF16)
        rs_z(hop).start()
        return carry

    wg_send[...] = own_sum(0)
    lax.fori_loop(1, NZ, rs_third, 0)
    lax.fori_loop(0, NZ, ag_third, 0)

    for hop in range(1, NZ):
        rs_z(hop).wait_recv()
        wg_send[...] += r3[hop].astype(F32)
    wg_send[...] = scale * wg_send[...]
    wg_copy = copy(wg_send, wg_recv, WG_COPY, sibling)
    wg_copy.start()
    wg_ref[:, own_half] = wg_send[...]

    def ig_part(hop, carry):
        cz = (z - hop + NZ) % NZ
        ag_a(hop).wait_recv()
        ag_b(hop).wait_recv()
        for cy in range(2):
            first = pl.multiple_of(chip(cz, cy, 0) * block, 2 * block)
            part = dot(val_full[...], wfull[pl.ds(first, 2 * block), :], 1, 1)
            columns = pl.ds(first, 2 * block)
            top, bottom = part[:ROWS], part[ROWS:]
            ig_ref[:, columns] = jnp.where(core == 0, top, bottom)
            ig_send[:, columns] = jnp.where(core == 0, bottom, top)
        return carry

    lax.fori_loop(0, NZ, ig_part, 0)
    ig_copy = copy(ig_send, ig_recv, IG_COPY, sibling)
    ig_copy.start()
    wg_copy.wait_recv()
    wg_ref[:, other_half] = wg_recv[...]
    ig_copy.wait_recv()
    ig_ref[...] += ig_recv[...]

    for single in (in_copy, back_copy, fwd_copy, val_copy, wg_copy, ig_copy):
        single.wait_send()

    def drain(hop, carry):
        for each in (ag_x, ag_y, ag_a, ag_b, rs_a, rs_b, rs_x, rs_y):
            each(hop).wait_send()
        return carry

    def drain_z(hop, carry):
        ag_z(hop).wait_send()
        rs_z(hop).wait_send()
        return carry

    lax.fori_loop(0, NZ, drain, 0)
    lax.fori_loop(1, NZ, drain_z, 0)


def on_chip_grid(inputs, values, gating, out_grad, weight, decay_rate, mode_gain):
    rows, width = inputs.shape[1:]
    channels = values.shape[2]
    modes = decay_rate.shape[0]
    block = weight.shape[0]
    tiles, half, mid = channels // LANES, channels // 2, block // 2
    scale = 1.0 / math.sqrt(rows * lax.axis_size("ctx") * lax.axis_size("dp"))
    vmem = pl.BlockSpec(memory_space=pltpu.VMEM)
    series = pltpu.VMEM((tiles, rows, LANES), F32)
    states = pltpu.VMEM((tiles, modes, RUNS, LANES), F32)
    ends = pltpu.VMEM((tiles, modes, LANES), F32)
    blocks = pltpu.VMEM((NZ, block, half), BF16)
    halves = pltpu.VMEM((NZ, mid, half), BF16)
    mode_coef = mode_gain * jnp.sqrt(-jnp.expm1(-2.0 * decay_rate))
    in_grad, gate_grad, weight_grad = pl.pallas_call(
        functools.partial(chip_kernel, scale),
        out_shape=(
            jax.ShapeDtypeStruct((rows, width), F32),
            jax.ShapeDtypeStruct((rows, channels), F32),
            jax.ShapeDtypeStruct((block, channels), F32),
        ),
        in_specs=[vmem] * 7,
        out_specs=(vmem,) * 3,
        scratch_shapes=[
            series, series, series, pltpu.VMEM((tiles, RUN, LANES), F32), states, states,
            ends, ends, ends, ends,
            pltpu.VMEM((2 * rows, width), BF16),
            pltpu.VMEM((2 * rows, half), BF16),
            pltpu.VMEM((rows, half), BF16),
            pltpu.VMEM((width, half), BF16),
            blocks, halves, halves, blocks, blocks, blocks, blocks, blocks, blocks,
            pltpu.VMEM((rows, width), F32),
            pltpu.VMEM((rows, width), F32),
            pltpu.VMEM((block, half), F32),
            pltpu.VMEM((block, half), F32),
            pltpu.SemaphoreType.DMA((COPIES,)),
            pltpu.SemaphoreType.DMA((COPIES,)),
        ],
        compiler_params=pltpu.CompilerParams(
            collective_id=0, has_side_effects=True, vmem_limit_bytes=56 * 1024 * 1024
        ),
    )(inputs[0], values[0], gating[0], out_grad[0], weight, decay_rate, mode_coef)
    return (in_grad[None], gate_grad[None], weight_grad)


def fits_chip_grid(mesh):
    return mesh.shape["ctx"] == 2 and mesh.shape["dp"] == 4 * NZ


def passed_along(block, axis, distance):
    devices = range(lax.axis_size(axis))
    route = [(i - distance, i) for i in devices if i - distance in devices]
    return lax.ppermute(block, axis, route)


def chain_combine(earlier, later):
    return (later[0] + later[1] * earlier[0], earlier[1] * later[1])


def power_rows(decay_rate, row_count, offset):
    steps = jnp.arange(row_count, dtype=jnp.float32) + offset
    return jnp.exp(-decay_rate[None, :, :] * steps[:, None, None])


def modal_tables(decay_rate, mode_gain, block_len):
    mode_coef = mode_gain * jnp.sqrt(-jnp.expm1(-2.0 * decay_rate))
    power_table = power_rows(decay_rate, block_len, 0.0)
    impulse = jnp.sum(mode_coef[None] * power_table, axis=1)
    sum_weights = power_table[::-1]
    inject_table = mode_coef[None] * power_rows(decay_rate, block_len, 1.0)
    step_decay = jnp.exp(-decay_rate * block_len)
    return (impulse, sum_weights, inject_table, step_decay)


def local_pass(series, tables):
    impulse, sum_weights, inject_table, step_decay = tables
    block_len = impulse.shape[0]
    mode_count = sum_weights.shape[1]
    blocked = series.reshape(-1, block_len, series.shape[-1])
    within_block = impulse[0][None, None, :] * blocked
    for lag_step in range(1, block_len):
        shifted = jnp.pad(blocked[:, : block_len - lag_step], ((0, 0), (lag_step, 0), (0, 0)))
        within_block = within_block + impulse[lag_step][None, None, :] * shifted
    block_sums = jnp.zeros((blocked.shape[0], mode_count, blocked.shape[2]), jnp.float32)
    for row_step in range(block_len):
        block_sums = block_sums + sum_weights[row_step][None] * blocked[:, row_step][:, None, :]
    block_decay = jnp.broadcast_to(step_decay, block_sums.shape)
    end_state, end_decay = lax.associative_scan(chain_combine, (block_sums, block_decay), axis=0)
    return (within_block, end_state, end_decay)


def finish_pass(within_block, end_state, end_decay, incoming, inject_table):
    total_state = end_state + end_decay * incoming[None]
    prior_state = jnp.concatenate([incoming[None], total_state[:-1]], axis=0)
    carried = within_block
    for mode_step in range(inject_table.shape[1]):
        carried = carried + inject_table[:, mode_step][None] * prior_state[:, mode_step][:, None, :]
    return carried.reshape(-1, within_block.shape[-1])


def entering(fwd_own, fwd_span, back_own, back_span):
    empty_state = jnp.zeros_like(fwd_own)
    n_ctx = lax.axis_size("ctx")

    def fwd_step(step_index, loop_state):
        received = passed_along(loop_state[1], "ctx", 1)
        return (received, fwd_own + fwd_span * received)

    def back_step(step_index, loop_state):
        received = passed_along(loop_state[1], "ctx", -1)
        return (received, back_own + back_span * received)

    fwd_in = lax.fori_loop(0, n_ctx - 1, fwd_step, (empty_state, fwd_own))[0]
    back_in = lax.fori_loop(0, n_ctx - 1, back_step, (empty_state, back_own))[0]
    return (fwd_in, back_in)


def on_device(inputs, values, gating, out_grad, weight, decay_rate, mode_gain):
    in_rows = inputs[0]
    tok_rows = in_rows.shape[0]
    n_ctx = lax.axis_size("ctx")
    n_dp = lax.axis_size("dp")
    tables = modal_tables(decay_rate, mode_gain, 16)
    fwd_within, fwd_end, fwd_decay = local_pass(values[0].astype(jnp.float32), tables)
    mix_grad = gating[0].astype(jnp.float32) * out_grad[0].astype(jnp.float32)
    back_within, back_end, back_decay = local_pass(jnp.flip(mix_grad, 0), tables)
    fwd_in, back_in = entering(fwd_end[-1], fwd_decay[-1], back_end[-1], back_decay[-1])
    val_grad = jnp.flip(
        finish_pass(back_within, back_end, back_decay, back_in, tables[2]), 0
    ).astype(jnp.bfloat16)
    mixed = finish_pass(fwd_within, fwd_end, fwd_decay, fwd_in, tables[2])
    gate_grad = out_grad[0].astype(jnp.float32) * mixed
    in_grad = lax.dot_general(
        val_grad,
        lax.all_gather(weight, "dp", axis=0, tiled=True),
        (((1,), (1,)), ((), ())),
        preferred_element_type=jnp.float32,
    )
    norm_factor = 1.0 / math.sqrt(tok_rows * n_ctx * n_dp)
    share = lax.psum_scatter(
        norm_factor
        * lax.dot_general(
            in_rows, val_grad, (((0,), (0,)), ((), ())), preferred_element_type=jnp.float32
        ),
        "dp",
        scatter_dimension=0,
        tiled=True,
    )
    weight_grad = lax.psum(share, "ctx")
    return (in_grad[None], gate_grad[None], weight_grad)


def solution(mesh):
    placed = (
        P("dp", "ctx", None),
        P("dp", "ctx", None),
        P("dp", "ctx", None),
        P("dp", "ctx", None),
        P("dp", None),
        P(),
        P(),
    )
    step = on_chip_grid if fits_chip_grid(mesh) else on_device
    return jax.shard_map(
        step,
        mesh=mesh,
        in_specs=placed,
        out_specs=(P("dp", "ctx", None), P("dp", "ctx", None), P("dp", None)),
        check_vma=False,
    )
```

```python
import functools
import math

import jax
import jax.numpy as jnp
from jax import lax
from jax.experimental import pallas as pl
from jax.experimental.pallas import tpu as pltpu
from jax.sharding import PartitionSpec as P

MESH = pl.DeviceIdType.MESH
F32 = jnp.float32
BF16 = jnp.bfloat16
LANES = 128
RUN = 16
RUNS = 8
ROWS = RUN * RUNS
NZ = 4

IN_COPY, BACK_COPY, FWD_COPY, VAL_COPY, WG_COPY = range(5)
AG_Z, AG_X, AG_Y, AG_A, AG_B, RS_A, RS_B, RS_X, RS_Y, RS_Z, IG_COPY = range(5, 49, 4)
COPIES = 49


def dot(lhs, rhs, lhs_dim, rhs_dim):
    return lax.dot_general(
        lhs, rhs, (((lhs_dim,), (rhs_dim,)), ((), ())), preferred_element_type=F32
    )


def lanes_of(tile):
    return pl.ds(pl.multiple_of(tile * LANES, LANES), LANES)


def run_rows(step):
    return pl.ds(step, RUNS, RUN)


def row_index():
    return lax.broadcasted_iota(jnp.int32, (RUNS, LANES), 0)


def shifted_runs(state, by, reverse):
    rows = row_index()
    if reverse:
        return jnp.where(rows < RUNS - by, pltpu.roll(state, RUNS - by, 0), 0.0)
    return jnp.where(rows >= by, pltpu.roll(state, by, 0), 0.0)


def spread(row):
    return jnp.broadcast_to(row, (RUNS, LANES))


def one_less_exp(u):
    series = 1.0
    for order in range(8, 1, -1):
        series = 1.0 - u * (1.0 / order) * series
    return jnp.where(u > 0.25, 1.0 - jnp.exp(-u), u * series)


def modes_of(decay_ref, gain_ref, tile):
    decay = decay_ref[:, lanes_of(tile)]
    lam = jnp.exp(-decay)
    coef = gain_ref[:, lanes_of(tile)] * jnp.sqrt(one_less_exp(2.0 * decay))
    return decay, lam, coef


def run_states(series, decay, lam, states, ends, tile, reverse):
    order = range(RUN - 1, -1, -1) if reverse else range(RUN)
    steps = [series[tile, run_rows(step), :] for step in order]
    over_run = jnp.exp(-float(RUN) * decay)
    for mode in range(decay.shape[0]):
        rate = spread(lam[mode : mode + 1])
        state = steps[0]
        for column in steps[1:]:
            state = rate * state + column
        span = spread(over_run[mode : mode + 1])
        for by in (1, 2, 4):
            state = state + span * shifted_runs(state, by, reverse)
            span = span * span
        states[tile, mode] = state
        last = 0 if reverse else RUNS - 1
        ends[tile, mode : mode + 1, :] = state[last : last + 1]


def run_outputs(series, impulse, decay, lam, coef, states, incoming, enters, result, tile, reverse):
    order = list(range(RUN - 1, -1, -1) if reverse else range(RUN))
    steps = [series[tile, run_rows(step), :] for step in order]
    lags = [spread(impulse[tile, lag : lag + 1, :]) for lag in range(RUN)]
    ahead = row_index()
    ahead = (RUNS - 1 - ahead if reverse else ahead).astype(F32) * float(RUN)
    rates, carried = [], []
    for mode in range(decay.shape[0]):
        rate = spread(lam[mode : mode + 1])
        entry = jnp.where(enters, spread(incoming[tile, mode : mode + 1, :]), 0.0)
        prior = shifted_runs(states[tile, mode], 1, reverse)
        prior = prior + jnp.exp(-ahead * spread(decay[mode : mode + 1])) * entry
        rates.append(rate)
        carried.append(spread(coef[mode : mode + 1]) * rate * prior)
    for at, step in enumerate(order):
        terms = [lags[at - back] * steps[back] for back in range(at + 1)] + carried
        while len(terms) > 1:
            odd = terms[-1:] if len(terms) % 2 else []
            terms = [a + b for a, b in zip(terms[::2], terms[1::2])] + odd
        result[tile, run_rows(step), :] = terms[0]
        carried = [rate * item for rate, item in zip(rates, carried)]


def chip_kernel(
    scale,
    in_ref, values_ref, gating_ref, grad_ref, weight_ref, decay_ref, gain_ref,
    ig_ref, gate_ref, wg_ref,
    series_f, series_b, result, impulse, states_f, states_b,
    ends_f, ends_b, enter_f, enter_b,
    in_full, val_full, val_send, wfull,
    s1, r1a, r1b, s2x, s2y, r2x, r2y, s3, r3,
    ig_send, ig_recv, wg_send, wg_recv,
    send_sem, recv_sem,
):
    core = lax.axis_index("ctx")
    dp = lax.axis_index("dp")
    z, y, x = dp // 4, (dp // 2) % 2, dp % 2
    tiles = series_f.shape[0]
    half_tiles = tiles // 2
    half = half_tiles * LANES
    block = weight_ref.shape[0]
    mid = block // 2

    def chip(cz, cy, cx):
        return cz * 4 + cy * 2 + cx

    sibling = (1 - core, dp)
    x_dev = (core, chip(z, y, 1 - x))
    y_dev = (core, chip(z, 1 - y, x))

    def z_dev(hop):
        return (core, chip((z + hop) % NZ, y, x))

    def copy(src, dst, which, device):
        return pltpu.make_async_remote_copy(
            src_ref=src, dst_ref=dst, send_sem=send_sem.at[which], recv_sem=recv_sem.at[which],
            device_id=device, device_id_type=MESH,
        )

    barrier = pltpu.get_barrier_semaphore()
    partners = [sibling, x_dev, y_dev] + [z_dev(hop) for hop in range(1, NZ)]
    for device in partners:
        pl.semaphore_signal(barrier, inc=1, device_id=device, device_id_type=MESH)
    pl.semaphore_wait(barrier, len(partners))

    def wrows(index, start=0, size=block):
        return wfull.at[pl.ds(pl.multiple_of(index * block + start, mid), size), :]

    own_half = pl.ds(pl.multiple_of(core * half, half), half)
    other_half = pl.ds(pl.multiple_of((1 - core) * half, half), half)
    own_rows = pl.ds(pl.multiple_of(core * ROWS, ROWS), ROWS)

    wrows(dp)[...] = weight_ref[:, own_half]

    def ag_z(hop):
        return copy(wrows(dp), wrows(dp), AG_Z + hop, z_dev(hop))

    def ag_x(hop):
        rows = wrows(chip((z - hop + NZ) % NZ, y, x))
        return copy(rows, rows, AG_X + hop, x_dev)

    def ag_y(hop):
        rows = wrows(chip((z - hop + NZ) % NZ, y, x))
        return copy(rows, rows, AG_Y + hop, y_dev)

    def ag_a(hop):
        rows = wrows(chip((z - hop + NZ) % NZ, y, 1 - x), 0, mid)
        return copy(rows, rows, AG_A + hop, y_dev)

    def ag_b(hop):
        rows = wrows(chip((z - hop + NZ) % NZ, 1 - y, x), mid, mid)
        return copy(rows, rows, AG_B + hop, x_dev)

    def ag_second(hop):
        ag_z(hop).wait_recv()
        ag_x(hop).start()
        ag_y(hop).start()

    def ag_third(hop):
        ag_x(hop).wait_recv()
        ag_a(hop).start()
        ag_y(hop).wait_recv()
        ag_b(hop).start()

    ag_z(1).start()
    ag_x(0).start()
    ag_y(0).start()
    in_copy = copy(in_ref, in_full.at[own_rows, :], IN_COPY, sibling)
    in_copy.start()
    in_full[own_rows, :] = in_ref[...]

    def back_states(tile, carry):
        lanes = lanes_of(tile)
        series_b[tile] = gating_ref[:, lanes].astype(F32) * grad_ref[:, lanes].astype(F32)
        decay, lam, coef = modes_of(decay_ref, gain_ref, tile)
        power = coef
        for lag in range(RUN):
            impulse[tile, lag : lag + 1, :] = jnp.sum(power, axis=0, keepdims=True)
            power = power * lam
        run_states(series_b, decay, lam, states_b, ends_b, tile, True)
        return carry

    def fwd_states(tile, carry):
        series_f[tile] = values_ref[:, lanes_of(tile)].astype(F32)
        decay, lam, coef = modes_of(decay_ref, gain_ref, tile)
        run_states(series_f, decay, lam, states_f, ends_f, tile, False)
        return carry

    lax.fori_loop(0, tiles, back_states, 0)
    back_copy = copy(ends_b, enter_b, BACK_COPY, sibling)
    back_copy.start()
    ag_z(3).start()
    lax.fori_loop(0, tiles, fwd_states, 0)
    fwd_copy = copy(ends_f, enter_f, FWD_COPY, sibling)
    fwd_copy.start()
    ag_second(1)
    ag_third(0)
    back_copy.wait_recv()

    def val_tile(tile):
        decay, lam, coef = modes_of(decay_ref, gain_ref, tile)
        run_outputs(
            series_b, impulse, decay, lam, coef, states_b, enter_b, core == 0, result, tile, True
        )
        return result[tile].astype(BF16)

    def val_other(tile, carry):
        val_send[:, lanes_of(tile)] = val_tile((1 - core) * half_tiles + tile)
        return carry

    def val_own(tile, carry):
        val_full[own_rows, lanes_of(tile)] = val_tile(core * half_tiles + tile)
        return carry

    lax.fori_loop(0, half_tiles, val_other, 0)
    val_copy = copy(val_send, val_full.at[own_rows, :], VAL_COPY, sibling)
    val_copy.start()
    lax.fori_loop(0, half_tiles, val_own, 0)
    ag_z(2).start()
    in_copy.wait_recv()
    val_copy.wait_recv()

    def term(index):
        columns = pl.ds(pl.multiple_of(index * block, block), block)
        return dot(in_full[:, columns], val_full[...], 0, 0)

    def rs_a(hop):
        return copy(s1.at[hop, pl.ds(0, mid), :], r1a.at[hop], RS_A + hop, y_dev)

    def rs_b(hop):
        return copy(s1.at[hop, pl.ds(mid, mid), :], r1b.at[hop], RS_B + hop, x_dev)

    def rs_x(hop):
        return copy(s2x.at[hop], r2x.at[hop], RS_X + hop, x_dev)

    def rs_y(hop):
        return copy(s2y.at[hop], r2y.at[hop], RS_Y + hop, y_dev)

    def rs_z(hop):
        return copy(s3.at[hop], r3.at[hop], RS_Z + hop, z_dev(hop))

    def rs_first(hop):
        s1[hop] = term(chip((z + hop) % NZ, 1 - y, 1 - x)).astype(BF16)
        rs_a(hop).start()
        rs_b(hop).start()

    def rs_second(hop):
        to_x = term(chip((z + hop) % NZ, y, 1 - x))
        rs_a(hop).wait_recv()
        s2x[hop, pl.ds(0, mid), :] = (to_x[:mid] + r1a[hop].astype(F32)).astype(BF16)
        s2x[hop, pl.ds(mid, mid), :] = to_x[mid:].astype(BF16)
        rs_x(hop).start()
        to_y = term(chip((z + hop) % NZ, 1 - y, x))
        rs_b(hop).wait_recv()
        s2y[hop, pl.ds(0, mid), :] = to_y[:mid].astype(BF16)
        s2y[hop, pl.ds(mid, mid), :] = (to_y[mid:] + r1b[hop].astype(F32)).astype(BF16)
        rs_y(hop).start()

    for hop in (1, 2, 3, 0):
        rs_first(hop)
    ag_second(3)

    fwd_copy.wait_recv()

    def gate_tile(tile, carry):
        decay, lam, coef = modes_of(decay_ref, gain_ref, tile)
        run_outputs(
            series_f, impulse, decay, lam, coef, states_f, enter_f, core == 1, result, tile, False
        )
        lanes = lanes_of(tile)
        gate_ref[:, lanes] = grad_ref[:, lanes].astype(F32) * result[tile]
        return carry

    lax.fori_loop(0, tiles, gate_tile, 0)

    for hop in (1, 2, 3, 0):
        rs_second(hop)
    ag_second(2)

    def own_sum(hop):
        total = term(chip((z + hop) % NZ, y, x))
        rs_x(hop).wait_recv()
        rs_y(hop).wait_recv()
        return total + r2x[hop].astype(F32) + r2y[hop].astype(F32)

    def rs_third(hop):
        s3[hop] = own_sum(hop).astype(BF16)
        rs_z(hop).start()

    rs_third(1)
    ag_third(1)
    rs_third(2)
    ag_third(3)
    rs_third(3)
    wg_send[...] = own_sum(0)
    ag_third(2)

    def ig_columns(hop):
        first = ((z - hop + NZ) % NZ) * 4 * block
        return pl.ds(pl.multiple_of(first, 4 * block), 4 * block)

    def ig_copy(hop):
        columns = ig_columns(hop)
        return copy(ig_send.at[:, columns], ig_recv.at[:, columns], IG_COPY + hop, sibling)

    def ig_part(hop):
        cz = (z - hop + NZ) % NZ
        ag_a(hop).wait_recv()
        ag_b(hop).wait_recv()
        for cy in range(2):
            first = pl.multiple_of(chip(cz, cy, 0) * block, 2 * block)
            part = dot(val_full[...], wfull[pl.ds(first, 2 * block), :], 1, 1)
            columns = pl.ds(first, 2 * block)
            top, bottom = part[:ROWS], part[ROWS:]
            ig_ref[:, columns] = jnp.where(core == 0, top, bottom)
            ig_send[:, columns] = jnp.where(core == 0, bottom, top)
        ig_copy(hop).start()

    def ig_finish(hop):
        columns = ig_columns(hop)
        ig_copy(hop).wait_recv()
        ig_ref[:, columns] += ig_recv[:, columns]

    ig_part(0)
    ig_part(1)
    ig_part(3)

    for hop in range(1, NZ):
        rs_z(hop).wait_recv()
        wg_send[...] += r3[hop].astype(F32)
    wg_send[...] = scale * wg_send[...]
    wg_copy = copy(wg_send, wg_recv, WG_COPY, sibling)
    wg_copy.start()
    wg_ref[:, own_half] = wg_send[...]

    ig_part(2)
    wg_copy.wait_recv()
    wg_ref[:, other_half] = wg_recv[...]
    for hop in (0, 1, 3, 2):
        ig_finish(hop)

    for single in (in_copy, back_copy, fwd_copy, val_copy, wg_copy):
        single.wait_send()

    def drain(hop, carry):
        for each in (ag_x, ag_y, ag_a, ag_b, rs_a, rs_b, rs_x, rs_y, ig_copy):
            each(hop).wait_send()
        return carry

    def drain_z(hop, carry):
        ag_z(hop).wait_send()
        rs_z(hop).wait_send()
        return carry

    lax.fori_loop(0, NZ, drain, 0)
    lax.fori_loop(1, NZ, drain_z, 0)


def on_chip_grid(inputs, values, gating, out_grad, weight, decay_rate, mode_gain):
    rows, width = inputs.shape[1:]
    channels = values.shape[2]
    modes = decay_rate.shape[0]
    block = weight.shape[0]
    tiles, half, mid = channels // LANES, channels // 2, block // 2
    scale = 1.0 / math.sqrt(rows * lax.axis_size("ctx") * lax.axis_size("dp"))
    vmem = pl.BlockSpec(memory_space=pltpu.VMEM)
    series = pltpu.VMEM((tiles, rows, LANES), F32)
    states = pltpu.VMEM((tiles, modes, RUNS, LANES), F32)
    ends = pltpu.VMEM((tiles, modes, LANES), F32)
    blocks = pltpu.VMEM((NZ, block, half), BF16)
    halves = pltpu.VMEM((NZ, mid, half), BF16)
    in_grad, gate_grad, weight_grad = pl.pallas_call(
        functools.partial(chip_kernel, scale),
        out_shape=(
            jax.ShapeDtypeStruct((rows, width), F32),
            jax.ShapeDtypeStruct((rows, channels), F32),
            jax.ShapeDtypeStruct((block, channels), F32),
        ),
        in_specs=[vmem] * 7,
        out_specs=(vmem,) * 3,
        scratch_shapes=[
            series, series, series, pltpu.VMEM((tiles, RUN, LANES), F32), states, states,
            ends, ends, ends, ends,
            pltpu.VMEM((2 * rows, width), BF16),
            pltpu.VMEM((2 * rows, half), BF16),
            pltpu.VMEM((rows, half), BF16),
            pltpu.VMEM((width, half), BF16),
            blocks, halves, halves, blocks, blocks, blocks, blocks, blocks, blocks,
            pltpu.VMEM((rows, width), F32),
            pltpu.VMEM((rows, width), F32),
            pltpu.VMEM((block, half), F32),
            pltpu.VMEM((block, half), F32),
            pltpu.SemaphoreType.DMA((COPIES,)),
            pltpu.SemaphoreType.DMA((COPIES,)),
        ],
        compiler_params=pltpu.CompilerParams(
            collective_id=0, has_side_effects=True, vmem_limit_bytes=56 * 1024 * 1024
        ),
    )(inputs[0], values[0], gating[0], out_grad[0], weight, decay_rate, mode_gain)
    return (in_grad[None], gate_grad[None], weight_grad)


def fits_chip_grid(mesh):
    return mesh.shape["ctx"] == 2 and mesh.shape["dp"] == 4 * NZ


def passed_along(block, axis, distance):
    devices = range(lax.axis_size(axis))
    route = [(i - distance, i) for i in devices if i - distance in devices]
    return lax.ppermute(block, axis, route)


def chain_combine(earlier, later):
    return (later[0] + later[1] * earlier[0], earlier[1] * later[1])


def power_rows(decay_rate, row_count, offset):
    steps = jnp.arange(row_count, dtype=jnp.float32) + offset
    return jnp.exp(-decay_rate[None, :, :] * steps[:, None, None])


def modal_tables(decay_rate, mode_gain, block_len):
    mode_coef = mode_gain * jnp.sqrt(-jnp.expm1(-2.0 * decay_rate))
    power_table = power_rows(decay_rate, block_len, 0.0)
    impulse = jnp.sum(mode_coef[None] * power_table, axis=1)
    sum_weights = power_table[::-1]
    inject_table = mode_coef[None] * power_rows(decay_rate, block_len, 1.0)
    step_decay = jnp.exp(-decay_rate * block_len)
    return (impulse, sum_weights, inject_table, step_decay)


def local_pass(series, tables):
    impulse, sum_weights, inject_table, step_decay = tables
    block_len = impulse.shape[0]
    mode_count = sum_weights.shape[1]
    blocked = series.reshape(-1, block_len, series.shape[-1])
    within_block = impulse[0][None, None, :] * blocked
    for lag_step in range(1, block_len):
        shifted = jnp.pad(blocked[:, : block_len - lag_step], ((0, 0), (lag_step, 0), (0, 0)))
        within_block = within_block + impulse[lag_step][None, None, :] * shifted
    block_sums = jnp.zeros((blocked.shape[0], mode_count, blocked.shape[2]), jnp.float32)
    for row_step in range(block_len):
        block_sums = block_sums + sum_weights[row_step][None] * blocked[:, row_step][:, None, :]
    block_decay = jnp.broadcast_to(step_decay, block_sums.shape)
    end_state, end_decay = lax.associative_scan(chain_combine, (block_sums, block_decay), axis=0)
    return (within_block, end_state, end_decay)


def finish_pass(within_block, end_state, end_decay, incoming, inject_table):
    total_state = end_state + end_decay * incoming[None]
    prior_state = jnp.concatenate([incoming[None], total_state[:-1]], axis=0)
    carried = within_block
    for mode_step in range(inject_table.shape[1]):
        carried = carried + inject_table[:, mode_step][None] * prior_state[:, mode_step][:, None, :]
    return carried.reshape(-1, within_block.shape[-1])


def entering(fwd_own, fwd_span, back_own, back_span):
    empty_state = jnp.zeros_like(fwd_own)
    n_ctx = lax.axis_size("ctx")

    def fwd_step(step_index, loop_state):
        received = passed_along(loop_state[1], "ctx", 1)
        return (received, fwd_own + fwd_span * received)

    def back_step(step_index, loop_state):
        received = passed_along(loop_state[1], "ctx", -1)
        return (received, back_own + back_span * received)

    fwd_in = lax.fori_loop(0, n_ctx - 1, fwd_step, (empty_state, fwd_own))[0]
    back_in = lax.fori_loop(0, n_ctx - 1, back_step, (empty_state, back_own))[0]
    return (fwd_in, back_in)


def on_device(inputs, values, gating, out_grad, weight, decay_rate, mode_gain):
    in_rows = inputs[0]
    tok_rows = in_rows.shape[0]
    n_ctx = lax.axis_size("ctx")
    n_dp = lax.axis_size("dp")
    tables = modal_tables(decay_rate, mode_gain, 16)
    fwd_within, fwd_end, fwd_decay = local_pass(values[0].astype(jnp.float32), tables)
    mix_grad = gating[0].astype(jnp.float32) * out_grad[0].astype(jnp.float32)
    back_within, back_end, back_decay = local_pass(jnp.flip(mix_grad, 0), tables)
    fwd_in, back_in = entering(fwd_end[-1], fwd_decay[-1], back_end[-1], back_decay[-1])
    val_grad = jnp.flip(
        finish_pass(back_within, back_end, back_decay, back_in, tables[2]), 0
    ).astype(jnp.bfloat16)
    mixed = finish_pass(fwd_within, fwd_end, fwd_decay, fwd_in, tables[2])
    gate_grad = out_grad[0].astype(jnp.float32) * mixed
    in_grad = lax.dot_general(
        val_grad,
        lax.all_gather(weight, "dp", axis=0, tiled=True),
        (((1,), (1,)), ((), ())),
        preferred_element_type=jnp.float32,
    )
    norm_factor = 1.0 / math.sqrt(tok_rows * n_ctx * n_dp)
    share = lax.psum_scatter(
        norm_factor
        * lax.dot_general(
            in_rows, val_grad, (((0,), (0,)), ((), ())), preferred_element_type=jnp.float32
        ),
        "dp",
        scatter_dimension=0,
        tiled=True,
    )
    weight_grad = lax.psum(share, "ctx")
    return (in_grad[None], gate_grad[None], weight_grad)


def solution(mesh):
    placed = (
        P("dp", "ctx", None),
        P("dp", "ctx", None),
        P("dp", "ctx", None),
        P("dp", "ctx", None),
        P("dp", None),
        P(),
        P(),
    )
    step = on_chip_grid if fits_chip_grid(mesh) else on_device
    return jax.shard_map(
        step,
        mesh=mesh,
        in_specs=placed,
        out_specs=(P("dp", "ctx", None), P("dp", "ctx", None), P("dp", None)),
        check_vma=False,
    )
```

```python
import functools
import math

import jax
import jax.numpy as jnp
from jax import lax
from jax.experimental import pallas as pl
from jax.experimental.pallas import tpu as pltpu
from jax.sharding import PartitionSpec as P

MESH = pl.DeviceIdType.MESH
F32 = jnp.float32
BF16 = jnp.bfloat16
LANES = 128
RUN = 16
RUNS = 8
ROWS = RUN * RUNS
NZ = 4

IN_COPY, BACK_COPY, FWD_COPY, VAL_COPY, WG_COPY = range(5)
AG_Z, AG_X, AG_Y, AG_A, AG_B, RS_A, RS_B, RS_X, RS_Y, RS_Z, IG_COPY = range(5, 49, 4)
COPIES = 49


def dot(lhs, rhs, lhs_dim, rhs_dim):
    return lax.dot_general(
        lhs, rhs, (((lhs_dim,), (rhs_dim,)), ((), ())), preferred_element_type=F32
    )


def lanes_of(tile):
    return pl.ds(pl.multiple_of(tile * LANES, LANES), LANES)


def run_rows(step):
    return pl.ds(step, RUNS, RUN)


def row_index():
    return lax.broadcasted_iota(jnp.int32, (RUNS, LANES), 0)


def shifted_runs(state, by, reverse):
    rows = row_index()
    if reverse:
        return jnp.where(rows < RUNS - by, pltpu.roll(state, RUNS - by, 0), 0.0)
    return jnp.where(rows >= by, pltpu.roll(state, by, 0), 0.0)


def spread(row):
    return jnp.broadcast_to(row, (RUNS, LANES))


def one_less_exp(u):
    series = 1.0
    for order in range(8, 1, -1):
        series = 1.0 - u * (1.0 / order) * series
    return jnp.where(u > 0.25, 1.0 - jnp.exp(-u), u * series)


def modes_of(decay_ref, gain_ref, tile):
    decay = decay_ref[:, lanes_of(tile)]
    lam = jnp.exp(-decay)
    coef = gain_ref[:, lanes_of(tile)] * jnp.sqrt(one_less_exp(2.0 * decay))
    return decay, lam, coef


def in_order(reverse):
    return range(RUN - 1, -1, -1) if reverse else range(RUN)


def run_states(series, decay, lam, states, ends, tile, reverse):
    modes = range(decay.shape[0])
    rates = [spread(lam[mode : mode + 1]) for mode in modes]
    held = None
    for step in in_order(reverse):
        column = series[tile, run_rows(step), :]
        held = [column] * len(rates) if held is None else [r * h + column for r, h in zip(rates, held)]
    over_run = jnp.exp(-float(RUN) * decay)
    spans = [spread(over_run[mode : mode + 1]) for mode in modes]
    for by in (1, 2, 4):
        held = [h + s * shifted_runs(h, by, reverse) for h, s in zip(held, spans)]
        spans = [s * s for s in spans]
    last = 0 if reverse else RUNS - 1
    for mode in modes:
        states[tile, mode] = held[mode]
        ends[tile, mode : mode + 1, :] = held[mode][last : last + 1]


def added(terms):
    while len(terms) > 1:
        odd = terms[-1:] if len(terms) % 2 else []
        terms = [a + b for a, b in zip(terms[::2], terms[1::2])] + odd
    return terms[0]


def run_within(series, impulse, result, tile, reverse):
    order = list(in_order(reverse))
    steps = [series[tile, run_rows(step), :] for step in order]
    lags = [spread(impulse[tile, lag : lag + 1, :]) for lag in range(RUN)]
    for at, step in enumerate(order):
        result[tile, run_rows(step), :] = added([lags[at - b] * steps[b] for b in range(at + 1)])


def run_carried(decay, lam, coef, states, incoming, enters, result, tile, reverse):
    ahead = row_index()
    ahead = (RUNS - 1 - ahead if reverse else ahead).astype(F32) * float(RUN)
    rates, carried = [], []
    for mode in range(decay.shape[0]):
        rate = spread(lam[mode : mode + 1])
        entry = jnp.where(enters, spread(incoming[tile, mode : mode + 1, :]), 0.0)
        prior = shifted_runs(states[tile, mode], 1, reverse)
        prior = prior + jnp.exp(-ahead * spread(decay[mode : mode + 1])) * entry
        rates.append(rate)
        carried.append(spread(coef[mode : mode + 1]) * rate * prior)
    for step in in_order(reverse):
        result[tile, run_rows(step), :] += added(carried)
        carried = [rate * item for rate, item in zip(rates, carried)]


def chip_kernel(
    scale,
    in_ref, values_ref, gating_ref, grad_ref, weight_ref, decay_ref, gain_ref,
    ig_ref, gate_ref, wg_ref,
    series_f, series_b, result, impulse, states_f, states_b,
    ends_f, ends_b, enter_f, enter_b,
    in_full, val_full, val_send, wfull,
    s1, r1a, r1b, s2x, s2y, r2x, r2y, s3, r3,
    ig_send, ig_recv, wg_send, wg_recv,
    send_sem, recv_sem,
):
    core = lax.axis_index("ctx")
    dp = lax.axis_index("dp")
    z, y, x = dp // 4, (dp // 2) % 2, dp % 2
    tiles = series_f.shape[0]
    half_tiles = tiles // 2
    half = half_tiles * LANES
    block = weight_ref.shape[0]
    mid = block // 2

    def chip(cz, cy, cx):
        return cz * 4 + cy * 2 + cx

    sibling = (1 - core, dp)
    x_dev = (core, chip(z, y, 1 - x))
    y_dev = (core, chip(z, 1 - y, x))

    def z_dev(hop):
        return (core, chip((z + hop) % NZ, y, x))

    def copy(src, dst, which, device):
        return pltpu.make_async_remote_copy(
            src_ref=src, dst_ref=dst, send_sem=send_sem.at[which], recv_sem=recv_sem.at[which],
            device_id=device, device_id_type=MESH,
        )

    barrier = pltpu.get_barrier_semaphore()
    partners = [sibling, x_dev, y_dev] + [z_dev(hop) for hop in range(1, NZ)]
    for device in partners:
        pl.semaphore_signal(barrier, inc=1, device_id=device, device_id_type=MESH)
    pl.semaphore_wait(barrier, len(partners))

    def wrows(index, start=0, size=block):
        return wfull.at[pl.ds(pl.multiple_of(index * block + start, mid), size), :]

    own_half = pl.ds(pl.multiple_of(core * half, half), half)
    other_half = pl.ds(pl.multiple_of((1 - core) * half, half), half)
    own_rows = pl.ds(pl.multiple_of(core * ROWS, ROWS), ROWS)

    wrows(dp)[...] = weight_ref[:, own_half]

    def ag_z(hop):
        return copy(wrows(dp), wrows(dp), AG_Z + hop, z_dev(hop))

    def ag_x(hop):
        rows = wrows(chip((z - hop + NZ) % NZ, y, x))
        return copy(rows, rows, AG_X + hop, x_dev)

    def ag_y(hop):
        rows = wrows(chip((z - hop + NZ) % NZ, y, x))
        return copy(rows, rows, AG_Y + hop, y_dev)

    def ag_a(hop):
        rows = wrows(chip((z - hop + NZ) % NZ, y, 1 - x), 0, mid)
        return copy(rows, rows, AG_A + hop, y_dev)

    def ag_b(hop):
        rows = wrows(chip((z - hop + NZ) % NZ, 1 - y, x), mid, mid)
        return copy(rows, rows, AG_B + hop, x_dev)

    def ag_second(hop):
        ag_z(hop).wait_recv()
        ag_x(hop).start()
        ag_y(hop).start()

    def ag_third(hop):
        ag_x(hop).wait_recv()
        ag_a(hop).start()
        ag_y(hop).wait_recv()
        ag_b(hop).start()

    ag_z(1).start()
    ag_x(0).start()
    ag_y(0).start()
    in_copy = copy(in_ref, in_full.at[own_rows, :], IN_COPY, sibling)
    in_copy.start()
    in_full[own_rows, :] = in_ref[...]

    def back_states(tile, carry):
        lanes = lanes_of(tile)
        series_b[tile] = gating_ref[:, lanes].astype(F32) * grad_ref[:, lanes].astype(F32)
        decay, lam, coef = modes_of(decay_ref, gain_ref, tile)
        power = coef
        for lag in range(RUN):
            impulse[tile, lag : lag + 1, :] = jnp.sum(power, axis=0, keepdims=True)
            power = power * lam
        run_states(series_b, decay, lam, states_b, ends_b, tile, True)
        return carry

    def fwd_states(tile, carry):
        series_f[tile] = values_ref[:, lanes_of(tile)].astype(F32)
        decay, lam, coef = modes_of(decay_ref, gain_ref, tile)
        run_states(series_f, decay, lam, states_f, ends_f, tile, False)
        return carry

    lax.fori_loop(0, tiles, back_states, 0)
    back_copy = copy(ends_b, enter_b, BACK_COPY, sibling)
    back_copy.start()
    ag_z(3).start()

    def back_within(tile, carry):
        run_within(series_b, impulse, result, tile, True)
        return carry

    lax.fori_loop(0, tiles, back_within, 0)
    back_copy.wait_recv()

    def val_tile(tile):
        decay, lam, coef = modes_of(decay_ref, gain_ref, tile)
        run_carried(decay, lam, coef, states_b, enter_b, core == 0, result, tile, True)
        return result[tile].astype(BF16)

    def val_other(tile, carry):
        val_send[:, lanes_of(tile)] = val_tile((1 - core) * half_tiles + tile)
        return carry

    def val_own(tile, carry):
        val_full[own_rows, lanes_of(tile)] = val_tile(core * half_tiles + tile)
        return carry

    lax.fori_loop(0, half_tiles, val_other, 0)
    val_copy = copy(val_send, val_full.at[own_rows, :], VAL_COPY, sibling)
    val_copy.start()
    ag_second(1)
    ag_third(0)
    lax.fori_loop(0, half_tiles, val_own, 0)
    ag_z(2).start()
    in_copy.wait_recv()
    val_copy.wait_recv()

    def term(index):
        columns = pl.ds(pl.multiple_of(index * block, block), block)
        return dot(in_full[:, columns], val_full[...], 0, 0)

    def rs_a(hop):
        return copy(s1.at[hop, pl.ds(0, mid), :], r1a.at[hop], RS_A + hop, y_dev)

    def rs_b(hop):
        return copy(s1.at[hop, pl.ds(mid, mid), :], r1b.at[hop], RS_B + hop, x_dev)

    def rs_x(hop):
        return copy(s2x.at[hop], r2x.at[hop], RS_X + hop, x_dev)

    def rs_y(hop):
        return copy(s2y.at[hop], r2y.at[hop], RS_Y + hop, y_dev)

    def rs_z(hop):
        return copy(s3.at[hop], r3.at[hop], RS_Z + hop, z_dev(hop))

    def rs_first(hop):
        s1[hop] = term(chip((z + hop) % NZ, 1 - y, 1 - x)).astype(BF16)
        rs_a(hop).start()
        rs_b(hop).start()

    def rs_second(hop):
        to_x = term(chip((z + hop) % NZ, y, 1 - x))
        rs_a(hop).wait_recv()
        s2x[hop, pl.ds(0, mid), :] = (to_x[:mid] + r1a[hop].astype(F32)).astype(BF16)
        s2x[hop, pl.ds(mid, mid), :] = to_x[mid:].astype(BF16)
        rs_x(hop).start()
        to_y = term(chip((z + hop) % NZ, 1 - y, x))
        rs_b(hop).wait_recv()
        s2y[hop, pl.ds(0, mid), :] = to_y[:mid].astype(BF16)
        s2y[hop, pl.ds(mid, mid), :] = (to_y[mid:] + r1b[hop].astype(F32)).astype(BF16)
        rs_y(hop).start()

    for hop in (1, 2, 3, 0):
        rs_first(hop)
    ag_second(3)
    lax.fori_loop(0, tiles, fwd_states, 0)
    fwd_copy = copy(ends_f, enter_f, FWD_COPY, sibling)
    fwd_copy.start()

    for hop in (1, 2, 3, 0):
        rs_second(hop)
    ag_second(2)

    fwd_copy.wait_recv()

    def gate_tile(tile, carry):
        decay, lam, coef = modes_of(decay_ref, gain_ref, tile)
        run_within(series_f, impulse, result, tile, False)
        run_carried(decay, lam, coef, states_f, enter_f, core == 1, result, tile, False)
        lanes = lanes_of(tile)
        gate_ref[:, lanes] = grad_ref[:, lanes].astype(F32) * result[tile]
        return carry

    lax.fori_loop(0, tiles, gate_tile, 0)

    def own_sum(hop):
        total = term(chip((z + hop) % NZ, y, x))
        rs_x(hop).wait_recv()
        rs_y(hop).wait_recv()
        return total + r2x[hop].astype(F32) + r2y[hop].astype(F32)

    def rs_third(hop):
        s3[hop] = own_sum(hop).astype(BF16)
        rs_z(hop).start()

    rs_third(1)
    ag_third(1)
    rs_third(2)
    ag_third(3)
    rs_third(3)
    wg_send[...] = own_sum(0)
    ag_third(2)

    def ig_columns(hop):
        first = ((z - hop + NZ) % NZ) * 4 * block
        return pl.ds(pl.multiple_of(first, 4 * block), 4 * block)

    def ig_copy(hop):
        columns = ig_columns(hop)
        return copy(ig_send.at[:, columns], ig_recv.at[:, columns], IG_COPY + hop, sibling)

    def ig_part(hop):
        cz = (z - hop + NZ) % NZ
        ag_a(hop).wait_recv()
        ag_b(hop).wait_recv()
        for cy in range(2):
            first = pl.multiple_of(chip(cz, cy, 0) * block, 2 * block)
            part = dot(val_full[...], wfull[pl.ds(first, 2 * block), :], 1, 1)
            columns = pl.ds(first, 2 * block)
            top, bottom = part[:ROWS], part[ROWS:]
            ig_ref[:, columns] = jnp.where(core == 0, top, bottom)
            ig_send[:, columns] = jnp.where(core == 0, bottom, top)
        ig_copy(hop).start()

    def ig_finish(hop):
        columns = ig_columns(hop)
        ig_copy(hop).wait_recv()
        ig_ref[:, columns] += ig_recv[:, columns]

    ig_part(0)
    ig_part(1)
    ig_part(3)

    for hop in range(1, NZ):
        rs_z(hop).wait_recv()
        wg_send[...] += r3[hop].astype(F32)
    wg_send[...] = scale * wg_send[...]
    wg_copy = copy(wg_send, wg_recv, WG_COPY, sibling)
    wg_copy.start()
    wg_ref[:, own_half] = wg_send[...]

    ig_part(2)
    wg_copy.wait_recv()
    wg_ref[:, other_half] = wg_recv[...]
    for hop in (0, 1, 3, 2):
        ig_finish(hop)

    for single in (in_copy, back_copy, fwd_copy, val_copy, wg_copy):
        single.wait_send()

    def drain(hop, carry):
        for each in (ag_x, ag_y, ag_a, ag_b, rs_a, rs_b, rs_x, rs_y, ig_copy):
            each(hop).wait_send()
        return carry

    def drain_z(hop, carry):
        ag_z(hop).wait_send()
        rs_z(hop).wait_send()
        return carry

    lax.fori_loop(0, NZ, drain, 0)
    lax.fori_loop(1, NZ, drain_z, 0)


def on_chip_grid(inputs, values, gating, out_grad, weight, decay_rate, mode_gain):
    rows, width = inputs.shape[1:]
    channels = values.shape[2]
    modes = decay_rate.shape[0]
    block = weight.shape[0]
    tiles, half, mid = channels // LANES, channels // 2, block // 2
    scale = 1.0 / math.sqrt(rows * lax.axis_size("ctx") * lax.axis_size("dp"))
    vmem = pl.BlockSpec(memory_space=pltpu.VMEM)
    series = pltpu.VMEM((tiles, rows, LANES), F32)
    states = pltpu.VMEM((tiles, modes, RUNS, LANES), F32)
    ends = pltpu.VMEM((tiles, modes, LANES), F32)
    blocks = pltpu.VMEM((NZ, block, half), BF16)
    halves = pltpu.VMEM((NZ, mid, half), BF16)
    in_grad, gate_grad, weight_grad = pl.pallas_call(
        functools.partial(chip_kernel, scale),
        out_shape=(
            jax.ShapeDtypeStruct((rows, width), F32),
            jax.ShapeDtypeStruct((rows, channels), F32),
            jax.ShapeDtypeStruct((block, channels), F32),
        ),
        in_specs=[vmem] * 7,
        out_specs=(vmem,) * 3,
        scratch_shapes=[
            series, series, series, pltpu.VMEM((tiles, RUN, LANES), F32), states, states,
            ends, ends, ends, ends,
            pltpu.VMEM((2 * rows, width), BF16),
            pltpu.VMEM((2 * rows, half), BF16),
            pltpu.VMEM((rows, half), BF16),
            pltpu.VMEM((width, half), BF16),
            blocks, halves, halves, blocks, blocks, blocks, blocks, blocks, blocks,
            pltpu.VMEM((rows, width), F32),
            pltpu.VMEM((rows, width), F32),
            pltpu.VMEM((block, half), F32),
            pltpu.VMEM((block, half), F32),
            pltpu.SemaphoreType.DMA((COPIES,)),
            pltpu.SemaphoreType.DMA((COPIES,)),
        ],
        compiler_params=pltpu.CompilerParams(
            collective_id=0, has_side_effects=True, vmem_limit_bytes=56 * 1024 * 1024
        ),
    )(inputs[0], values[0], gating[0], out_grad[0], weight, decay_rate, mode_gain)
    return (in_grad[None], gate_grad[None], weight_grad)


def fits_chip_grid(mesh):
    return mesh.shape["ctx"] == 2 and mesh.shape["dp"] == 4 * NZ


def passed_along(block, axis, distance):
    devices = range(lax.axis_size(axis))
    route = [(i - distance, i) for i in devices if i - distance in devices]
    return lax.ppermute(block, axis, route)


def chain_combine(earlier, later):
    return (later[0] + later[1] * earlier[0], earlier[1] * later[1])


def power_rows(decay_rate, row_count, offset):
    steps = jnp.arange(row_count, dtype=jnp.float32) + offset
    return jnp.exp(-decay_rate[None, :, :] * steps[:, None, None])


def modal_tables(decay_rate, mode_gain, block_len):
    mode_coef = mode_gain * jnp.sqrt(-jnp.expm1(-2.0 * decay_rate))
    power_table = power_rows(decay_rate, block_len, 0.0)
    impulse = jnp.sum(mode_coef[None] * power_table, axis=1)
    sum_weights = power_table[::-1]
    inject_table = mode_coef[None] * power_rows(decay_rate, block_len, 1.0)
    step_decay = jnp.exp(-decay_rate * block_len)
    return (impulse, sum_weights, inject_table, step_decay)


def local_pass(series, tables):
    impulse, sum_weights, inject_table, step_decay = tables
    block_len = impulse.shape[0]
    mode_count = sum_weights.shape[1]
    blocked = series.reshape(-1, block_len, series.shape[-1])
    within_block = impulse[0][None, None, :] * blocked
    for lag_step in range(1, block_len):
        shifted = jnp.pad(blocked[:, : block_len - lag_step], ((0, 0), (lag_step, 0), (0, 0)))
        within_block = within_block + impulse[lag_step][None, None, :] * shifted
    block_sums = jnp.zeros((blocked.shape[0], mode_count, blocked.shape[2]), jnp.float32)
    for row_step in range(block_len):
        block_sums = block_sums + sum_weights[row_step][None] * blocked[:, row_step][:, None, :]
    block_decay = jnp.broadcast_to(step_decay, block_sums.shape)
    end_state, end_decay = lax.associative_scan(chain_combine, (block_sums, block_decay), axis=0)
    return (within_block, end_state, end_decay)


def finish_pass(within_block, end_state, end_decay, incoming, inject_table):
    total_state = end_state + end_decay * incoming[None]
    prior_state = jnp.concatenate([incoming[None], total_state[:-1]], axis=0)
    carried = within_block
    for mode_step in range(inject_table.shape[1]):
        carried = carried + inject_table[:, mode_step][None] * prior_state[:, mode_step][:, None, :]
    return carried.reshape(-1, within_block.shape[-1])


def entering(fwd_own, fwd_span, back_own, back_span):
    empty_state = jnp.zeros_like(fwd_own)
    n_ctx = lax.axis_size("ctx")

    def fwd_step(step_index, loop_state):
        received = passed_along(loop_state[1], "ctx", 1)
        return (received, fwd_own + fwd_span * received)

    def back_step(step_index, loop_state):
        received = passed_along(loop_state[1], "ctx", -1)
        return (received, back_own + back_span * received)

    fwd_in = lax.fori_loop(0, n_ctx - 1, fwd_step, (empty_state, fwd_own))[0]
    back_in = lax.fori_loop(0, n_ctx - 1, back_step, (empty_state, back_own))[0]
    return (fwd_in, back_in)


def on_device(inputs, values, gating, out_grad, weight, decay_rate, mode_gain):
    in_rows = inputs[0]
    tok_rows = in_rows.shape[0]
    n_ctx = lax.axis_size("ctx")
    n_dp = lax.axis_size("dp")
    tables = modal_tables(decay_rate, mode_gain, 16)
    fwd_within, fwd_end, fwd_decay = local_pass(values[0].astype(jnp.float32), tables)
    mix_grad = gating[0].astype(jnp.float32) * out_grad[0].astype(jnp.float32)
    back_within, back_end, back_decay = local_pass(jnp.flip(mix_grad, 0), tables)
    fwd_in, back_in = entering(fwd_end[-1], fwd_decay[-1], back_end[-1], back_decay[-1])
    val_grad = jnp.flip(
        finish_pass(back_within, back_end, back_decay, back_in, tables[2]), 0
    ).astype(jnp.bfloat16)
    mixed = finish_pass(fwd_within, fwd_end, fwd_decay, fwd_in, tables[2])
    gate_grad = out_grad[0].astype(jnp.float32) * mixed
    in_grad = lax.dot_general(
        val_grad,
        lax.all_gather(weight, "dp", axis=0, tiled=True),
        (((1,), (1,)), ((), ())),
        preferred_element_type=jnp.float32,
    )
    norm_factor = 1.0 / math.sqrt(tok_rows * n_ctx * n_dp)
    share = lax.psum_scatter(
        norm_factor
        * lax.dot_general(
            in_rows, val_grad, (((0,), (0,)), ((), ())), preferred_element_type=jnp.float32
        ),
        "dp",
        scatter_dimension=0,
        tiled=True,
    )
    weight_grad = lax.psum(share, "ctx")
    return (in_grad[None], gate_grad[None], weight_grad)


def solution(mesh):
    placed = (
        P("dp", "ctx", None),
        P("dp", "ctx", None),
        P("dp", "ctx", None),
        P("dp", "ctx", None),
        P("dp", None),
        P(),
        P(),
    )
    step = on_chip_grid if fits_chip_grid(mesh) else on_device
    return jax.shard_map(
        step,
        mesh=mesh,
        in_specs=placed,
        out_specs=(P("dp", "ctx", None), P("dp", "ctx", None), P("dp", None)),
        check_vma=False,
    )
```

```python
import functools
import math

import jax
import jax.numpy as jnp
from jax import lax
from jax.experimental import pallas as pl
from jax.experimental.pallas import tpu as pltpu
from jax.sharding import PartitionSpec as P

MESH = pl.DeviceIdType.MESH
F32 = jnp.float32
BF16 = jnp.bfloat16
LANES = 128
RUN = 16
RUNS = 8
ROWS = RUN * RUNS
NZ = 4

IN_COPY, BACK_COPY, FWD_COPY, VAL_COPY, WG_COPY = range(5)
AG_Z, AG_X, AG_Y, AG_A, AG_B, RS_A, RS_B, RS_X, RS_Y, RS_Z, IG_COPY, AG_P = range(5, 53, 4)
COPIES = 53


def dot(lhs, rhs, lhs_dim, rhs_dim):
    return lax.dot_general(
        lhs, rhs, (((lhs_dim,), (rhs_dim,)), ((), ())), preferred_element_type=F32
    )


def lanes_of(tile):
    return pl.ds(pl.multiple_of(tile * LANES, LANES), LANES)


def run_rows(step):
    return pl.ds(step, RUNS, RUN)


def row_index():
    return lax.broadcasted_iota(jnp.int32, (RUNS, LANES), 0)


def shifted_runs(state, by, reverse):
    rows = row_index()
    if reverse:
        return jnp.where(rows < RUNS - by, pltpu.roll(state, RUNS - by, 0), 0.0)
    return jnp.where(rows >= by, pltpu.roll(state, by, 0), 0.0)


def spread(row):
    return jnp.broadcast_to(row, (RUNS, LANES))


def one_less_exp(u):
    series = 1.0
    for order in range(8, 1, -1):
        series = 1.0 - u * (1.0 / order) * series
    return jnp.where(u > 0.25, 1.0 - jnp.exp(-u), u * series)


def modes_of(decay_ref, gain_ref, tile):
    decay = decay_ref[:, lanes_of(tile)]
    lam = jnp.exp(-decay)
    coef = gain_ref[:, lanes_of(tile)] * jnp.sqrt(one_less_exp(2.0 * decay))
    return decay, lam, coef


def in_order(reverse):
    return range(RUN - 1, -1, -1) if reverse else range(RUN)


def run_states(series, decay, lam, states, ends, tile, reverse):
    modes = range(decay.shape[0])
    rates = [spread(lam[mode : mode + 1]) for mode in modes]
    held = None
    for step in in_order(reverse):
        column = series[tile, run_rows(step), :]
        held = [column] * len(rates) if held is None else [r * h + column for r, h in zip(rates, held)]
    over_run = jnp.exp(-float(RUN) * decay)
    spans = [spread(over_run[mode : mode + 1]) for mode in modes]
    for by in (1, 2, 4):
        held = [h + s * shifted_runs(h, by, reverse) for h, s in zip(held, spans)]
        spans = [s * s for s in spans]
    last = 0 if reverse else RUNS - 1
    for mode in modes:
        states[tile, mode] = held[mode]
        ends[tile, mode : mode + 1, :] = held[mode][last : last + 1]


def added(terms):
    while len(terms) > 1:
        odd = terms[-1:] if len(terms) % 2 else []
        terms = [a + b for a, b in zip(terms[::2], terms[1::2])] + odd
    return terms[0]


def run_within(series, impulse, result, tile, reverse):
    order = list(in_order(reverse))
    steps = [series[tile, run_rows(step), :] for step in order]
    lags = [spread(impulse[tile, lag : lag + 1, :]) for lag in range(RUN)]
    for at, step in enumerate(order):
        result[tile, run_rows(step), :] = added([lags[at - b] * steps[b] for b in range(at + 1)])


def run_carried(decay, lam, coef, states, incoming, enters, result, tile, reverse):
    ahead = row_index()
    ahead = (RUNS - 1 - ahead if reverse else ahead).astype(F32) * float(RUN)
    rates, carried = [], []
    for mode in range(decay.shape[0]):
        rate = spread(lam[mode : mode + 1])
        entry = jnp.where(enters, spread(incoming[tile, mode : mode + 1, :]), 0.0)
        prior = shifted_runs(states[tile, mode], 1, reverse)
        prior = prior + jnp.exp(-ahead * spread(decay[mode : mode + 1])) * entry
        rates.append(rate)
        carried.append(spread(coef[mode : mode + 1]) * rate * prior)
    for step in in_order(reverse):
        result[tile, run_rows(step), :] += added(carried)
        carried = [rate * item for rate, item in zip(rates, carried)]


def chip_kernel(
    scale,
    in_hbm, values_hbm, gating_hbm, grad_hbm, weight_hbm, decay_ref, gain_ref,
    ig_ref, gate_ref, wg_ref,
    values_ref, gating_ref, grad_ref, series_f, series_b, result, impulse, states_f, states_b,
    ends_f, ends_b, enter_f, enter_b,
    in_full, val_full, val_send, wfull,
    s1, r1a, r1b, s2x, s2y, r2x, r2y, s3, r3,
    ig_send, ig_recv, wg_send, wg_recv,
    send_sem, recv_sem, load_sem,
):
    core = lax.axis_index("ctx")
    dp = lax.axis_index("dp")
    z, y, x = dp // 4, (dp // 2) % 2, dp % 2
    tiles = series_f.shape[0]
    half_tiles = tiles // 2
    half = half_tiles * LANES
    block = weight_hbm.shape[0]
    mid = block // 2
    cut = block // 4

    def chip(cz, cy, cx):
        return cz * 4 + cy * 2 + cx

    sibling = (1 - core, dp)
    x_dev = (core, chip(z, y, 1 - x))
    y_dev = (core, chip(z, 1 - y, x))

    def z_dev(hop):
        return (core, chip((z + hop) % NZ, y, x))

    def copy(src, dst, which, device):
        return pltpu.make_async_remote_copy(
            src_ref=src, dst_ref=dst, send_sem=send_sem.at[which], recv_sem=recv_sem.at[which],
            device_id=device, device_id_type=MESH,
        )

    own_half = pl.ds(pl.multiple_of(core * half, half), half)
    other_half = pl.ds(pl.multiple_of((1 - core) * half, half), half)
    own_rows = pl.ds(pl.multiple_of(core * ROWS, ROWS), ROWS)

    def load(src, dst, which):
        return pltpu.make_async_copy(src, dst, load_sem.at[which])

    weight_load = load(weight_hbm.at[:, own_half], wfull.at[dp], 0)
    gating_load = load(gating_hbm, gating_ref, 1)
    grad_load = load(grad_hbm, grad_ref, 2)
    in_load = load(in_hbm, in_full.at[own_rows, :], 3)
    values_load = load(values_hbm, values_ref, 4)
    for each in (weight_load, gating_load, grad_load, in_load, values_load):
        each.start()

    barrier = pltpu.get_barrier_semaphore()
    partners = [sibling, x_dev, y_dev] + [z_dev(hop) for hop in range(1, NZ)]
    for device in partners:
        pl.semaphore_signal(barrier, inc=1, device_id=device, device_id_type=MESH)
    pl.semaphore_wait(barrier, len(partners))

    def wrows(index, start=0, size=block):
        return wfull.at[index, pl.ds(start, size), :]

    weight_load.wait()

    def from_hop(hop):
        return (z - hop + NZ) % NZ

    def ag_z(hop):
        rows = wrows(dp, cut, block - cut)
        return copy(rows, rows, AG_Z + hop, z_dev(hop))

    def ag_p(hop):
        rows = wfull.at[pl.ds(z * 4, 4), pl.ds(0, cut), :]
        return copy(rows, rows, AG_P + hop, z_dev(hop))

    def whole(hop, cy, cx):
        index = chip(from_hop(hop), cy, cx)
        return wrows(index, cut, block - cut) if hop else wrows(index)

    def first_part(hop, cy, cx):
        index = chip(from_hop(hop), cy, cx)
        return wrows(index, cut, (block - cut) // 2) if hop else wrows(index, 0, mid)

    def second_part(hop, cy, cx):
        index = chip(from_hop(hop), cy, cx)
        size = (block - cut) // 2 if hop else mid
        return wrows(index, block - size, size)

    def ag_x(hop):
        rows = whole(hop, y, x)
        return copy(rows, rows, AG_X + hop, x_dev)

    def ag_y(hop):
        rows = whole(hop, y, x)
        return copy(rows, rows, AG_Y + hop, y_dev)

    def ag_a(hop):
        rows = first_part(hop, y, 1 - x)
        return copy(rows, rows, AG_A + hop, y_dev)

    def ag_b(hop):
        rows = second_part(hop, 1 - y, x)
        return copy(rows, rows, AG_B + hop, x_dev)

    def ag_second(hop):
        ag_z(hop).wait_recv()
        ag_x(hop).start()
        ag_y(hop).start()

    def ag_third(hop):
        ag_x(hop).wait_recv()
        ag_a(hop).start()
        ag_y(hop).wait_recv()
        ag_b(hop).start()

    ag_z(1).start()
    ag_x(0).start()
    ag_y(0).start()
    in_copy = copy(in_hbm, in_full.at[own_rows, :], IN_COPY, sibling)
    in_copy.start()
    gating_load.wait()
    grad_load.wait()

    def back_states(tile, carry):
        lanes = lanes_of(tile)
        series_b[tile] = gating_ref[:, lanes].astype(F32) * grad_ref[:, lanes].astype(F32)
        decay, lam, coef = modes_of(decay_ref, gain_ref, tile)
        power = coef
        for lag in range(RUN):
            impulse[tile, lag : lag + 1, :] = jnp.sum(power, axis=0, keepdims=True)
            power = power * lam
        run_states(series_b, decay, lam, states_b, ends_b, tile, True)
        return carry

    def fwd_states(tile, carry):
        series_f[tile] = values_ref[:, lanes_of(tile)].astype(F32)
        decay, lam, coef = modes_of(decay_ref, gain_ref, tile)
        run_states(series_f, decay, lam, states_f, ends_f, tile, False)
        return carry

    lax.fori_loop(0, tiles, back_states, 0)
    back_copy = copy(ends_b, enter_b, BACK_COPY, sibling)
    back_copy.start()
    ag_z(3).start()

    def back_within(tile, carry):
        run_within(series_b, impulse, result, tile, True)
        return carry

    lax.fori_loop(0, tiles, back_within, 0)
    back_copy.wait_recv()

    def val_tile(tile):
        decay, lam, coef = modes_of(decay_ref, gain_ref, tile)
        run_carried(decay, lam, coef, states_b, enter_b, core == 0, result, tile, True)
        return result[tile].astype(BF16)

    def val_other(tile, carry):
        val_send[:, lanes_of(tile)] = val_tile((1 - core) * half_tiles + tile)
        return carry

    def val_own(tile, carry):
        val_full[own_rows, lanes_of(tile)] = val_tile(core * half_tiles + tile)
        return carry

    lax.fori_loop(0, half_tiles, val_other, 0)
    val_copy = copy(val_send, val_full.at[own_rows, :], VAL_COPY, sibling)
    val_copy.start()
    ag_second(1)
    ag_third(0)
    lax.fori_loop(0, half_tiles, val_own, 0)
    ag_z(2).start()
    in_load.wait()
    in_copy.wait_recv()
    val_copy.wait_recv()

    def term(index):
        columns = pl.ds(pl.multiple_of(index * block, block), block)
        return dot(in_full[:, columns], val_full[...], 0, 0)

    def rs_a(hop):
        return copy(s1.at[hop, pl.ds(0, mid), :], r1a.at[hop], RS_A + hop, y_dev)

    def rs_b(hop):
        return copy(s1.at[hop, pl.ds(mid, mid), :], r1b.at[hop], RS_B + hop, x_dev)

    def rs_x(hop):
        return copy(s2x.at[hop], r2x.at[hop], RS_X + hop, x_dev)

    def rs_y(hop):
        return copy(s2y.at[hop], r2y.at[hop], RS_Y + hop, y_dev)

    def rs_z(hop):
        return copy(s3.at[hop], r3.at[hop], RS_Z + hop, z_dev(hop))

    def rs_first(hop):
        s1[hop] = term(chip((z + hop) % NZ, 1 - y, 1 - x)).astype(BF16)
        rs_a(hop).start()
        rs_b(hop).start()

    def rs_second(hop):
        to_x = term(chip((z + hop) % NZ, y, 1 - x))
        rs_a(hop).wait_recv()
        s2x[hop, pl.ds(0, mid), :] = (to_x[:mid] + r1a[hop].astype(F32)).astype(BF16)
        s2x[hop, pl.ds(mid, mid), :] = to_x[mid:].astype(BF16)
        rs_x(hop).start()
        to_y = term(chip((z + hop) % NZ, 1 - y, x))
        rs_b(hop).wait_recv()
        s2y[hop, pl.ds(0, mid), :] = to_y[:mid].astype(BF16)
        s2y[hop, pl.ds(mid, mid), :] = (to_y[mid:] + r1b[hop].astype(F32)).astype(BF16)
        rs_y(hop).start()

    for hop in (1, 2, 3, 0):
        rs_first(hop)
    ag_second(3)
    ag_a(0).wait_recv()
    for hop in (1, 3, 2):
        ag_p(hop).start()
    values_load.wait()
    lax.fori_loop(0, tiles, fwd_states, 0)
    fwd_copy = copy(ends_f, enter_f, FWD_COPY, sibling)
    fwd_copy.start()

    for hop in (1, 2, 3, 0):
        rs_second(hop)
    ag_second(2)

    fwd_copy.wait_recv()

    def gate_tile(tile, carry):
        decay, lam, coef = modes_of(decay_ref, gain_ref, tile)
        run_within(series_f, impulse, result, tile, False)
        run_carried(decay, lam, coef, states_f, enter_f, core == 1, result, tile, False)
        lanes = lanes_of(tile)
        gate_ref[:, lanes] = grad_ref[:, lanes].astype(F32) * result[tile]
        return carry

    lax.fori_loop(0, tiles, gate_tile, 0)

    def own_sum(hop):
        total = term(chip((z + hop) % NZ, y, x))
        rs_x(hop).wait_recv()
        rs_y(hop).wait_recv()
        return total + r2x[hop].astype(F32) + r2y[hop].astype(F32)

    def rs_third(hop):
        s3[hop] = own_sum(hop).astype(BF16)
        rs_z(hop).start()

    rs_third(1)
    ag_third(1)
    rs_third(2)
    ag_third(3)
    rs_third(3)
    wg_send[...] = own_sum(0)
    ag_third(2)

    def ig_columns(hop):
        first = ((z - hop + NZ) % NZ) * 4 * block
        return pl.ds(pl.multiple_of(first, 4 * block), 4 * block)

    def ig_copy(hop):
        columns = ig_columns(hop)
        return copy(ig_send.at[:, columns], ig_recv.at[:, columns], IG_COPY + hop, sibling)

    def ig_part(hop):
        cz = (z - hop + NZ) % NZ
        if hop:
            ag_a(hop).wait_recv()
            ag_p(hop).wait_recv()
        ag_b(hop).wait_recv()
        for cy in range(2):
            pair = chip(cz, cy, 0)
            first = pl.multiple_of(pair * block, 2 * block)
            rows = wfull[pl.ds(pair, 2)].reshape(2 * block, half)
            part = dot(val_full[...], rows, 1, 1)
            columns = pl.ds(first, 2 * block)
            top, bottom = part[:ROWS], part[ROWS:]
            ig_ref[:, columns] = jnp.where(core == 0, top, bottom)
            ig_send[:, columns] = jnp.where(core == 0, bottom, top)
        ig_copy(hop).start()

    def ig_finish(hop):
        columns = ig_columns(hop)
        ig_copy(hop).wait_recv()
        ig_ref[:, columns] += ig_recv[:, columns]

    ig_part(0)
    ig_part(1)
    ig_part(3)

    for hop in range(1, NZ):
        rs_z(hop).wait_recv()
        wg_send[...] += r3[hop].astype(F32)
    wg_send[...] = scale * wg_send[...]
    wg_copy = copy(wg_send, wg_recv, WG_COPY, sibling)
    wg_copy.start()
    wg_ref[:, own_half] = wg_send[...]

    ig_part(2)
    wg_copy.wait_recv()
    wg_ref[:, other_half] = wg_recv[...]
    for hop in (0, 1, 3, 2):
        ig_finish(hop)

    for single in (in_copy, back_copy, fwd_copy, val_copy, wg_copy):
        single.wait_send()

    for hop in range(NZ):
        for each in (ag_x, ag_y, ag_a, ag_b, rs_a, rs_b, rs_x, rs_y, ig_copy):
            each(hop).wait_send()
        if hop:
            for each in (ag_z, ag_p, rs_z):
                each(hop).wait_send()


def on_chip_grid(inputs, values, gating, out_grad, weight, decay_rate, mode_gain):
    rows, width = inputs.shape[1:]
    channels = values.shape[2]
    modes = decay_rate.shape[0]
    block = weight.shape[0]
    tiles, half, mid = channels // LANES, channels // 2, block // 2
    scale = 1.0 / math.sqrt(rows * lax.axis_size("ctx") * lax.axis_size("dp"))
    vmem = pl.BlockSpec(memory_space=pltpu.VMEM)
    series = pltpu.VMEM((tiles, rows, LANES), F32)
    states = pltpu.VMEM((tiles, modes, RUNS, LANES), F32)
    ends = pltpu.VMEM((tiles, modes, LANES), F32)
    blocks = pltpu.VMEM((NZ, block, half), BF16)
    halves = pltpu.VMEM((NZ, mid, half), BF16)
    in_grad, gate_grad, weight_grad = pl.pallas_call(
        functools.partial(chip_kernel, scale),
        out_shape=(
            jax.ShapeDtypeStruct((rows, width), F32),
            jax.ShapeDtypeStruct((rows, channels), F32),
            jax.ShapeDtypeStruct((block, channels), F32),
        ),
        in_specs=[pl.BlockSpec(memory_space=pl.ANY)] * 5 + [vmem] * 2,
        out_specs=(vmem,) * 3,
        scratch_shapes=[
            pltpu.VMEM((rows, channels), BF16),
            pltpu.VMEM((rows, channels), BF16),
            pltpu.VMEM((rows, channels), BF16),
            series, series, series, pltpu.VMEM((tiles, RUN, LANES), F32), states, states,
            ends, ends, ends, ends,
            pltpu.VMEM((2 * rows, width), BF16),
            pltpu.VMEM((2 * rows, half), BF16),
            pltpu.VMEM((rows, half), BF16),
            pltpu.VMEM((width // block, block, half), BF16),
            blocks, halves, halves, blocks, blocks, blocks, blocks, blocks, blocks,
            pltpu.VMEM((rows, width), F32),
            pltpu.VMEM((rows, width), F32),
            pltpu.VMEM((block, half), F32),
            pltpu.VMEM((block, half), F32),
            pltpu.SemaphoreType.DMA((COPIES,)),
            pltpu.SemaphoreType.DMA((COPIES,)),
            pltpu.SemaphoreType.DMA((5,)),
        ],
        compiler_params=pltpu.CompilerParams(
            collective_id=0, has_side_effects=True, vmem_limit_bytes=56 * 1024 * 1024
        ),
    )(inputs[0], values[0], gating[0], out_grad[0], weight, decay_rate, mode_gain)
    return (in_grad[None], gate_grad[None], weight_grad)


def fits_chip_grid(mesh):
    return mesh.shape["ctx"] == 2 and mesh.shape["dp"] == 4 * NZ


def passed_along(block, axis, distance):
    devices = range(lax.axis_size(axis))
    route = [(i - distance, i) for i in devices if i - distance in devices]
    return lax.ppermute(block, axis, route)


def chain_combine(earlier, later):
    return (later[0] + later[1] * earlier[0], earlier[1] * later[1])


def power_rows(decay_rate, row_count, offset):
    steps = jnp.arange(row_count, dtype=jnp.float32) + offset
    return jnp.exp(-decay_rate[None, :, :] * steps[:, None, None])


def modal_tables(decay_rate, mode_gain, block_len):
    mode_coef = mode_gain * jnp.sqrt(-jnp.expm1(-2.0 * decay_rate))
    power_table = power_rows(decay_rate, block_len, 0.0)
    impulse = jnp.sum(mode_coef[None] * power_table, axis=1)
    sum_weights = power_table[::-1]
    inject_table = mode_coef[None] * power_rows(decay_rate, block_len, 1.0)
    step_decay = jnp.exp(-decay_rate * block_len)
    return (impulse, sum_weights, inject_table, step_decay)


def local_pass(series, tables):
    impulse, sum_weights, inject_table, step_decay = tables
    block_len = impulse.shape[0]
    mode_count = sum_weights.shape[1]
    blocked = series.reshape(-1, block_len, series.shape[-1])
    within_block = impulse[0][None, None, :] * blocked
    for lag_step in range(1, block_len):
        shifted = jnp.pad(blocked[:, : block_len - lag_step], ((0, 0), (lag_step, 0), (0, 0)))
        within_block = within_block + impulse[lag_step][None, None, :] * shifted
    block_sums = jnp.zeros((blocked.shape[0], mode_count, blocked.shape[2]), jnp.float32)
    for row_step in range(block_len):
        block_sums = block_sums + sum_weights[row_step][None] * blocked[:, row_step][:, None, :]
    block_decay = jnp.broadcast_to(step_decay, block_sums.shape)
    end_state, end_decay = lax.associative_scan(chain_combine, (block_sums, block_decay), axis=0)
    return (within_block, end_state, end_decay)


def finish_pass(within_block, end_state, end_decay, incoming, inject_table):
    total_state = end_state + end_decay * incoming[None]
    prior_state = jnp.concatenate([incoming[None], total_state[:-1]], axis=0)
    carried = within_block
    for mode_step in range(inject_table.shape[1]):
        carried = carried + inject_table[:, mode_step][None] * prior_state[:, mode_step][:, None, :]
    return carried.reshape(-1, within_block.shape[-1])


def entering(fwd_own, fwd_span, back_own, back_span):
    empty_state = jnp.zeros_like(fwd_own)
    n_ctx = lax.axis_size("ctx")

    def fwd_step(step_index, loop_state):
        received = passed_along(loop_state[1], "ctx", 1)
        return (received, fwd_own + fwd_span * received)

    def back_step(step_index, loop_state):
        received = passed_along(loop_state[1], "ctx", -1)
        return (received, back_own + back_span * received)

    fwd_in = lax.fori_loop(0, n_ctx - 1, fwd_step, (empty_state, fwd_own))[0]
    back_in = lax.fori_loop(0, n_ctx - 1, back_step, (empty_state, back_own))[0]
    return (fwd_in, back_in)


def on_device(inputs, values, gating, out_grad, weight, decay_rate, mode_gain):
    in_rows = inputs[0]
    tok_rows = in_rows.shape[0]
    n_ctx = lax.axis_size("ctx")
    n_dp = lax.axis_size("dp")
    tables = modal_tables(decay_rate, mode_gain, 16)
    fwd_within, fwd_end, fwd_decay = local_pass(values[0].astype(jnp.float32), tables)
    mix_grad = gating[0].astype(jnp.float32) * out_grad[0].astype(jnp.float32)
    back_within, back_end, back_decay = local_pass(jnp.flip(mix_grad, 0), tables)
    fwd_in, back_in = entering(fwd_end[-1], fwd_decay[-1], back_end[-1], back_decay[-1])
    val_grad = jnp.flip(
        finish_pass(back_within, back_end, back_decay, back_in, tables[2]), 0
    ).astype(jnp.bfloat16)
    mixed = finish_pass(fwd_within, fwd_end, fwd_decay, fwd_in, tables[2])
    gate_grad = out_grad[0].astype(jnp.float32) * mixed
    in_grad = lax.dot_general(
        val_grad,
        lax.all_gather(weight, "dp", axis=0, tiled=True),
        (((1,), (1,)), ((), ())),
        preferred_element_type=jnp.float32,
    )
    norm_factor = 1.0 / math.sqrt(tok_rows * n_ctx * n_dp)
    share = lax.psum_scatter(
        norm_factor
        * lax.dot_general(
            in_rows, val_grad, (((0,), (0,)), ((), ())), preferred_element_type=jnp.float32
        ),
        "dp",
        scatter_dimension=0,
        tiled=True,
    )
    weight_grad = lax.psum(share, "ctx")
    return (in_grad[None], gate_grad[None], weight_grad)


def solution(mesh):
    placed = (
        P("dp", "ctx", None),
        P("dp", "ctx", None),
        P("dp", "ctx", None),
        P("dp", "ctx", None),
        P("dp", None),
        P(),
        P(),
    )
    step = on_chip_grid if fits_chip_grid(mesh) else on_device
    return jax.shard_map(
        step,
        mesh=mesh,
        in_specs=placed,
        out_specs=(P("dp", "ctx", None), P("dp", "ctx", None), P("dp", None)),
        check_vma=False,
    )
```

```python
import functools
import math

import jax
import jax.numpy as jnp
from jax import lax
from jax.experimental import pallas as pl
from jax.experimental.pallas import tpu as pltpu
from jax.sharding import PartitionSpec as P

MESH = pl.DeviceIdType.MESH
F32 = jnp.float32
BF16 = jnp.bfloat16
LANES = 128
RUN = 16
RUNS = 8
ROWS = RUN * RUNS
NZ = 4

IN_COPY, BACK_COPY, FWD_COPY, VAL_COPY, WG_COPY = range(5)
AG_Z, AG_X, AG_Y, AG_A, AG_B, RS_A, RS_B, RS_X, RS_Y, RS_Z, IG_COPY, AG_P = range(5, 53, 4)
COPIES = 53


def dot(lhs, rhs, lhs_dim, rhs_dim):
    return lax.dot_general(
        lhs, rhs, (((lhs_dim,), (rhs_dim,)), ((), ())), preferred_element_type=F32
    )


def lanes_of(tile):
    return pl.ds(pl.multiple_of(tile * LANES, LANES), LANES)


def run_rows(step):
    return pl.ds(step, RUNS, RUN)


def row_index():
    return lax.broadcasted_iota(jnp.int32, (RUNS, LANES), 0)


def shifted_runs(state, by, reverse):
    rows = row_index()
    if reverse:
        return jnp.where(rows < RUNS - by, pltpu.roll(state, RUNS - by, 0), 0.0)
    return jnp.where(rows >= by, pltpu.roll(state, by, 0), 0.0)


def spread(row):
    return jnp.broadcast_to(row, (RUNS, LANES))


def one_less_exp(u):
    series = 1.0
    for order in range(8, 1, -1):
        series = 1.0 - u * (1.0 / order) * series
    return jnp.where(u > 0.25, 1.0 - jnp.exp(-u), u * series)


def modes_of(decay_ref, gain_ref, tile):
    decay = decay_ref[:, lanes_of(tile)]
    lam = jnp.exp(-decay)
    coef = gain_ref[:, lanes_of(tile)] * jnp.sqrt(one_less_exp(2.0 * decay))
    return decay, lam, coef


def in_order(reverse):
    return range(RUN - 1, -1, -1) if reverse else range(RUN)


def run_states(series, decay, lam, states, ends, tile, reverse):
    modes = range(decay.shape[0])
    rates = [spread(lam[mode : mode + 1]) for mode in modes]
    held = None
    for step in in_order(reverse):
        column = series[tile, run_rows(step), :]
        held = [column] * len(rates) if held is None else [r * h + column for r, h in zip(rates, held)]
    over_run = jnp.exp(-float(RUN) * decay)
    spans = [spread(over_run[mode : mode + 1]) for mode in modes]
    for by in (1, 2, 4):
        held = [h + s * shifted_runs(h, by, reverse) for h, s in zip(held, spans)]
        spans = [s * s for s in spans]
    last = 0 if reverse else RUNS - 1
    for mode in modes:
        states[tile, mode] = held[mode]
        ends[tile, mode : mode + 1, :] = held[mode][last : last + 1]


def added(terms):
    while len(terms) > 1:
        odd = terms[-1:] if len(terms) % 2 else []
        terms = [a + b for a, b in zip(terms[::2], terms[1::2])] + odd
    return terms[0]


def run_within(series, impulse, result, tile, reverse):
    order = list(in_order(reverse))
    steps = [series[tile, run_rows(step), :] for step in order]
    lags = [spread(impulse[tile, lag : lag + 1, :]) for lag in range(RUN)]
    for at, step in enumerate(order):
        result[tile, run_rows(step), :] = added([lags[at - b] * steps[b] for b in range(at + 1)])


def run_carried(decay, lam, coef, states, incoming, enters, result, tile, reverse):
    ahead = row_index()
    ahead = (RUNS - 1 - ahead if reverse else ahead).astype(F32) * float(RUN)
    rates, carried = [], []
    for mode in range(decay.shape[0]):
        rate = spread(lam[mode : mode + 1])
        entry = jnp.where(enters, spread(incoming[tile, mode : mode + 1, :]), 0.0)
        prior = shifted_runs(states[tile, mode], 1, reverse)
        prior = prior + jnp.exp(-ahead * spread(decay[mode : mode + 1])) * entry
        rates.append(rate)
        carried.append(spread(coef[mode : mode + 1]) * rate * prior)
    for step in in_order(reverse):
        result[tile, run_rows(step), :] += added(carried)
        carried = [rate * item for rate, item in zip(rates, carried)]


def chip_kernel(
    scale,
    in_hbm, values_hbm, gating_hbm, grad_hbm, weight_hbm, decay_ref, gain_ref,
    ig_ref, gate_ref, wg_ref,
    values_ref, gating_ref, grad_ref, series_f, series_b, result, impulse, states_f, states_b,
    ends_f, ends_b, enter_f, enter_b,
    in_full, val_full, val_send, wfull,
    s1, r1a, r1b, s2x, s2y, r2x, r2y, s3, r3,
    ig_send, ig_recv, wg_send, wg_recv,
    send_sem, recv_sem, load_sem,
):
    core = lax.axis_index("ctx")
    dp = lax.axis_index("dp")
    z, y, x = dp // 4, (dp // 2) % 2, dp % 2
    tiles = series_f.shape[0]
    half_tiles = tiles // 2
    half = half_tiles * LANES
    block = weight_hbm.shape[0]
    mid = block // 2
    cut = block // 4

    def chip(cz, cy, cx):
        return cz * 4 + cy * 2 + cx

    sibling = (1 - core, dp)
    x_dev = (core, chip(z, y, 1 - x))
    y_dev = (core, chip(z, 1 - y, x))

    def z_dev(hop):
        return (core, chip((z + hop) % NZ, y, x))

    def copy(src, dst, which, device):
        return pltpu.make_async_remote_copy(
            src_ref=src, dst_ref=dst, send_sem=send_sem.at[which], recv_sem=recv_sem.at[which],
            device_id=device, device_id_type=MESH,
        )

    own_half = pl.ds(pl.multiple_of(core * half, half), half)
    other_half = pl.ds(pl.multiple_of((1 - core) * half, half), half)
    own_rows = pl.ds(pl.multiple_of(core * ROWS, ROWS), ROWS)

    def load(src, dst, which):
        return pltpu.make_async_copy(src, dst, load_sem.at[which])

    weight_load = load(weight_hbm.at[:, own_half], wfull.at[dp], 0)
    gating_load = load(gating_hbm, gating_ref, 1)
    grad_load = load(grad_hbm, grad_ref, 2)
    in_load = load(in_hbm, in_full.at[own_rows, :], 3)
    values_load = load(values_hbm, values_ref, 4)
    for each in (weight_load, gating_load, grad_load, in_load, values_load):
        each.start()

    barrier = pltpu.get_barrier_semaphore()
    partners = [sibling, x_dev, y_dev] + [z_dev(hop) for hop in range(1, NZ)]
    for device in partners:
        pl.semaphore_signal(barrier, inc=1, device_id=device, device_id_type=MESH)
    pl.semaphore_wait(barrier, len(partners))

    def wrows(index, start=0, size=block):
        return wfull.at[index, pl.ds(start, size), :]

    weight_load.wait()

    def from_hop(hop):
        return (z - hop + NZ) % NZ

    def ag_z(hop):
        rows = wrows(dp, cut, block - cut)
        return copy(rows, rows, AG_Z + hop, z_dev(hop))

    def ag_p(hop):
        rows = wfull.at[pl.ds(z * 4, 4), pl.ds(0, cut), :]
        return copy(rows, rows, AG_P + hop, z_dev(hop))

    def whole(hop, cy, cx):
        index = chip(from_hop(hop), cy, cx)
        return wrows(index, cut, block - cut) if hop else wrows(index)

    def first_part(hop, cy, cx):
        index = chip(from_hop(hop), cy, cx)
        return wrows(index, cut, (block - cut) // 2) if hop else wrows(index, 0, mid)

    def second_part(hop, cy, cx):
        index = chip(from_hop(hop), cy, cx)
        size = (block - cut) // 2 if hop else mid
        return wrows(index, block - size, size)

    def ag_x(hop):
        rows = whole(hop, y, x)
        return copy(rows, rows, AG_X + hop, x_dev)

    def ag_y(hop):
        rows = whole(hop, y, x)
        return copy(rows, rows, AG_Y + hop, y_dev)

    def ag_a(hop):
        rows = first_part(hop, y, 1 - x)
        return copy(rows, rows, AG_A + hop, y_dev)

    def ag_b(hop):
        rows = second_part(hop, 1 - y, x)
        return copy(rows, rows, AG_B + hop, x_dev)

    def ag_second(hop):
        ag_z(hop).wait_recv()
        ag_x(hop).start()
        ag_y(hop).start()

    def ag_third(hop):
        ag_x(hop).wait_recv()
        ag_a(hop).start()
        ag_y(hop).wait_recv()
        ag_b(hop).start()

    ag_z(1).start()
    ag_x(0).start()
    ag_y(0).start()
    in_copy = copy(in_hbm, in_full.at[own_rows, :], IN_COPY, sibling)
    in_copy.start()
    gating_load.wait()
    grad_load.wait()

    def back_states(tile, carry):
        lanes = lanes_of(tile)
        series_b[tile] = gating_ref[:, lanes].astype(F32) * grad_ref[:, lanes].astype(F32)
        decay, lam, coef = modes_of(decay_ref, gain_ref, tile)
        power = coef
        for lag in range(RUN):
            impulse[tile, lag : lag + 1, :] = jnp.sum(power, axis=0, keepdims=True)
            power = power * lam
        run_states(series_b, decay, lam, states_b, ends_b, tile, True)
        return carry

    def fwd_states(tile, carry):
        series_f[tile] = values_ref[:, lanes_of(tile)].astype(F32)
        decay, lam, coef = modes_of(decay_ref, gain_ref, tile)
        run_states(series_f, decay, lam, states_f, ends_f, tile, False)
        return carry

    lax.fori_loop(0, tiles, back_states, 0)
    back_copy = copy(ends_b, enter_b, BACK_COPY, sibling)
    back_copy.start()
    ag_z(3).start()

    def back_within(tile, carry):
        run_within(series_b, impulse, result, tile, True)
        return carry

    lax.fori_loop(0, tiles, back_within, 0)
    ag_z(2).start()
    ag_third(0)
    back_copy.wait_recv()

    def val_tile(tile):
        decay, lam, coef = modes_of(decay_ref, gain_ref, tile)
        run_carried(decay, lam, coef, states_b, enter_b, core == 0, result, tile, True)
        return result[tile].astype(BF16)

    def val_other(tile, carry):
        val_send[:, lanes_of(tile)] = val_tile((1 - core) * half_tiles + tile)
        return carry

    def val_own(tile, carry):
        val_full[own_rows, lanes_of(tile)] = val_tile(core * half_tiles + tile)
        return carry

    lax.fori_loop(0, half_tiles, val_other, 0)
    val_copy = copy(val_send, val_full.at[own_rows, :], VAL_COPY, sibling)
    val_copy.start()
    ag_second(1)
    lax.fori_loop(0, half_tiles, val_own, 0)
    in_load.wait()
    in_copy.wait_recv()
    val_copy.wait_recv()

    def term(index):
        columns = pl.ds(pl.multiple_of(index * block, block), block)
        return dot(in_full[:, columns], val_full[...], 0, 0)

    def rs_a(hop):
        return copy(s1.at[hop, pl.ds(0, mid), :], r1a.at[hop], RS_A + hop, y_dev)

    def rs_b(hop):
        return copy(s1.at[hop, pl.ds(mid, mid), :], r1b.at[hop], RS_B + hop, x_dev)

    def rs_x(hop):
        return copy(s2x.at[hop], r2x.at[hop], RS_X + hop, x_dev)

    def rs_y(hop):
        return copy(s2y.at[hop], r2y.at[hop], RS_Y + hop, y_dev)

    def rs_z(hop):
        return copy(s3.at[hop], r3.at[hop], RS_Z + hop, z_dev(hop))

    def rs_first(hop):
        s1[hop] = term(chip((z + hop) % NZ, 1 - y, 1 - x)).astype(BF16)
        rs_a(hop).start()
        rs_b(hop).start()

    def rs_second(hop):
        to_x = term(chip((z + hop) % NZ, y, 1 - x))
        rs_a(hop).wait_recv()
        s2x[hop, pl.ds(0, mid), :] = (to_x[:mid] + r1a[hop].astype(F32)).astype(BF16)
        s2x[hop, pl.ds(mid, mid), :] = to_x[mid:].astype(BF16)
        rs_x(hop).start()
        to_y = term(chip((z + hop) % NZ, 1 - y, x))
        rs_b(hop).wait_recv()
        s2y[hop, pl.ds(0, mid), :] = to_y[:mid].astype(BF16)
        s2y[hop, pl.ds(mid, mid), :] = (to_y[mid:] + r1b[hop].astype(F32)).astype(BF16)
        rs_y(hop).start()

    rs_first(1)
    ag_a(0).wait_recv()
    for hop in (1, 3, 2):
        ag_p(hop).start()
    for hop in (2, 3, 0):
        rs_first(hop)
    ag_second(3)
    values_load.wait()
    lax.fori_loop(0, tiles, fwd_states, 0)
    fwd_copy = copy(ends_f, enter_f, FWD_COPY, sibling)
    fwd_copy.start()

    for hop in (1, 2, 3, 0):
        rs_second(hop)
    ag_second(2)

    fwd_copy.wait_recv()

    def gate_tile(tile, carry):
        decay, lam, coef = modes_of(decay_ref, gain_ref, tile)
        run_within(series_f, impulse, result, tile, False)
        run_carried(decay, lam, coef, states_f, enter_f, core == 1, result, tile, False)
        lanes = lanes_of(tile)
        gate_ref[:, lanes] = grad_ref[:, lanes].astype(F32) * result[tile]
        return carry

    lax.fori_loop(0, tiles, gate_tile, 0)

    def own_sum(hop):
        total = term(chip((z + hop) % NZ, y, x))
        rs_x(hop).wait_recv()
        rs_y(hop).wait_recv()
        return total + r2x[hop].astype(F32) + r2y[hop].astype(F32)

    def rs_third(hop):
        s3[hop] = own_sum(hop).astype(BF16)
        rs_z(hop).start()

    rs_third(1)
    ag_third(1)
    rs_third(2)
    ag_third(3)
    rs_third(3)
    wg_send[...] = own_sum(0)
    ag_third(2)

    def ig_columns(hop):
        first = ((z - hop + NZ) % NZ) * 4 * block
        return pl.ds(pl.multiple_of(first, 4 * block), 4 * block)

    def ig_copy(hop):
        columns = ig_columns(hop)
        return copy(ig_send.at[:, columns], ig_recv.at[:, columns], IG_COPY + hop, sibling)

    def ig_part(hop):
        cz = (z - hop + NZ) % NZ
        if hop:
            ag_a(hop).wait_recv()
            ag_p(hop).wait_recv()
        ag_b(hop).wait_recv()
        for cy in range(2):
            pair = chip(cz, cy, 0)
            first = pl.multiple_of(pair * block, 2 * block)
            rows = wfull[pl.ds(pair, 2)].reshape(2 * block, half)
            part = dot(val_full[...], rows, 1, 1)
            columns = pl.ds(first, 2 * block)
            top, bottom = part[:ROWS], part[ROWS:]
            ig_ref[:, columns] = jnp.where(core == 0, top, bottom)
            ig_send[:, columns] = jnp.where(core == 0, bottom, top)
        ig_copy(hop).start()

    def ig_finish(hop):
        columns = ig_columns(hop)
        ig_copy(hop).wait_recv()
        ig_ref[:, columns] += ig_recv[:, columns]

    ig_part(0)
    ig_part(1)
    ig_part(3)

    for hop in range(1, NZ):
        rs_z(hop).wait_recv()
        wg_send[...] += r3[hop].astype(F32)
    wg_send[...] = scale * wg_send[...]
    wg_copy = copy(wg_send, wg_recv, WG_COPY, sibling)
    wg_copy.start()
    wg_ref[:, own_half] = wg_send[...]

    ig_part(2)
    wg_copy.wait_recv()
    wg_ref[:, other_half] = wg_recv[...]
    for hop in (0, 1, 3, 2):
        ig_finish(hop)

    for single in (in_copy, back_copy, fwd_copy, val_copy, wg_copy):
        single.wait_send()

    for hop in range(NZ):
        for each in (ag_x, ag_y, ag_a, ag_b, rs_a, rs_b, rs_x, rs_y, ig_copy):
            each(hop).wait_send()
        if hop:
            for each in (ag_z, ag_p, rs_z):
                each(hop).wait_send()


def write_kernel(ig_ref, gate_ref, wg_ref, ig_out, gate_out, wg_out):
    ig_out[0] = ig_ref[...]
    gate_out[0] = gate_ref[...]
    wg_out[...] = wg_ref[...]


def written(in_grad, gate_grad, weight_grad):
    steps = 4
    flat = [pl.BlockSpec((a.shape[0] // steps, a.shape[1]), lambda i: (i, 0)) for a in (in_grad, gate_grad, weight_grad)]
    rows, width = in_grad.shape
    channels = gate_grad.shape[1]
    return pl.pallas_call(
        write_kernel,
        grid=(steps,),
        out_shape=(
            jax.ShapeDtypeStruct((1, rows, width), F32),
            jax.ShapeDtypeStruct((1, rows, channels), F32),
            jax.ShapeDtypeStruct(weight_grad.shape, F32),
        ),
        in_specs=flat,
        out_specs=(
            pl.BlockSpec((1, rows // steps, width), lambda i: (0, i, 0)),
            pl.BlockSpec((1, rows // steps, channels), lambda i: (0, i, 0)),
            flat[2],
        ),
    )(in_grad, gate_grad, weight_grad)


def on_chip_grid(inputs, values, gating, out_grad, weight, decay_rate, mode_gain):
    rows, width = inputs.shape[1:]
    channels = values.shape[2]
    modes = decay_rate.shape[0]
    block = weight.shape[0]
    tiles, half, mid = channels // LANES, channels // 2, block // 2
    scale = 1.0 / math.sqrt(rows * lax.axis_size("ctx") * lax.axis_size("dp"))
    vmem = pl.BlockSpec(memory_space=pltpu.VMEM)
    series = pltpu.VMEM((tiles, rows, LANES), F32)
    states = pltpu.VMEM((tiles, modes, RUNS, LANES), F32)
    ends = pltpu.VMEM((tiles, modes, LANES), F32)
    blocks = pltpu.VMEM((NZ, block, half), BF16)
    halves = pltpu.VMEM((NZ, mid, half), BF16)
    in_grad, gate_grad, weight_grad = pl.pallas_call(
        functools.partial(chip_kernel, scale),
        out_shape=(
            jax.ShapeDtypeStruct((rows, width), F32),
            jax.ShapeDtypeStruct((rows, channels), F32),
            jax.ShapeDtypeStruct((block, channels), F32),
        ),
        in_specs=[pl.BlockSpec(memory_space=pl.ANY)] * 5 + [vmem] * 2,
        out_specs=(vmem,) * 3,
        scratch_shapes=[
            pltpu.VMEM((rows, channels), BF16),
            pltpu.VMEM((rows, channels), BF16),
            pltpu.VMEM((rows, channels), BF16),
            series, series, series, pltpu.VMEM((tiles, RUN, LANES), F32), states, states,
            ends, ends, ends, ends,
            pltpu.VMEM((2 * rows, width), BF16),
            pltpu.VMEM((2 * rows, half), BF16),
            pltpu.VMEM((rows, half), BF16),
            pltpu.VMEM((width // block, block, half), BF16),
            blocks, halves, halves, blocks, blocks, blocks, blocks, blocks, blocks,
            pltpu.VMEM((rows, width), F32),
            pltpu.VMEM((rows, width), F32),
            pltpu.VMEM((block, half), F32),
            pltpu.VMEM((block, half), F32),
            pltpu.SemaphoreType.DMA((COPIES,)),
            pltpu.SemaphoreType.DMA((COPIES,)),
            pltpu.SemaphoreType.DMA((5,)),
        ],
        compiler_params=pltpu.CompilerParams(
            collective_id=0, has_side_effects=True, vmem_limit_bytes=56 * 1024 * 1024
        ),
    )(inputs[0], values[0], gating[0], out_grad[0], weight, decay_rate, mode_gain)
    return written(in_grad, gate_grad, weight_grad)


def fits_chip_grid(mesh):
    return mesh.shape["ctx"] == 2 and mesh.shape["dp"] == 4 * NZ


def passed_along(block, axis, distance):
    devices = range(lax.axis_size(axis))
    route = [(i - distance, i) for i in devices if i - distance in devices]
    return lax.ppermute(block, axis, route)


def chain_combine(earlier, later):
    return (later[0] + later[1] * earlier[0], earlier[1] * later[1])


def power_rows(decay_rate, row_count, offset):
    steps = jnp.arange(row_count, dtype=jnp.float32) + offset
    return jnp.exp(-decay_rate[None, :, :] * steps[:, None, None])


def modal_tables(decay_rate, mode_gain, block_len):
    mode_coef = mode_gain * jnp.sqrt(-jnp.expm1(-2.0 * decay_rate))
    power_table = power_rows(decay_rate, block_len, 0.0)
    impulse = jnp.sum(mode_coef[None] * power_table, axis=1)
    sum_weights = power_table[::-1]
    inject_table = mode_coef[None] * power_rows(decay_rate, block_len, 1.0)
    step_decay = jnp.exp(-decay_rate * block_len)
    return (impulse, sum_weights, inject_table, step_decay)


def local_pass(series, tables):
    impulse, sum_weights, inject_table, step_decay = tables
    block_len = impulse.shape[0]
    mode_count = sum_weights.shape[1]
    blocked = series.reshape(-1, block_len, series.shape[-1])
    within_block = impulse[0][None, None, :] * blocked
    for lag_step in range(1, block_len):
        shifted = jnp.pad(blocked[:, : block_len - lag_step], ((0, 0), (lag_step, 0), (0, 0)))
        within_block = within_block + impulse[lag_step][None, None, :] * shifted
    block_sums = jnp.zeros((blocked.shape[0], mode_count, blocked.shape[2]), jnp.float32)
    for row_step in range(block_len):
        block_sums = block_sums + sum_weights[row_step][None] * blocked[:, row_step][:, None, :]
    block_decay = jnp.broadcast_to(step_decay, block_sums.shape)
    end_state, end_decay = lax.associative_scan(chain_combine, (block_sums, block_decay), axis=0)
    return (within_block, end_state, end_decay)


def finish_pass(within_block, end_state, end_decay, incoming, inject_table):
    total_state = end_state + end_decay * incoming[None]
    prior_state = jnp.concatenate([incoming[None], total_state[:-1]], axis=0)
    carried = within_block
    for mode_step in range(inject_table.shape[1]):
        carried = carried + inject_table[:, mode_step][None] * prior_state[:, mode_step][:, None, :]
    return carried.reshape(-1, within_block.shape[-1])


def entering(fwd_own, fwd_span, back_own, back_span):
    empty_state = jnp.zeros_like(fwd_own)
    n_ctx = lax.axis_size("ctx")

    def fwd_step(step_index, loop_state):
        received = passed_along(loop_state[1], "ctx", 1)
        return (received, fwd_own + fwd_span * received)

    def back_step(step_index, loop_state):
        received = passed_along(loop_state[1], "ctx", -1)
        return (received, back_own + back_span * received)

    fwd_in = lax.fori_loop(0, n_ctx - 1, fwd_step, (empty_state, fwd_own))[0]
    back_in = lax.fori_loop(0, n_ctx - 1, back_step, (empty_state, back_own))[0]
    return (fwd_in, back_in)


def on_device(inputs, values, gating, out_grad, weight, decay_rate, mode_gain):
    in_rows = inputs[0]
    tok_rows = in_rows.shape[0]
    n_ctx = lax.axis_size("ctx")
    n_dp = lax.axis_size("dp")
    tables = modal_tables(decay_rate, mode_gain, 16)
    fwd_within, fwd_end, fwd_decay = local_pass(values[0].astype(jnp.float32), tables)
    mix_grad = gating[0].astype(jnp.float32) * out_grad[0].astype(jnp.float32)
    back_within, back_end, back_decay = local_pass(jnp.flip(mix_grad, 0), tables)
    fwd_in, back_in = entering(fwd_end[-1], fwd_decay[-1], back_end[-1], back_decay[-1])
    val_grad = jnp.flip(
        finish_pass(back_within, back_end, back_decay, back_in, tables[2]), 0
    ).astype(jnp.bfloat16)
    mixed = finish_pass(fwd_within, fwd_end, fwd_decay, fwd_in, tables[2])
    gate_grad = out_grad[0].astype(jnp.float32) * mixed
    in_grad = lax.dot_general(
        val_grad,
        lax.all_gather(weight, "dp", axis=0, tiled=True),
        (((1,), (1,)), ((), ())),
        preferred_element_type=jnp.float32,
    )
    norm_factor = 1.0 / math.sqrt(tok_rows * n_ctx * n_dp)
    share = lax.psum_scatter(
        norm_factor
        * lax.dot_general(
            in_rows, val_grad, (((0,), (0,)), ((), ())), preferred_element_type=jnp.float32
        ),
        "dp",
        scatter_dimension=0,
        tiled=True,
    )
    weight_grad = lax.psum(share, "ctx")
    return (in_grad[None], gate_grad[None], weight_grad)


def solution(mesh):
    placed = (
        P("dp", "ctx", None),
        P("dp", "ctx", None),
        P("dp", "ctx", None),
        P("dp", "ctx", None),
        P("dp", None),
        P(),
        P(),
    )
    step = on_chip_grid if fits_chip_grid(mesh) else on_device
    return jax.shard_map(
        step,
        mesh=mesh,
        in_specs=placed,
        out_specs=(P("dp", "ctx", None), P("dp", "ctx", None), P("dp", None)),
        check_vma=False,
    )
```

```python
import functools
import math

import jax
import jax.numpy as jnp
from jax import lax
from jax.experimental import pallas as pl
from jax.experimental.pallas import tpu as pltpu
from jax.sharding import PartitionSpec as P

MESH = pl.DeviceIdType.MESH
F32 = jnp.float32
BF16 = jnp.bfloat16
LANES = 128
RUN = 16
RUNS = 8
ROWS = RUN * RUNS
NZ = 4

IN_COPY, BACK_COPY, FWD_COPY, VAL_COPY, WG_COPY = range(5)
AG_Z, AG_X, AG_Y, AG_A, AG_B, RS_A, RS_B, RS_X, RS_Y, RS_Z, IG_COPY, AG_P = range(5, 53, 4)
AG_ZF, AG_PF, COPIES = range(53, 56)
WRITES = 4


def dot(lhs, rhs, lhs_dim, rhs_dim):
    return lax.dot_general(
        lhs, rhs, (((lhs_dim,), (rhs_dim,)), ((), ())), preferred_element_type=F32
    )


def own_plane(hop):
    return isinstance(hop, int) and hop == 0


def lanes_of(tile):
    return pl.ds(pl.multiple_of(tile * LANES, LANES), LANES)


def run_rows(step):
    return pl.ds(step, RUNS, RUN)


def row_index():
    return lax.broadcasted_iota(jnp.int32, (RUNS, LANES), 0)


def shifted_runs(state, by, reverse):
    rows = row_index()
    if reverse:
        return jnp.where(rows < RUNS - by, pltpu.roll(state, RUNS - by, 0), 0.0)
    return jnp.where(rows >= by, pltpu.roll(state, by, 0), 0.0)


def spread(row):
    return jnp.broadcast_to(row, (RUNS, LANES))


def one_less_exp(u):
    series = 1.0
    for order in range(8, 1, -1):
        series = 1.0 - u * (1.0 / order) * series
    return jnp.where(u > 0.25, 1.0 - jnp.exp(-u), u * series)


def modes_of(decay_ref, gain_ref, tile):
    decay = decay_ref[:, lanes_of(tile)]
    lam = jnp.exp(-decay)
    coef = gain_ref[:, lanes_of(tile)] * jnp.sqrt(one_less_exp(2.0 * decay))
    return decay, lam, coef


def in_order(reverse):
    return range(RUN - 1, -1, -1) if reverse else range(RUN)


def run_states(series, decay, lam, states, ends, tile, reverse):
    modes = range(decay.shape[0])
    rates = [spread(lam[mode : mode + 1]) for mode in modes]
    held = None
    for step in in_order(reverse):
        column = series[tile, run_rows(step), :]
        held = [column] * len(rates) if held is None else [r * h + column for r, h in zip(rates, held)]
    over_run = jnp.exp(-float(RUN) * decay)
    spans = [spread(over_run[mode : mode + 1]) for mode in modes]
    for by in (1, 2, 4):
        held = [h + s * shifted_runs(h, by, reverse) for h, s in zip(held, spans)]
        spans = [s * s for s in spans]
    last = 0 if reverse else RUNS - 1
    for mode in modes:
        states[tile, mode] = held[mode]
        ends[tile, mode : mode + 1, :] = held[mode][last : last + 1]


def added(terms):
    while len(terms) > 1:
        odd = terms[-1:] if len(terms) % 2 else []
        terms = [a + b for a, b in zip(terms[::2], terms[1::2])] + odd
    return terms[0]


def run_within(series, impulse, result, tile, reverse):
    order = list(in_order(reverse))
    steps = [series[tile, run_rows(step), :] for step in order]
    lags = [spread(impulse[tile, lag : lag + 1, :]) for lag in range(RUN)]
    for at, step in enumerate(order):
        result[tile, run_rows(step), :] = added([lags[at - b] * steps[b] for b in range(at + 1)])


def run_carried(decay, lam, coef, states, incoming, enters, result, tile, reverse):
    ahead = row_index()
    ahead = (RUNS - 1 - ahead if reverse else ahead).astype(F32) * float(RUN)
    rates, carried = [], []
    for mode in range(decay.shape[0]):
        rate = spread(lam[mode : mode + 1])
        entry = jnp.where(enters, spread(incoming[tile, mode : mode + 1, :]), 0.0)
        prior = shifted_runs(states[tile, mode], 1, reverse)
        prior = prior + jnp.exp(-ahead * spread(decay[mode : mode + 1])) * entry
        rates.append(rate)
        carried.append(spread(coef[mode : mode + 1]) * rate * prior)
    for step in in_order(reverse):
        result[tile, run_rows(step), :] += added(carried)
        carried = [rate * item for rate, item in zip(rates, carried)]


def chip_kernel(
    scale,
    in_hbm, values_hbm, gating_hbm, grad_hbm, weight_hbm, decay_ref, gain_ref,
    ig_ref, gate_ref, wg_ref,
    values_ref, gating_ref, grad_ref, series_f, series_b, result, impulse, states_f, states_b,
    ends_f, ends_b, enter_f, enter_b,
    in_full, val_full, val_send, wfull,
    s1, r1a, r1b, s2x, s2y, r2x, r2y, s3, r3,
    ig_send, ig_recv, wg_send, wg_recv,
    send_sem, recv_sem, load_sem,
):
    core = lax.axis_index("ctx")
    dp = lax.axis_index("dp")
    z, y, x = dp // 4, (dp // 2) % 2, dp % 2
    tiles = series_f.shape[0]
    half_tiles = tiles // 2
    half = half_tiles * LANES
    block = weight_hbm.shape[0]
    mid = block // 2
    cut = 3 * block // 8

    def chip(cz, cy, cx):
        return cz * 4 + cy * 2 + cx

    sibling = (1 - core, dp)
    x_dev = (core, chip(z, y, 1 - x))
    y_dev = (core, chip(z, 1 - y, x))

    def z_dev(hop):
        return (core, chip((z + hop) % NZ, y, x))

    def copy(src, dst, which, device, into=None):
        into = which if into is None else into
        return pltpu.make_async_remote_copy(
            src_ref=src, dst_ref=dst, send_sem=send_sem.at[which], recv_sem=recv_sem.at[into],
            device_id=device, device_id_type=MESH,
        )

    own_half = pl.ds(pl.multiple_of(core * half, half), half)
    other_half = pl.ds(pl.multiple_of((1 - core) * half, half), half)
    own_rows = pl.ds(pl.multiple_of(core * ROWS, ROWS), ROWS)

    def load(src, dst, which):
        return pltpu.make_async_copy(src, dst, load_sem.at[which])

    weight_load = load(weight_hbm.at[:, own_half], wfull.at[dp], 0)
    gating_load = load(gating_hbm, gating_ref, 1)
    grad_load = load(grad_hbm, grad_ref, 2)
    in_load = load(in_hbm, in_full.at[own_rows, :], 3)
    values_load = load(values_hbm, values_ref, 4)
    for each in (weight_load, gating_load, grad_load, in_load, values_load):
        each.start()

    barrier = pltpu.get_barrier_semaphore()
    partners = [sibling, x_dev, y_dev] + [z_dev(hop) for hop in range(1, NZ)]
    for device in partners:
        pl.semaphore_signal(barrier, inc=1, device_id=device, device_id_type=MESH)
    pl.semaphore_wait(barrier, len(partners))

    def wrows(index, start=0, size=block):
        return wfull.at[index, pl.ds(start, size), :]

    weight_load.wait()

    edge = (z == 0) | (z == NZ - 1)
    near = jnp.where(z == 0, 3, 1)
    second = jnp.where(edge, 2, 3)
    last = jnp.where(z == 0, 1, jnp.where(z == NZ - 1, 3, 2))

    def from_hop(hop):
        return (z - hop + NZ) % NZ

    def z_rows():
        return wrows(dp, cut, block - cut)

    def p_rows(cz):
        return wfull.at[pl.ds(cz * 4, 4), pl.ds(0, cut), :]

    def ag_z(hop):
        return copy(z_rows(), z_rows(), AG_Z + hop, z_dev(hop))

    def ag_p(hop):
        return copy(p_rows(z), p_rows(z), AG_P + hop, z_dev(hop))

    beside = (core, chip(jnp.where(z == 2, 3, 0), y, x))
    beside_hop = jnp.where(z == 2, 3, 1)

    def ag_zf():
        rows = wrows(chip(from_hop(2), y, x), cut, block - cut)
        return copy(rows, rows, AG_ZF, beside, AG_Z + beside_hop)

    def ag_pf():
        rows = p_rows(from_hop(2))
        return copy(rows, rows, AG_PF, beside, AG_P + beside_hop)

    def if_direct(hop, act):
        if hop == 2:
            act()
        else:
            pl.when(z != (NZ - 1 if hop == 1 else 0))(act)

    mid_cut = 3 * block // 4

    def whole(hop, cy, cx):
        index = chip(from_hop(hop), cy, cx)
        return wrows(index) if own_plane(hop) else wrows(index, cut, block - cut)

    def first_part(hop, cy, cx):
        index = chip(from_hop(hop), cy, cx)
        return wrows(index, 0, cut) if own_plane(hop) else wrows(index, cut, mid_cut - cut)

    def second_part(hop, cy, cx):
        index = chip(from_hop(hop), cy, cx)
        start = cut if own_plane(hop) else mid_cut
        return wrows(index, start, block - start)

    def ag_x(hop):
        rows = whole(hop, y, x)
        return copy(rows, rows, AG_X + hop, x_dev)

    def ag_y(hop):
        rows = whole(hop, y, x)
        return copy(rows, rows, AG_Y + hop, y_dev)

    def ag_a(hop):
        rows = first_part(hop, y, 1 - x)
        return copy(rows, rows, AG_A + hop, y_dev)

    def ag_b(hop):
        rows = second_part(hop, 1 - y, x)
        return copy(rows, rows, AG_B + hop, x_dev)

    def ag_second(hop):
        ag_z(hop).wait_recv()
        ag_x(hop).start()
        ag_y(hop).start()

    def ag_third(hop):
        ag_x(hop).wait_recv()
        ag_a(hop).start()
        ag_y(hop).wait_recv()
        ag_b(hop).start()

    if_direct(1, lambda: ag_z(1).start())
    if_direct(3, lambda: ag_z(3).start())
    ag_x(0).start()
    ag_y(0).start()
    in_copy = copy(in_hbm, in_full.at[own_rows, :], IN_COPY, sibling)
    in_copy.start()
    gating_load.wait()
    grad_load.wait()

    def back_states(tile, carry):
        lanes = lanes_of(tile)
        series_b[tile] = gating_ref[:, lanes].astype(F32) * grad_ref[:, lanes].astype(F32)
        decay, lam, coef = modes_of(decay_ref, gain_ref, tile)
        power = coef
        for lag in range(RUN):
            impulse[tile, lag : lag + 1, :] = jnp.sum(power, axis=0, keepdims=True)
            power = power * lam
        run_states(series_b, decay, lam, states_b, ends_b, tile, True)
        return carry

    def fwd_states(tile, carry):
        series_f[tile] = values_ref[:, lanes_of(tile)].astype(F32)
        decay, lam, coef = modes_of(decay_ref, gain_ref, tile)
        run_states(series_f, decay, lam, states_f, ends_f, tile, False)
        return carry

    lax.fori_loop(0, tiles, back_states, 0)
    back_copy = copy(ends_b, enter_b, BACK_COPY, sibling)
    back_copy.start()
    ag_z(2).start()

    def back_within(tile, carry):
        run_within(series_b, impulse, result, tile, True)
        return carry

    lax.fori_loop(0, tiles, back_within, 0)
    ag_third(0)
    ag_second(near)
    back_copy.wait_recv()

    def val_tile(tile):
        decay, lam, coef = modes_of(decay_ref, gain_ref, tile)
        run_carried(decay, lam, coef, states_b, enter_b, core == 0, result, tile, True)
        return result[tile].astype(BF16)

    def val_other(tile, carry):
        val_send[:, lanes_of(tile)] = val_tile((1 - core) * half_tiles + tile)
        return carry

    def val_own(tile, carry):
        val_full[own_rows, lanes_of(tile)] = val_tile(core * half_tiles + tile)
        return carry

    lax.fori_loop(0, half_tiles, val_other, 0)
    val_copy = copy(val_send, val_full.at[own_rows, :], VAL_COPY, sibling)
    val_copy.start()
    ag_second(second)
    lax.fori_loop(0, half_tiles, val_own, 0)
    in_load.wait()
    in_copy.wait_recv()
    val_copy.wait_recv()

    def term(index):
        columns = pl.ds(pl.multiple_of(index * block, block), block)
        return dot(in_full[:, columns], val_full[...], 0, 0)

    def rs_a(hop):
        return copy(s1.at[hop, pl.ds(0, mid), :], r1a.at[hop], RS_A + hop, y_dev)

    def rs_b(hop):
        return copy(s1.at[hop, pl.ds(mid, mid), :], r1b.at[hop], RS_B + hop, x_dev)

    def rs_x(hop):
        return copy(s2x.at[hop], r2x.at[hop], RS_X + hop, x_dev)

    def rs_y(hop):
        return copy(s2y.at[hop], r2y.at[hop], RS_Y + hop, y_dev)

    def rs_z(hop):
        return copy(s3.at[hop], r3.at[hop], RS_Z + hop, z_dev(hop))

    def rs_first(hop):
        s1[hop] = term(chip((z + hop) % NZ, 1 - y, 1 - x)).astype(BF16)
        rs_a(hop).start()
        rs_b(hop).start()

    def rs_second(hop):
        to_x = term(chip((z + hop) % NZ, y, 1 - x))
        rs_a(hop).wait_recv()
        s2x[hop, pl.ds(0, mid), :] = (to_x[:mid] + r1a[hop].astype(F32)).astype(BF16)
        s2x[hop, pl.ds(mid, mid), :] = to_x[mid:].astype(BF16)
        rs_x(hop).start()
        to_y = term(chip((z + hop) % NZ, 1 - y, x))
        rs_b(hop).wait_recv()
        s2y[hop, pl.ds(0, mid), :] = to_y[:mid].astype(BF16)
        s2y[hop, pl.ds(mid, mid), :] = (to_y[mid:] + r1b[hop].astype(F32)).astype(BF16)
        rs_y(hop).start()

    rs_first(1)
    ag_a(0).wait_recv()
    if_direct(1, lambda: ag_p(1).start())
    if_direct(3, lambda: ag_p(3).start())
    ag_p(2).start()
    for hop in (2, 3, 0):
        rs_first(hop)

    @pl.when(jnp.logical_not(edge))
    def _():
        ag_second(2)
        ag_zf().start()

    values_load.wait()
    lax.fori_loop(0, tiles, fwd_states, 0)
    fwd_copy = copy(ends_f, enter_f, FWD_COPY, sibling)
    fwd_copy.start()

    for hop in (1, 2, 3, 0):
        rs_second(hop)

    @pl.when(edge)
    def _():
        ag_second(last)

    @pl.when(jnp.logical_not(edge))
    def _():
        ag_p(2).wait_recv()
        ag_pf().start()


    fwd_copy.wait_recv()

    def gate_tile(tile, carry):
        decay, lam, coef = modes_of(decay_ref, gain_ref, tile)
        run_within(series_f, impulse, result, tile, False)
        run_carried(decay, lam, coef, states_f, enter_f, core == 1, result, tile, False)
        lanes = lanes_of(tile)
        gate_ref[:, lanes] = grad_ref[:, lanes].astype(F32) * result[tile]
        return carry

    lax.fori_loop(0, tiles, gate_tile, 0)

    def own_sum(hop):
        total = term(chip((z + hop) % NZ, y, x))
        rs_x(hop).wait_recv()
        rs_y(hop).wait_recv()
        return total + r2x[hop].astype(F32) + r2y[hop].astype(F32)

    def rs_third(hop):
        s3[hop] = own_sum(hop).astype(BF16)
        rs_z(hop).start()

    rs_third(1)
    ag_third(near)
    rs_third(2)
    ag_third(second)
    rs_third(3)
    wg_send[...] = own_sum(0)
    ag_third(last)

    def ig_columns(hop):
        first = ((z - hop + NZ) % NZ) * 4 * block
        return pl.ds(pl.multiple_of(first, 4 * block), 4 * block)

    def ig_copy(hop):
        columns = ig_columns(hop)
        return copy(ig_send.at[:, columns], ig_recv.at[:, columns], IG_COPY + hop, sibling)

    def ig_part(hop):
        cz = (z - hop + NZ) % NZ
        if not own_plane(hop):
            ag_a(hop).wait_recv()
            pl.when(edge | (hop != 2))(lambda: ag_p(hop).wait_recv())
        ag_b(hop).wait_recv()
        for cy in range(2):
            pair = chip(cz, cy, 0)
            first = pl.multiple_of(pair * block, 2 * block)
            rows = wfull[pl.ds(pair, 2)].reshape(2 * block, half)
            part = dot(val_full[...], rows, 1, 1)
            columns = pl.ds(first, 2 * block)
            top, bottom = part[:ROWS], part[ROWS:]
            ig_ref[:, columns] = jnp.where(core == 0, top, bottom)
            ig_send[:, columns] = jnp.where(core == 0, bottom, top)
        ig_copy(hop).start()

    def ig_finish(hop):
        columns = ig_columns(hop)
        ig_copy(hop).wait_recv()
        ig_ref[:, columns] += ig_recv[:, columns]

    ig_part(0)
    ig_part(near)
    ig_part(second)

    for hop in range(1, NZ):
        rs_z(hop).wait_recv()
        wg_send[...] += r3[hop].astype(F32)
    wg_send[...] = scale * wg_send[...]
    wg_copy = copy(wg_send, wg_recv, WG_COPY, sibling)
    wg_copy.start()
    wg_ref[:, own_half] = wg_send[...]

    ig_part(last)
    wg_copy.wait_recv()
    wg_ref[:, other_half] = wg_recv[...]
    for hop in (0, near, second, last):
        ig_finish(hop)

    for single in (in_copy, back_copy, fwd_copy, val_copy, wg_copy):
        single.wait_send()

    for hop in range(NZ):
        for each in (ag_x, ag_y, ag_a, ag_b, rs_a, rs_b, rs_x, rs_y, ig_copy):
            each(hop).wait_send()
        if hop:
            rs_z(hop).wait_send()
            if_direct(hop, lambda: ag_z(hop).wait_send())
            if_direct(hop, lambda: ag_p(hop).wait_send())

    @pl.when(jnp.logical_not(edge))
    def _():
        ag_zf().wait_send()
        ag_pf().wait_send()


def write_kernel(ig_ref, gate_ref, wg_ref, ig_out, gate_out, wg_out, sems):
    pairs = ((ig_ref, ig_out.at[0]), (gate_ref, gate_out.at[0]), (wg_ref, wg_out))
    moves = []
    for which, (src, dst) in enumerate(pairs):
        part = src.shape[0] // WRITES
        for at in range(WRITES):
            rows = pl.ds(at * part, part)
            sem = sems.at[which * WRITES + at]
            moves.append(pltpu.make_async_copy(src.at[rows, :], dst.at[rows, :], sem))
    for move in moves:
        move.start()
    for move in moves:
        move.wait()


def written(in_grad, gate_grad, weight_grad):
    anywhere = pl.BlockSpec(memory_space=pl.ANY)
    return pl.pallas_call(
        write_kernel,
        out_shape=(
            jax.ShapeDtypeStruct((1,) + in_grad.shape, F32),
            jax.ShapeDtypeStruct((1,) + gate_grad.shape, F32),
            jax.ShapeDtypeStruct(weight_grad.shape, F32),
        ),
        in_specs=[anywhere] * 3,
        out_specs=(anywhere,) * 3,
        scratch_shapes=[pltpu.SemaphoreType.DMA((3 * WRITES,))],
    )(in_grad, gate_grad, weight_grad)


def on_chip_grid(inputs, values, gating, out_grad, weight, decay_rate, mode_gain):
    rows, width = inputs.shape[1:]
    channels = values.shape[2]
    modes = decay_rate.shape[0]
    block = weight.shape[0]
    tiles, half, mid = channels // LANES, channels // 2, block // 2
    scale = 1.0 / math.sqrt(rows * lax.axis_size("ctx") * lax.axis_size("dp"))
    vmem = pl.BlockSpec(memory_space=pltpu.VMEM)
    series = pltpu.VMEM((tiles, rows, LANES), F32)
    states = pltpu.VMEM((tiles, modes, RUNS, LANES), F32)
    ends = pltpu.VMEM((tiles, modes, LANES), F32)
    blocks = pltpu.VMEM((NZ, block, half), BF16)
    halves = pltpu.VMEM((NZ, mid, half), BF16)
    in_grad, gate_grad, weight_grad = pl.pallas_call(
        functools.partial(chip_kernel, scale),
        out_shape=(
            jax.ShapeDtypeStruct((rows, width), F32),
            jax.ShapeDtypeStruct((rows, channels), F32),
            jax.ShapeDtypeStruct((block, channels), F32),
        ),
        in_specs=[pl.BlockSpec(memory_space=pl.ANY)] * 5 + [vmem] * 2,
        out_specs=(vmem,) * 3,
        scratch_shapes=[
            pltpu.VMEM((rows, channels), BF16),
            pltpu.VMEM((rows, channels), BF16),
            pltpu.VMEM((rows, channels), BF16),
            series, series, series, pltpu.VMEM((tiles, RUN, LANES), F32), states, states,
            ends, ends, ends, ends,
            pltpu.VMEM((2 * rows, width), BF16),
            pltpu.VMEM((2 * rows, half), BF16),
            pltpu.VMEM((rows, half), BF16),
            pltpu.VMEM((width // block, block, half), BF16),
            blocks, halves, halves, blocks, blocks, blocks, blocks, blocks, blocks,
            pltpu.VMEM((rows, width), F32),
            pltpu.VMEM((rows, width), F32),
            pltpu.VMEM((block, half), F32),
            pltpu.VMEM((block, half), F32),
            pltpu.SemaphoreType.DMA((COPIES,)),
            pltpu.SemaphoreType.DMA((COPIES,)),
            pltpu.SemaphoreType.DMA((5,)),
        ],
        compiler_params=pltpu.CompilerParams(
            collective_id=0, has_side_effects=True, vmem_limit_bytes=40 * 1024 * 1024
        ),
    )(inputs[0], values[0], gating[0], out_grad[0], weight, decay_rate, mode_gain)
    return written(in_grad, gate_grad, weight_grad)


def fits_chip_grid(mesh):
    return mesh.shape["ctx"] == 2 and mesh.shape["dp"] == 4 * NZ


def passed_along(block, axis, distance):
    devices = range(lax.axis_size(axis))
    route = [(i - distance, i) for i in devices if i - distance in devices]
    return lax.ppermute(block, axis, route)


def chain_combine(earlier, later):
    return (later[0] + later[1] * earlier[0], earlier[1] * later[1])


def power_rows(decay_rate, row_count, offset):
    steps = jnp.arange(row_count, dtype=jnp.float32) + offset
    return jnp.exp(-decay_rate[None, :, :] * steps[:, None, None])


def modal_tables(decay_rate, mode_gain, block_len):
    mode_coef = mode_gain * jnp.sqrt(-jnp.expm1(-2.0 * decay_rate))
    power_table = power_rows(decay_rate, block_len, 0.0)
    impulse = jnp.sum(mode_coef[None] * power_table, axis=1)
    sum_weights = power_table[::-1]
    inject_table = mode_coef[None] * power_rows(decay_rate, block_len, 1.0)
    step_decay = jnp.exp(-decay_rate * block_len)
    return (impulse, sum_weights, inject_table, step_decay)


def local_pass(series, tables):
    impulse, sum_weights, inject_table, step_decay = tables
    block_len = impulse.shape[0]
    mode_count = sum_weights.shape[1]
    blocked = series.reshape(-1, block_len, series.shape[-1])
    within_block = impulse[0][None, None, :] * blocked
    for lag_step in range(1, block_len):
        shifted = jnp.pad(blocked[:, : block_len - lag_step], ((0, 0), (lag_step, 0), (0, 0)))
        within_block = within_block + impulse[lag_step][None, None, :] * shifted
    block_sums = jnp.zeros((blocked.shape[0], mode_count, blocked.shape[2]), jnp.float32)
    for row_step in range(block_len):
        block_sums = block_sums + sum_weights[row_step][None] * blocked[:, row_step][:, None, :]
    block_decay = jnp.broadcast_to(step_decay, block_sums.shape)
    end_state, end_decay = lax.associative_scan(chain_combine, (block_sums, block_decay), axis=0)
    return (within_block, end_state, end_decay)


def finish_pass(within_block, end_state, end_decay, incoming, inject_table):
    total_state = end_state + end_decay * incoming[None]
    prior_state = jnp.concatenate([incoming[None], total_state[:-1]], axis=0)
    carried = within_block
    for mode_step in range(inject_table.shape[1]):
        carried = carried + inject_table[:, mode_step][None] * prior_state[:, mode_step][:, None, :]
    return carried.reshape(-1, within_block.shape[-1])


def entering(fwd_own, fwd_span, back_own, back_span):
    empty_state = jnp.zeros_like(fwd_own)
    n_ctx = lax.axis_size("ctx")

    def fwd_step(step_index, loop_state):
        received = passed_along(loop_state[1], "ctx", 1)
        return (received, fwd_own + fwd_span * received)

    def back_step(step_index, loop_state):
        received = passed_along(loop_state[1], "ctx", -1)
        return (received, back_own + back_span * received)

    fwd_in = lax.fori_loop(0, n_ctx - 1, fwd_step, (empty_state, fwd_own))[0]
    back_in = lax.fori_loop(0, n_ctx - 1, back_step, (empty_state, back_own))[0]
    return (fwd_in, back_in)


def on_device(inputs, values, gating, out_grad, weight, decay_rate, mode_gain):
    in_rows = inputs[0]
    tok_rows = in_rows.shape[0]
    n_ctx = lax.axis_size("ctx")
    n_dp = lax.axis_size("dp")
    tables = modal_tables(decay_rate, mode_gain, 16)
    fwd_within, fwd_end, fwd_decay = local_pass(values[0].astype(jnp.float32), tables)
    mix_grad = gating[0].astype(jnp.float32) * out_grad[0].astype(jnp.float32)
    back_within, back_end, back_decay = local_pass(jnp.flip(mix_grad, 0), tables)
    fwd_in, back_in = entering(fwd_end[-1], fwd_decay[-1], back_end[-1], back_decay[-1])
    val_grad = jnp.flip(
        finish_pass(back_within, back_end, back_decay, back_in, tables[2]), 0
    ).astype(jnp.bfloat16)
    mixed = finish_pass(fwd_within, fwd_end, fwd_decay, fwd_in, tables[2])
    gate_grad = out_grad[0].astype(jnp.float32) * mixed
    in_grad = lax.dot_general(
        val_grad,
        lax.all_gather(weight, "dp", axis=0, tiled=True),
        (((1,), (1,)), ((), ())),
        preferred_element_type=jnp.float32,
    )
    norm_factor = 1.0 / math.sqrt(tok_rows * n_ctx * n_dp)
    share = lax.psum_scatter(
        norm_factor
        * lax.dot_general(
            in_rows, val_grad, (((0,), (0,)), ((), ())), preferred_element_type=jnp.float32
        ),
        "dp",
        scatter_dimension=0,
        tiled=True,
    )
    weight_grad = lax.psum(share, "ctx")
    return (in_grad[None], gate_grad[None], weight_grad)


def solution(mesh):
    placed = (
        P("dp", "ctx", None),
        P("dp", "ctx", None),
        P("dp", "ctx", None),
        P("dp", "ctx", None),
        P("dp", None),
        P(),
        P(),
    )
    step = on_chip_grid if fits_chip_grid(mesh) else on_device
    return jax.shard_map(
        step,
        mesh=mesh,
        in_specs=placed,
        out_specs=(P("dp", "ctx", None), P("dp", "ctx", None), P("dp", None)),
        check_vma=False,
    )
```

```python
import functools
import math

import jax
import jax.numpy as jnp
from jax import lax
from jax.experimental import pallas as pl
from jax.experimental.pallas import tpu as pltpu
from jax.sharding import PartitionSpec as P

MESH = pl.DeviceIdType.MESH
F32 = jnp.float32
BF16 = jnp.bfloat16
LANES = 128
RUN = 16
RUNS = 8
ROWS = RUN * RUNS
NZ = 4

IN_COPY, BACK_COPY, FWD_COPY, VAL_COPY, WG_COPY = range(5)
AG_Z, AG_X, AG_Y, AG_A, AG_B, RS_A, RS_B, RS_X, RS_Y, RS_Z, IG_COPY, AG_P = range(5, 53, 4)
AG_ZF, AG_PF, COPIES = range(53, 56)
WRITES = 4


def dot(lhs, rhs, lhs_dim, rhs_dim):
    return lax.dot_general(
        lhs, rhs, (((lhs_dim,), (rhs_dim,)), ((), ())), preferred_element_type=F32
    )


def own_plane(hop):
    return isinstance(hop, int) and hop == 0


def lanes_of(tile):
    return pl.ds(pl.multiple_of(tile * LANES, LANES), LANES)


def run_rows(step):
    return pl.ds(step, RUNS, RUN)


def row_index():
    return lax.broadcasted_iota(jnp.int32, (RUNS, LANES), 0)


def shifted_runs(state, by, reverse):
    rows = row_index()
    if reverse:
        return jnp.where(rows < RUNS - by, pltpu.roll(state, RUNS - by, 0), 0.0)
    return jnp.where(rows >= by, pltpu.roll(state, by, 0), 0.0)


def spread(row):
    return jnp.broadcast_to(row, (RUNS, LANES))


def one_less_exp(u):
    series = 1.0
    for order in range(8, 1, -1):
        series = 1.0 - u * (1.0 / order) * series
    return jnp.where(u > 0.25, 1.0 - jnp.exp(-u), u * series)


def modes_of(decay_ref, gain_ref, tile):
    decay = decay_ref[:, lanes_of(tile)]
    lam = jnp.exp(-decay)
    coef = gain_ref[:, lanes_of(tile)] * jnp.sqrt(one_less_exp(2.0 * decay))
    return decay, lam, coef


def in_order(reverse):
    return range(RUN - 1, -1, -1) if reverse else range(RUN)


def run_states(series, decay, lam, states, ends, tile, reverse):
    modes = range(decay.shape[0])
    rates = [spread(lam[mode : mode + 1]) for mode in modes]
    held = None
    for step in in_order(reverse):
        column = series[tile, run_rows(step), :]
        held = [column] * len(rates) if held is None else [r * h + column for r, h in zip(rates, held)]
    over_run = jnp.exp(-float(RUN) * decay)
    spans = [spread(over_run[mode : mode + 1]) for mode in modes]
    for by in (1, 2, 4):
        held = [h + s * shifted_runs(h, by, reverse) for h, s in zip(held, spans)]
        spans = [s * s for s in spans]
    last = 0 if reverse else RUNS - 1
    for mode in modes:
        states[tile, mode] = held[mode]
        ends[tile, mode : mode + 1, :] = held[mode][last : last + 1]


def added(terms):
    while len(terms) > 1:
        odd = terms[-1:] if len(terms) % 2 else []
        terms = [a + b for a, b in zip(terms[::2], terms[1::2])] + odd
    return terms[0]


def run_within(series, impulse, result, tile, reverse):
    order = list(in_order(reverse))
    steps = [series[tile, run_rows(step), :] for step in order]
    lags = [spread(impulse[tile, lag : lag + 1, :]) for lag in range(RUN)]
    for at, step in enumerate(order):
        result[tile, run_rows(step), :] = added([lags[at - b] * steps[b] for b in range(at + 1)])


def run_carried(decay, lam, coef, states, incoming, enters, result, tile, reverse):
    ahead = row_index()
    ahead = (RUNS - 1 - ahead if reverse else ahead).astype(F32) * float(RUN)
    rates, carried = [], []
    for mode in range(decay.shape[0]):
        rate = spread(lam[mode : mode + 1])
        entry = jnp.where(enters, spread(incoming[tile, mode : mode + 1, :]), 0.0)
        prior = shifted_runs(states[tile, mode], 1, reverse)
        prior = prior + jnp.exp(-ahead * spread(decay[mode : mode + 1])) * entry
        rates.append(rate)
        carried.append(spread(coef[mode : mode + 1]) * rate * prior)
    for step in in_order(reverse):
        result[tile, run_rows(step), :] += added(carried)
        carried = [rate * item for rate, item in zip(rates, carried)]


def chip_kernel(
    scale,
    in_hbm, values_hbm, gating_hbm, grad_hbm, weight_hbm, decay_ref, gain_ref,
    ig_hbm, gate_hbm, wg_hbm,
    ig_ref, gate_ref, wg_ref, values_ref, gating_ref, grad_ref, series_f, series_b, result, impulse, states_f, states_b,
    ends_f, ends_b, enter_f, enter_b,
    in_full, val_full, val_send, wfull,
    s1, r1a, r1b, s2x, s2y, r2x, r2y, s3, r3,
    ig_send, ig_recv, wg_send, wg_recv,
    send_sem, recv_sem, load_sem, store_sem,
):
    core = lax.axis_index("ctx")
    dp = lax.axis_index("dp")
    z, y, x = dp // 4, (dp // 2) % 2, dp % 2
    tiles = series_f.shape[0]
    half_tiles = tiles // 2
    half = half_tiles * LANES
    block = weight_hbm.shape[0]
    mid = block // 2
    cut = 3 * block // 8

    def chip(cz, cy, cx):
        return cz * 4 + cy * 2 + cx

    sibling = (1 - core, dp)
    x_dev = (core, chip(z, y, 1 - x))
    y_dev = (core, chip(z, 1 - y, x))

    def z_dev(hop):
        return (core, chip((z + hop) % NZ, y, x))

    def copy(src, dst, which, device, into=None):
        into = which if into is None else into
        return pltpu.make_async_remote_copy(
            src_ref=src, dst_ref=dst, send_sem=send_sem.at[which], recv_sem=recv_sem.at[into],
            device_id=device, device_id_type=MESH,
        )

    own_half = pl.ds(pl.multiple_of(core * half, half), half)
    other_half = pl.ds(pl.multiple_of((1 - core) * half, half), half)
    own_rows = pl.ds(pl.multiple_of(core * ROWS, ROWS), ROWS)

    def load(src, dst, which):
        return pltpu.make_async_copy(src, dst, load_sem.at[which])

    weight_load = load(weight_hbm.at[:, own_half], wfull.at[dp], 0)
    gating_load = load(gating_hbm, gating_ref, 1)
    grad_load = load(grad_hbm, grad_ref, 2)
    in_load = load(in_hbm, in_full.at[own_rows, :], 3)
    values_load = load(values_hbm, values_ref, 4)
    for each in (weight_load, gating_load, grad_load, in_load, values_load):
        each.start()

    barrier = pltpu.get_barrier_semaphore()
    partners = [sibling, x_dev, y_dev] + [z_dev(hop) for hop in range(1, NZ)]
    for device in partners:
        pl.semaphore_signal(barrier, inc=1, device_id=device, device_id_type=MESH)
    pl.semaphore_wait(barrier, len(partners))

    def wrows(index, start=0, size=block):
        return wfull.at[index, pl.ds(start, size), :]

    weight_load.wait()

    edge = (z == 0) | (z == NZ - 1)
    near = jnp.where(z == 0, 3, 1)
    second = jnp.where(edge, 2, 3)
    last = jnp.where(z == 0, 1, jnp.where(z == NZ - 1, 3, 2))

    def from_hop(hop):
        return (z - hop + NZ) % NZ

    def z_rows():
        return wrows(dp, cut, block - cut)

    def p_rows(cz):
        return wfull.at[pl.ds(cz * 4, 4), pl.ds(0, cut), :]

    def ag_z(hop):
        return copy(z_rows(), z_rows(), AG_Z + hop, z_dev(hop))

    def ag_p(hop):
        return copy(p_rows(z), p_rows(z), AG_P + hop, z_dev(hop))

    beside = (core, chip(jnp.where(z == 2, 3, 0), y, x))
    beside_hop = jnp.where(z == 2, 3, 1)

    def ag_zf():
        rows = wrows(chip(from_hop(2), y, x), cut, block - cut)
        return copy(rows, rows, AG_ZF, beside, AG_Z + beside_hop)

    def ag_pf():
        rows = p_rows(from_hop(2))
        return copy(rows, rows, AG_PF, beside, AG_P + beside_hop)

    def if_direct(hop, act):
        if hop == 2:
            act()
        else:
            pl.when(z != (NZ - 1 if hop == 1 else 0))(act)

    mid_cut = 3 * block // 4

    def whole(hop, cy, cx):
        index = chip(from_hop(hop), cy, cx)
        return wrows(index) if own_plane(hop) else wrows(index, cut, block - cut)

    def first_part(hop, cy, cx):
        index = chip(from_hop(hop), cy, cx)
        return wrows(index, 0, cut) if own_plane(hop) else wrows(index, cut, mid_cut - cut)

    def second_part(hop, cy, cx):
        index = chip(from_hop(hop), cy, cx)
        start = cut if own_plane(hop) else mid_cut
        return wrows(index, start, block - start)

    def ag_x(hop):
        rows = whole(hop, y, x)
        return copy(rows, rows, AG_X + hop, x_dev)

    def ag_y(hop):
        rows = whole(hop, y, x)
        return copy(rows, rows, AG_Y + hop, y_dev)

    def ag_a(hop):
        rows = first_part(hop, y, 1 - x)
        return copy(rows, rows, AG_A + hop, y_dev)

    def ag_b(hop):
        rows = second_part(hop, 1 - y, x)
        return copy(rows, rows, AG_B + hop, x_dev)

    def ag_second(hop):
        ag_z(hop).wait_recv()
        ag_x(hop).start()
        ag_y(hop).start()

    def ag_third(hop):
        ag_x(hop).wait_recv()
        ag_a(hop).start()
        ag_y(hop).wait_recv()
        ag_b(hop).start()

    if_direct(1, lambda: ag_z(1).start())
    if_direct(3, lambda: ag_z(3).start())
    ag_x(0).start()
    ag_y(0).start()
    in_copy = copy(in_hbm, in_full.at[own_rows, :], IN_COPY, sibling)
    in_copy.start()
    gating_load.wait()
    grad_load.wait()

    def back_states(tile, carry):
        lanes = lanes_of(tile)
        series_b[tile] = gating_ref[:, lanes].astype(F32) * grad_ref[:, lanes].astype(F32)
        decay, lam, coef = modes_of(decay_ref, gain_ref, tile)
        power = coef
        for lag in range(RUN):
            impulse[tile, lag : lag + 1, :] = jnp.sum(power, axis=0, keepdims=True)
            power = power * lam
        run_states(series_b, decay, lam, states_b, ends_b, tile, True)
        return carry

    def fwd_states(tile, carry):
        series_f[tile] = values_ref[:, lanes_of(tile)].astype(F32)
        decay, lam, coef = modes_of(decay_ref, gain_ref, tile)
        run_states(series_f, decay, lam, states_f, ends_f, tile, False)
        return carry

    lax.fori_loop(0, tiles, back_states, 0)
    back_copy = copy(ends_b, enter_b, BACK_COPY, sibling)
    back_copy.start()
    ag_z(2).start()

    def back_within(tile, carry):
        run_within(series_b, impulse, result, tile, True)
        return carry

    lax.fori_loop(0, tiles, back_within, 0)
    ag_third(0)
    ag_second(near)
    back_copy.wait_recv()

    def val_tile(tile):
        decay, lam, coef = modes_of(decay_ref, gain_ref, tile)
        run_carried(decay, lam, coef, states_b, enter_b, core == 0, result, tile, True)
        return result[tile].astype(BF16)

    def val_other(tile, carry):
        val_send[:, lanes_of(tile)] = val_tile((1 - core) * half_tiles + tile)
        return carry

    def val_own(tile, carry):
        val_full[own_rows, lanes_of(tile)] = val_tile(core * half_tiles + tile)
        return carry

    lax.fori_loop(0, half_tiles, val_other, 0)
    val_copy = copy(val_send, val_full.at[own_rows, :], VAL_COPY, sibling)
    val_copy.start()
    ag_second(second)
    lax.fori_loop(0, half_tiles, val_own, 0)
    in_load.wait()
    in_copy.wait_recv()
    val_copy.wait_recv()

    def term(index):
        columns = pl.ds(pl.multiple_of(index * block, block), block)
        return dot(in_full[:, columns], val_full[...], 0, 0)

    def rs_a(hop):
        return copy(s1.at[hop, pl.ds(0, mid), :], r1a.at[hop], RS_A + hop, y_dev)

    def rs_b(hop):
        return copy(s1.at[hop, pl.ds(mid, mid), :], r1b.at[hop], RS_B + hop, x_dev)

    def rs_x(hop):
        return copy(s2x.at[hop], r2x.at[hop], RS_X + hop, x_dev)

    def rs_y(hop):
        return copy(s2y.at[hop], r2y.at[hop], RS_Y + hop, y_dev)

    def rs_z(hop):
        return copy(s3.at[hop], r3.at[hop], RS_Z + hop, z_dev(hop))

    def rs_first(hop):
        s1[hop] = term(chip((z + hop) % NZ, 1 - y, 1 - x)).astype(BF16)
        rs_a(hop).start()
        rs_b(hop).start()

    def rs_second(hop):
        to_x = term(chip((z + hop) % NZ, y, 1 - x))
        rs_a(hop).wait_recv()
        s2x[hop, pl.ds(0, mid), :] = (to_x[:mid] + r1a[hop].astype(F32)).astype(BF16)
        s2x[hop, pl.ds(mid, mid), :] = to_x[mid:].astype(BF16)
        rs_x(hop).start()
        to_y = term(chip((z + hop) % NZ, 1 - y, x))
        rs_b(hop).wait_recv()
        s2y[hop, pl.ds(0, mid), :] = to_y[:mid].astype(BF16)
        s2y[hop, pl.ds(mid, mid), :] = (to_y[mid:] + r1b[hop].astype(F32)).astype(BF16)
        rs_y(hop).start()

    rs_first(1)
    ag_a(0).wait_recv()
    if_direct(1, lambda: ag_p(1).start())
    if_direct(3, lambda: ag_p(3).start())
    ag_p(2).start()
    for hop in (2, 3, 0):
        rs_first(hop)

    @pl.when(jnp.logical_not(edge))
    def _():
        ag_second(2)
        ag_zf().start()

    values_load.wait()
    lax.fori_loop(0, tiles, fwd_states, 0)
    fwd_copy = copy(ends_f, enter_f, FWD_COPY, sibling)
    fwd_copy.start()

    for hop in (1, 2, 3, 0):
        rs_second(hop)

    @pl.when(edge)
    def _():
        ag_second(last)

    @pl.when(jnp.logical_not(edge))
    def _():
        ag_p(2).wait_recv()
        ag_pf().start()


    fwd_copy.wait_recv()

    def gate_tile(tile, carry):
        decay, lam, coef = modes_of(decay_ref, gain_ref, tile)
        run_within(series_f, impulse, result, tile, False)
        run_carried(decay, lam, coef, states_f, enter_f, core == 1, result, tile, False)
        lanes = lanes_of(tile)
        gate_ref[:, lanes] = grad_ref[:, lanes].astype(F32) * result[tile]
        return carry

    lax.fori_loop(0, tiles, gate_tile, 0)
    gate_store = pltpu.make_async_copy(gate_ref, gate_hbm, store_sem.at[0])
    gate_store.start()

    def own_sum(hop):
        total = term(chip((z + hop) % NZ, y, x))
        rs_x(hop).wait_recv()
        rs_y(hop).wait_recv()
        return total + r2x[hop].astype(F32) + r2y[hop].astype(F32)

    def rs_third(hop):
        s3[hop] = own_sum(hop).astype(BF16)
        rs_z(hop).start()

    rs_third(1)
    ag_third(near)
    rs_third(2)
    ag_third(second)
    rs_third(3)
    wg_send[...] = own_sum(0)
    ag_third(last)

    def ig_columns(hop):
        first = ((z - hop + NZ) % NZ) * 4 * block
        return pl.ds(pl.multiple_of(first, 4 * block), 4 * block)

    def ig_copy(hop):
        columns = ig_columns(hop)
        return copy(ig_send.at[:, columns], ig_recv.at[:, columns], IG_COPY + hop, sibling)

    def ig_part(hop):
        cz = (z - hop + NZ) % NZ
        if not own_plane(hop):
            ag_a(hop).wait_recv()
            pl.when(edge | (hop != 2))(lambda: ag_p(hop).wait_recv())
        ag_b(hop).wait_recv()
        for cy in range(2):
            pair = chip(cz, cy, 0)
            first = pl.multiple_of(pair * block, 2 * block)
            rows = wfull[pl.ds(pair, 2)].reshape(2 * block, half)
            part = dot(val_full[...], rows, 1, 1)
            columns = pl.ds(first, 2 * block)
            top, bottom = part[:ROWS], part[ROWS:]
            ig_ref[:, columns] = jnp.where(core == 0, top, bottom)
            ig_send[:, columns] = jnp.where(core == 0, bottom, top)
        ig_copy(hop).start()

    def ig_finish(hop):
        columns = ig_columns(hop)
        ig_copy(hop).wait_recv()
        ig_ref[:, columns] += ig_recv[:, columns]

    def ig_store(at, hop):
        columns = ig_columns(hop)
        src, dst = ig_ref.at[:, columns], ig_hbm.at[:, columns]
        return pltpu.make_async_copy(src, dst, store_sem.at[2 + at])

    ig_part(0)
    ig_part(near)
    ig_part(second)

    for hop in range(1, NZ):
        rs_z(hop).wait_recv()
        wg_send[...] += r3[hop].astype(F32)
    wg_send[...] = scale * wg_send[...]
    wg_copy = copy(wg_send, wg_recv, WG_COPY, sibling)
    wg_copy.start()
    wg_ref[:, own_half] = wg_send[...]

    ig_part(last)
    wg_copy.wait_recv()
    wg_ref[:, other_half] = wg_recv[...]
    wg_store = pltpu.make_async_copy(wg_ref, wg_hbm, store_sem.at[1])
    wg_store.start()
    for at, hop in enumerate((0, near, second, last)):
        ig_finish(hop)
        ig_store(at, hop).start()

    gate_store.wait()
    wg_store.wait()
    for at, hop in enumerate((0, near, second, last)):
        ig_store(at, hop).wait()
    for single in (in_copy, back_copy, fwd_copy, val_copy, wg_copy):
        single.wait_send()

    for hop in range(NZ):
        for each in (ag_x, ag_y, ag_a, ag_b, rs_a, rs_b, rs_x, rs_y, ig_copy):
            each(hop).wait_send()
        if hop:
            rs_z(hop).wait_send()
            if_direct(hop, lambda: ag_z(hop).wait_send())
            if_direct(hop, lambda: ag_p(hop).wait_send())

    @pl.when(jnp.logical_not(edge))
    def _():
        ag_zf().wait_send()
        ag_pf().wait_send()


def write_kernel(ig_ref, gate_ref, wg_ref, ig_out, gate_out, wg_out, held, sems):
    pairs = ((gate_ref, gate_out.at[0]), (wg_ref, wg_out), (ig_ref, ig_out.at[0]))
    reads, writes = [], []
    for which, (src, dst) in enumerate(pairs):
        part = src.shape[0] // WRITES
        for at in range(WRITES):
            rows = pl.ds(at * part, part)
            stage = held.at[which, rows, :]
            index = which * WRITES + at
            reads.append(pltpu.make_async_copy(src.at[rows, :], stage, sems.at[0, index]))
            writes.append(pltpu.make_async_copy(stage, dst.at[rows, :], sems.at[1, index]))
    for read in reads:
        read.start()
    for read, write in zip(reads, writes):
        read.wait()
        write.start()
    for write in writes:
        write.wait()


def written(in_grad, gate_grad, weight_grad):
    anywhere = pl.BlockSpec(memory_space=pl.ANY)
    return pl.pallas_call(
        write_kernel,
        out_shape=(
            jax.ShapeDtypeStruct((1,) + in_grad.shape, F32),
            jax.ShapeDtypeStruct((1,) + gate_grad.shape, F32),
            jax.ShapeDtypeStruct(weight_grad.shape, F32),
        ),
        in_specs=[anywhere] * 3,
        out_specs=(anywhere,) * 3,
        scratch_shapes=[
            pltpu.VMEM((3,) + in_grad.shape, F32),
            pltpu.SemaphoreType.DMA((2, 3 * WRITES)),
        ],
    )(in_grad, gate_grad, weight_grad)


def on_chip_grid(inputs, values, gating, out_grad, weight, decay_rate, mode_gain):
    rows, width = inputs.shape[1:]
    channels = values.shape[2]
    modes = decay_rate.shape[0]
    block = weight.shape[0]
    tiles, half, mid = channels // LANES, channels // 2, block // 2
    scale = 1.0 / math.sqrt(rows * lax.axis_size("ctx") * lax.axis_size("dp"))
    vmem = pl.BlockSpec(memory_space=pltpu.VMEM)
    series = pltpu.VMEM((tiles, rows, LANES), F32)
    states = pltpu.VMEM((tiles, modes, RUNS, LANES), F32)
    ends = pltpu.VMEM((tiles, modes, LANES), F32)
    blocks = pltpu.VMEM((NZ, block, half), BF16)
    halves = pltpu.VMEM((NZ, mid, half), BF16)
    in_grad, gate_grad, weight_grad = pl.pallas_call(
        functools.partial(chip_kernel, scale),
        out_shape=(
            jax.ShapeDtypeStruct((rows, width), F32),
            jax.ShapeDtypeStruct((rows, channels), F32),
            jax.ShapeDtypeStruct((block, channels), F32),
        ),
        in_specs=[pl.BlockSpec(memory_space=pl.ANY)] * 5 + [vmem] * 2,
        out_specs=(pl.BlockSpec(memory_space=pl.ANY),) * 3,
        scratch_shapes=[
            pltpu.VMEM((rows, width), F32),
            pltpu.VMEM((rows, channels), F32),
            pltpu.VMEM((block, channels), F32),
            pltpu.VMEM((rows, channels), BF16),
            pltpu.VMEM((rows, channels), BF16),
            pltpu.VMEM((rows, channels), BF16),
            series, series, series, pltpu.VMEM((tiles, RUN, LANES), F32), states, states,
            ends, ends, ends, ends,
            pltpu.VMEM((2 * rows, width), BF16),
            pltpu.VMEM((2 * rows, half), BF16),
            pltpu.VMEM((rows, half), BF16),
            pltpu.VMEM((width // block, block, half), BF16),
            blocks, halves, halves, blocks, blocks, blocks, blocks, blocks, blocks,
            pltpu.VMEM((rows, width), F32),
            pltpu.VMEM((rows, width), F32),
            pltpu.VMEM((block, half), F32),
            pltpu.VMEM((block, half), F32),
            pltpu.SemaphoreType.DMA((COPIES,)),
            pltpu.SemaphoreType.DMA((COPIES,)),
            pltpu.SemaphoreType.DMA((5,)),
            pltpu.SemaphoreType.DMA((2 + NZ,)),
        ],
        compiler_params=pltpu.CompilerParams(
            collective_id=0, has_side_effects=True, vmem_limit_bytes=56 * 1024 * 1024
        ),
    )(inputs[0], values[0], gating[0], out_grad[0], weight, decay_rate, mode_gain)
    return written(in_grad, gate_grad, weight_grad)


def fits_chip_grid(mesh):
    return mesh.shape["ctx"] == 2 and mesh.shape["dp"] == 4 * NZ


def passed_along(block, axis, distance):
    devices = range(lax.axis_size(axis))
    route = [(i - distance, i) for i in devices if i - distance in devices]
    return lax.ppermute(block, axis, route)


def chain_combine(earlier, later):
    return (later[0] + later[1] * earlier[0], earlier[1] * later[1])


def power_rows(decay_rate, row_count, offset):
    steps = jnp.arange(row_count, dtype=jnp.float32) + offset
    return jnp.exp(-decay_rate[None, :, :] * steps[:, None, None])


def modal_tables(decay_rate, mode_gain, block_len):
    mode_coef = mode_gain * jnp.sqrt(-jnp.expm1(-2.0 * decay_rate))
    power_table = power_rows(decay_rate, block_len, 0.0)
    impulse = jnp.sum(mode_coef[None] * power_table, axis=1)
    sum_weights = power_table[::-1]
    inject_table = mode_coef[None] * power_rows(decay_rate, block_len, 1.0)
    step_decay = jnp.exp(-decay_rate * block_len)
    return (impulse, sum_weights, inject_table, step_decay)


def local_pass(series, tables):
    impulse, sum_weights, inject_table, step_decay = tables
    block_len = impulse.shape[0]
    mode_count = sum_weights.shape[1]
    blocked = series.reshape(-1, block_len, series.shape[-1])
    within_block = impulse[0][None, None, :] * blocked
    for lag_step in range(1, block_len):
        shifted = jnp.pad(blocked[:, : block_len - lag_step], ((0, 0), (lag_step, 0), (0, 0)))
        within_block = within_block + impulse[lag_step][None, None, :] * shifted
    block_sums = jnp.zeros((blocked.shape[0], mode_count, blocked.shape[2]), jnp.float32)
    for row_step in range(block_len):
        block_sums = block_sums + sum_weights[row_step][None] * blocked[:, row_step][:, None, :]
    block_decay = jnp.broadcast_to(step_decay, block_sums.shape)
    end_state, end_decay = lax.associative_scan(chain_combine, (block_sums, block_decay), axis=0)
    return (within_block, end_state, end_decay)


def finish_pass(within_block, end_state, end_decay, incoming, inject_table):
    total_state = end_state + end_decay * incoming[None]
    prior_state = jnp.concatenate([incoming[None], total_state[:-1]], axis=0)
    carried = within_block
    for mode_step in range(inject_table.shape[1]):
        carried = carried + inject_table[:, mode_step][None] * prior_state[:, mode_step][:, None, :]
    return carried.reshape(-1, within_block.shape[-1])


def entering(fwd_own, fwd_span, back_own, back_span):
    empty_state = jnp.zeros_like(fwd_own)
    n_ctx = lax.axis_size("ctx")

    def fwd_step(step_index, loop_state):
        received = passed_along(loop_state[1], "ctx", 1)
        return (received, fwd_own + fwd_span * received)

    def back_step(step_index, loop_state):
        received = passed_along(loop_state[1], "ctx", -1)
        return (received, back_own + back_span * received)

    fwd_in = lax.fori_loop(0, n_ctx - 1, fwd_step, (empty_state, fwd_own))[0]
    back_in = lax.fori_loop(0, n_ctx - 1, back_step, (empty_state, back_own))[0]
    return (fwd_in, back_in)


def on_device(inputs, values, gating, out_grad, weight, decay_rate, mode_gain):
    in_rows = inputs[0]
    tok_rows = in_rows.shape[0]
    n_ctx = lax.axis_size("ctx")
    n_dp = lax.axis_size("dp")
    tables = modal_tables(decay_rate, mode_gain, 16)
    fwd_within, fwd_end, fwd_decay = local_pass(values[0].astype(jnp.float32), tables)
    mix_grad = gating[0].astype(jnp.float32) * out_grad[0].astype(jnp.float32)
    back_within, back_end, back_decay = local_pass(jnp.flip(mix_grad, 0), tables)
    fwd_in, back_in = entering(fwd_end[-1], fwd_decay[-1], back_end[-1], back_decay[-1])
    val_grad = jnp.flip(
        finish_pass(back_within, back_end, back_decay, back_in, tables[2]), 0
    ).astype(jnp.bfloat16)
    mixed = finish_pass(fwd_within, fwd_end, fwd_decay, fwd_in, tables[2])
    gate_grad = out_grad[0].astype(jnp.float32) * mixed
    in_grad = lax.dot_general(
        val_grad,
        lax.all_gather(weight, "dp", axis=0, tiled=True),
        (((1,), (1,)), ((), ())),
        preferred_element_type=jnp.float32,
    )
    norm_factor = 1.0 / math.sqrt(tok_rows * n_ctx * n_dp)
    share = lax.psum_scatter(
        norm_factor
        * lax.dot_general(
            in_rows, val_grad, (((0,), (0,)), ((), ())), preferred_element_type=jnp.float32
        ),
        "dp",
        scatter_dimension=0,
        tiled=True,
    )
    weight_grad = lax.psum(share, "ctx")
    return (in_grad[None], gate_grad[None], weight_grad)


def solution(mesh):
    placed = (
        P("dp", "ctx", None),
        P("dp", "ctx", None),
        P("dp", "ctx", None),
        P("dp", "ctx", None),
        P("dp", None),
        P(),
        P(),
    )
    step = on_chip_grid if fits_chip_grid(mesh) else on_device
    return jax.shard_map(
        step,
        mesh=mesh,
        in_specs=placed,
        out_specs=(P("dp", "ctx", None), P("dp", "ctx", None), P("dp", None)),
        check_vma=False,
    )
```

```python
import functools
import math

import jax
import jax.numpy as jnp
from jax import lax
from jax.experimental import pallas as pl
from jax.experimental.pallas import tpu as pltpu
from jax.sharding import PartitionSpec as P

MESH = pl.DeviceIdType.MESH
F32 = jnp.float32
BF16 = jnp.bfloat16
LANES = 128
RUN = 16
RUNS = 8
ROWS = RUN * RUNS
NZ = 4

IN_COPY, BACK_COPY, FWD_COPY, VAL_COPY, WG_COPY = range(5)
AG_Z, AG_X, AG_Y, AG_A, AG_B, RS_A, RS_B, RS_X, RS_Y, RS_Z, IG_COPY, AG_P = range(5, 53, 4)
AG_ZF, AG_PF, COPIES = range(53, 56)
WRITES = 4


def dot(lhs, rhs, lhs_dim, rhs_dim):
    return lax.dot_general(
        lhs, rhs, (((lhs_dim,), (rhs_dim,)), ((), ())), preferred_element_type=F32
    )


def own_plane(hop):
    return isinstance(hop, int) and hop == 0


def lanes_of(tile):
    return pl.ds(pl.multiple_of(tile * LANES, LANES), LANES)


def run_rows(step):
    return pl.ds(step, RUNS, RUN)


def row_index():
    return lax.broadcasted_iota(jnp.int32, (RUNS, LANES), 0)


def shifted_runs(state, by, reverse):
    rows = row_index()
    if reverse:
        return jnp.where(rows < RUNS - by, pltpu.roll(state, RUNS - by, 0), 0.0)
    return jnp.where(rows >= by, pltpu.roll(state, by, 0), 0.0)


def spread(row):
    return jnp.broadcast_to(row, (RUNS, LANES))


def one_less_exp(u):
    series = 1.0
    for order in range(8, 1, -1):
        series = 1.0 - u * (1.0 / order) * series
    return jnp.where(u > 0.25, 1.0 - jnp.exp(-u), u * series)


def modes_of(decay_ref, gain_ref, tile):
    decay = decay_ref[:, lanes_of(tile)]
    lam = jnp.exp(-decay)
    coef = gain_ref[:, lanes_of(tile)] * jnp.sqrt(one_less_exp(2.0 * decay))
    return decay, lam, coef


def in_order(reverse):
    return range(RUN - 1, -1, -1) if reverse else range(RUN)


def run_states(series, decay, lam, states, ends, tile, reverse):
    modes = range(decay.shape[0])
    rates = [spread(lam[mode : mode + 1]) for mode in modes]
    held = None
    for step in in_order(reverse):
        column = series[tile, run_rows(step), :]
        held = [column] * len(rates) if held is None else [r * h + column for r, h in zip(rates, held)]
    over_run = jnp.exp(-float(RUN) * decay)
    spans = [spread(over_run[mode : mode + 1]) for mode in modes]
    for by in (1, 2, 4):
        held = [h + s * shifted_runs(h, by, reverse) for h, s in zip(held, spans)]
        spans = [s * s for s in spans]
    last = 0 if reverse else RUNS - 1
    for mode in modes:
        states[tile, mode] = held[mode]
        ends[tile, mode : mode + 1, :] = held[mode][last : last + 1]


def added(terms):
    while len(terms) > 1:
        odd = terms[-1:] if len(terms) % 2 else []
        terms = [a + b for a, b in zip(terms[::2], terms[1::2])] + odd
    return terms[0]


def run_within(series, impulse, result, tile, reverse):
    order = list(in_order(reverse))
    steps = [series[tile, run_rows(step), :] for step in order]
    lags = [spread(impulse[tile, lag : lag + 1, :]) for lag in range(RUN)]
    for at, step in enumerate(order):
        result[tile, run_rows(step), :] = added([lags[at - b] * steps[b] for b in range(at + 1)])


def run_carried(decay, lam, coef, states, incoming, enters, result, tile, reverse):
    ahead = row_index()
    ahead = (RUNS - 1 - ahead if reverse else ahead).astype(F32) * float(RUN)
    rates, carried = [], []
    for mode in range(decay.shape[0]):
        rate = spread(lam[mode : mode + 1])
        entry = jnp.where(enters, spread(incoming[tile, mode : mode + 1, :]), 0.0)
        prior = shifted_runs(states[tile, mode], 1, reverse)
        prior = prior + jnp.exp(-ahead * spread(decay[mode : mode + 1])) * entry
        rates.append(rate)
        carried.append(spread(coef[mode : mode + 1]) * rate * prior)
    for step in in_order(reverse):
        result[tile, run_rows(step), :] += added(carried)
        carried = [rate * item for rate, item in zip(rates, carried)]


def chip_kernel(
    scale,
    in_hbm, values_hbm, gating_hbm, grad_hbm, weight_hbm, decay_ref, gain_ref,
    ig_hbm, gate_hbm, wg_hbm,
    ig_ref, gate_ref, wg_ref, values_ref, gating_ref, grad_ref, series_f, series_b, result, impulse, states_f, states_b,
    ends_f, ends_b, enter_f, enter_b,
    in_full, val_full, val_send, wfull,
    s1, r1a, r1b, s2x, s2y, r2x, r2y, s3, r3,
    ig_send, ig_recv, wg_send, wg_recv,
    send_sem, recv_sem, load_sem, store_sem,
):
    core = lax.axis_index("ctx")
    dp = lax.axis_index("dp")
    z, y, x = dp // 4, (dp // 2) % 2, dp % 2
    tiles = series_f.shape[0]
    half_tiles = tiles // 2
    half = half_tiles * LANES
    block = weight_hbm.shape[0]
    mid = block // 2
    cut = 3 * block // 8

    def chip(cz, cy, cx):
        return cz * 4 + cy * 2 + cx

    sibling = (1 - core, dp)
    x_dev = (core, chip(z, y, 1 - x))
    y_dev = (core, chip(z, 1 - y, x))

    def z_dev(hop):
        return (core, chip((z + hop) % NZ, y, x))

    def copy(src, dst, which, device, into=None):
        into = which if into is None else into
        return pltpu.make_async_remote_copy(
            src_ref=src, dst_ref=dst, send_sem=send_sem.at[which], recv_sem=recv_sem.at[into],
            device_id=device, device_id_type=MESH,
        )

    own_half = pl.ds(pl.multiple_of(core * half, half), half)
    other_half = pl.ds(pl.multiple_of((1 - core) * half, half), half)
    own_rows = pl.ds(pl.multiple_of(core * ROWS, ROWS), ROWS)

    def load(src, dst, which):
        return pltpu.make_async_copy(src, dst, load_sem.at[which])

    weight_load = load(weight_hbm.at[:, own_half], wfull.at[dp], 0)
    gating_load = load(gating_hbm, gating_ref, 1)
    grad_load = load(grad_hbm, grad_ref, 2)
    in_load = load(in_hbm, in_full.at[own_rows, :], 3)
    values_load = load(values_hbm, values_ref, 4)
    for each in (weight_load, gating_load, grad_load, in_load, values_load):
        each.start()

    barrier = pltpu.get_barrier_semaphore()
    partners = [sibling, x_dev, y_dev] + [z_dev(hop) for hop in range(1, NZ)]
    for device in partners:
        pl.semaphore_signal(barrier, inc=1, device_id=device, device_id_type=MESH)
    pl.semaphore_wait(barrier, len(partners))

    def wrows(index, start=0, size=block):
        return wfull.at[index, pl.ds(start, size), :]

    weight_load.wait()

    edge = (z == 0) | (z == NZ - 1)
    near = jnp.where(z == 0, 3, 1)
    second = jnp.where(edge, 2, 3)
    last = jnp.where(z == 0, 1, jnp.where(z == NZ - 1, 3, 2))

    def from_hop(hop):
        return (z - hop + NZ) % NZ

    def z_rows():
        return wrows(dp, cut, block - cut)

    def p_rows(cz):
        return wfull.at[pl.ds(cz * 4, 4), pl.ds(0, cut), :]

    def ag_z(hop):
        return copy(z_rows(), z_rows(), AG_Z + hop, z_dev(hop))

    def ag_p(hop):
        return copy(p_rows(z), p_rows(z), AG_P + hop, z_dev(hop))

    beside = (core, chip(jnp.where(z == 2, 3, 0), y, x))
    beside_hop = jnp.where(z == 2, 3, 1)

    def ag_zf():
        rows = wrows(chip(from_hop(2), y, x), cut, block - cut)
        return copy(rows, rows, AG_ZF, beside, AG_Z + beside_hop)

    def ag_pf():
        rows = p_rows(from_hop(2))
        return copy(rows, rows, AG_PF, beside, AG_P + beside_hop)

    def if_direct(hop, act):
        if hop == 2:
            act()
        else:
            pl.when(z != (NZ - 1 if hop == 1 else 0))(act)

    mid_cut = 3 * block // 4

    def whole(hop, cy, cx):
        index = chip(from_hop(hop), cy, cx)
        return wrows(index) if own_plane(hop) else wrows(index, cut, block - cut)

    def first_part(hop, cy, cx):
        index = chip(from_hop(hop), cy, cx)
        return wrows(index, 0, cut) if own_plane(hop) else wrows(index, cut, mid_cut - cut)

    def second_part(hop, cy, cx):
        index = chip(from_hop(hop), cy, cx)
        start = cut if own_plane(hop) else mid_cut
        return wrows(index, start, block - start)

    def ag_x(hop):
        rows = whole(hop, y, x)
        return copy(rows, rows, AG_X + hop, x_dev)

    def ag_y(hop):
        rows = whole(hop, y, x)
        return copy(rows, rows, AG_Y + hop, y_dev)

    def ag_a(hop):
        rows = first_part(hop, y, 1 - x)
        return copy(rows, rows, AG_A + hop, y_dev)

    def ag_b(hop):
        rows = second_part(hop, 1 - y, x)
        return copy(rows, rows, AG_B + hop, x_dev)

    def ag_second(hop):
        ag_z(hop).wait_recv()
        ag_x(hop).start()
        ag_y(hop).start()

    def ag_third(hop):
        ag_x(hop).wait_recv()
        ag_a(hop).start()
        ag_y(hop).wait_recv()
        ag_b(hop).start()

    if_direct(1, lambda: ag_z(1).start())
    if_direct(3, lambda: ag_z(3).start())
    ag_x(0).start()
    ag_y(0).start()
    in_copy = copy(in_hbm, in_full.at[own_rows, :], IN_COPY, sibling)
    in_copy.start()
    gating_load.wait()
    grad_load.wait()

    def back_states(tile, carry):
        lanes = lanes_of(tile)
        series_b[tile] = gating_ref[:, lanes].astype(F32) * grad_ref[:, lanes].astype(F32)
        decay, lam, coef = modes_of(decay_ref, gain_ref, tile)
        power = coef
        for lag in range(RUN):
            impulse[tile, lag : lag + 1, :] = jnp.sum(power, axis=0, keepdims=True)
            power = power * lam
        run_states(series_b, decay, lam, states_b, ends_b, tile, True)
        return carry

    def fwd_states(tile, carry):
        series_f[tile] = values_ref[:, lanes_of(tile)].astype(F32)
        decay, lam, coef = modes_of(decay_ref, gain_ref, tile)
        run_states(series_f, decay, lam, states_f, ends_f, tile, False)
        return carry

    lax.fori_loop(0, tiles, back_states, 0)
    back_copy = copy(ends_b, enter_b, BACK_COPY, sibling)
    back_copy.start()
    ag_z(2).start()

    def back_within(tile, carry):
        run_within(series_b, impulse, result, tile, True)
        return carry

    lax.fori_loop(0, tiles, back_within, 0)
    ag_third(0)
    ag_second(near)
    back_copy.wait_recv()

    def val_tile(tile):
        decay, lam, coef = modes_of(decay_ref, gain_ref, tile)
        run_carried(decay, lam, coef, states_b, enter_b, core == 0, result, tile, True)
        return result[tile].astype(BF16)

    def val_other(tile, carry):
        val_send[:, lanes_of(tile)] = val_tile((1 - core) * half_tiles + tile)
        return carry

    def val_own(tile, carry):
        val_full[own_rows, lanes_of(tile)] = val_tile(core * half_tiles + tile)
        return carry

    lax.fori_loop(0, half_tiles, val_other, 0)
    val_copy = copy(val_send, val_full.at[own_rows, :], VAL_COPY, sibling)
    val_copy.start()
    ag_second(second)
    lax.fori_loop(0, half_tiles, val_own, 0)
    in_load.wait()
    in_copy.wait_recv()
    val_copy.wait_recv()

    def term(index):
        columns = pl.ds(pl.multiple_of(index * block, block), block)
        return dot(in_full[:, columns], val_full[...], 0, 0)

    def rs_a(hop):
        return copy(s1.at[hop, pl.ds(0, mid), :], r1a.at[hop], RS_A + hop, y_dev)

    def rs_b(hop):
        return copy(s1.at[hop, pl.ds(mid, mid), :], r1b.at[hop], RS_B + hop, x_dev)

    def rs_x(hop):
        return copy(s2x.at[hop], r2x.at[hop], RS_X + hop, x_dev)

    def rs_y(hop):
        return copy(s2y.at[hop], r2y.at[hop], RS_Y + hop, y_dev)

    def rs_z(hop):
        return copy(s3.at[hop], r3.at[hop], RS_Z + hop, z_dev(hop))

    def rs_first(hop):
        s1[hop] = term(chip((z + hop) % NZ, 1 - y, 1 - x)).astype(BF16)
        rs_a(hop).start()
        rs_b(hop).start()

    def rs_second(hop):
        to_x = term(chip((z + hop) % NZ, y, 1 - x))
        rs_a(hop).wait_recv()
        s2x[hop, pl.ds(0, mid), :] = (to_x[:mid] + r1a[hop].astype(F32)).astype(BF16)
        s2x[hop, pl.ds(mid, mid), :] = to_x[mid:].astype(BF16)
        rs_x(hop).start()
        to_y = term(chip((z + hop) % NZ, 1 - y, x))
        rs_b(hop).wait_recv()
        s2y[hop, pl.ds(0, mid), :] = to_y[:mid].astype(BF16)
        s2y[hop, pl.ds(mid, mid), :] = (to_y[mid:] + r1b[hop].astype(F32)).astype(BF16)
        rs_y(hop).start()

    rs_first(1)
    ag_a(0).wait_recv()
    if_direct(1, lambda: ag_p(1).start())
    if_direct(3, lambda: ag_p(3).start())
    ag_p(2).start()
    for hop in (2, 3, 0):
        rs_first(hop)

    @pl.when(jnp.logical_not(edge))
    def _():
        ag_second(2)
        ag_zf().start()

    values_load.wait()
    lax.fori_loop(0, tiles, fwd_states, 0)
    fwd_copy = copy(ends_f, enter_f, FWD_COPY, sibling)
    fwd_copy.start()

    for hop in (1, 2, 3, 0):
        rs_second(hop)

    @pl.when(edge)
    def _():
        ag_second(last)

    @pl.when(jnp.logical_not(edge))
    def _():
        ag_p(2).wait_recv()
        ag_pf().start()


    fwd_copy.wait_recv()

    def gate_tile(tile, carry):
        decay, lam, coef = modes_of(decay_ref, gain_ref, tile)
        run_within(series_f, impulse, result, tile, False)
        run_carried(decay, lam, coef, states_f, enter_f, core == 1, result, tile, False)
        lanes = lanes_of(tile)
        gate_ref[:, lanes] = grad_ref[:, lanes].astype(F32) * result[tile]
        return carry

    lax.fori_loop(0, tiles, gate_tile, 0)
    gate_store = pltpu.make_async_copy(gate_ref, gate_hbm, store_sem.at[0])
    gate_store.start()

    def own_sum(hop):
        total = term(chip((z + hop) % NZ, y, x))
        rs_x(hop).wait_recv()
        rs_y(hop).wait_recv()
        return total + r2x[hop].astype(F32) + r2y[hop].astype(F32)

    def rs_third(hop):
        s3[hop] = own_sum(hop).astype(BF16)
        rs_z(hop).start()

    rs_third(1)
    ag_third(near)
    rs_third(2)
    ag_third(second)
    rs_third(3)
    ag_third(last)
    wg_send[...] = own_sum(0)

    def ig_columns(hop):
        first = ((z - hop + NZ) % NZ) * 4 * block
        return pl.ds(pl.multiple_of(first, 4 * block), 4 * block)

    def ig_copy(hop):
        columns = ig_columns(hop)
        return copy(ig_send.at[:, columns], ig_recv.at[:, columns], IG_COPY + hop, sibling)

    def ig_part(hop):
        cz = (z - hop + NZ) % NZ
        if not own_plane(hop):
            ag_a(hop).wait_recv()
            pl.when(edge | (hop != 2))(lambda: ag_p(hop).wait_recv())
        ag_b(hop).wait_recv()
        for cy in range(2):
            pair = chip(cz, cy, 0)
            first = pl.multiple_of(pair * block, 2 * block)
            rows = wfull[pl.ds(pair, 2)].reshape(2 * block, half)
            part = dot(val_full[...], rows, 1, 1)
            columns = pl.ds(first, 2 * block)
            top, bottom = part[:ROWS], part[ROWS:]
            ig_ref[:, columns] = jnp.where(core == 0, top, bottom)
            ig_send[:, columns] = jnp.where(core == 0, bottom, top)
        ig_copy(hop).start()

    def ig_finish(hop):
        columns = ig_columns(hop)
        ig_copy(hop).wait_recv()
        ig_ref[:, columns] += ig_recv[:, columns]

    def ig_store(at, hop):
        columns = ig_columns(hop)
        src, dst = ig_ref.at[:, columns], ig_hbm.at[:, columns]
        return pltpu.make_async_copy(src, dst, store_sem.at[2 + at])

    ig_part(0)
    ig_part(near)
    ig_part(second)

    for hop in range(1, NZ):
        rs_z(hop).wait_recv()
        wg_send[...] += r3[hop].astype(F32)
    wg_send[...] = scale * wg_send[...]
    wg_copy = copy(wg_send, wg_recv, WG_COPY, sibling)
    wg_copy.start()
    wg_ref[:, own_half] = wg_send[...]

    ig_part(last)
    wg_copy.wait_recv()
    wg_ref[:, other_half] = wg_recv[...]
    wg_store = pltpu.make_async_copy(wg_ref, wg_hbm, store_sem.at[1])
    wg_store.start()
    for at, hop in enumerate((0, near, second, last)):
        ig_finish(hop)
        ig_store(at, hop).start()

    gate_store.wait()
    wg_store.wait()
    for at, hop in enumerate((0, near, second, last)):
        ig_store(at, hop).wait()
    for single in (in_copy, back_copy, fwd_copy, val_copy, wg_copy):
        single.wait_send()

    for hop in range(NZ):
        for each in (ag_x, ag_y, ag_a, ag_b, rs_a, rs_b, rs_x, rs_y, ig_copy):
            each(hop).wait_send()
        if hop:
            rs_z(hop).wait_send()
            if_direct(hop, lambda: ag_z(hop).wait_send())
            if_direct(hop, lambda: ag_p(hop).wait_send())

    @pl.when(jnp.logical_not(edge))
    def _():
        ag_zf().wait_send()
        ag_pf().wait_send()


def write_kernel(ig_ref, gate_ref, wg_ref, ig_out, gate_out, wg_out, held, sems):
    pairs = ((gate_ref, gate_out.at[0]), (wg_ref, wg_out), (ig_ref, ig_out.at[0]))
    reads, writes = [], []
    for which, (src, dst) in enumerate(pairs):
        part = src.shape[0] // WRITES
        for at in range(WRITES):
            rows = pl.ds(at * part, part)
            stage = held.at[which, rows, :]
            index = which * WRITES + at
            reads.append(pltpu.make_async_copy(src.at[rows, :], stage, sems.at[0, index]))
            writes.append(pltpu.make_async_copy(stage, dst.at[rows, :], sems.at[1, index]))
    for read in reads:
        read.start()
    for read, write in zip(reads, writes):
        read.wait()
        write.start()
    for write in writes:
        write.wait()


def written(in_grad, gate_grad, weight_grad):
    anywhere = pl.BlockSpec(memory_space=pl.ANY)
    return pl.pallas_call(
        write_kernel,
        out_shape=(
            jax.ShapeDtypeStruct((1,) + in_grad.shape, F32),
            jax.ShapeDtypeStruct((1,) + gate_grad.shape, F32),
            jax.ShapeDtypeStruct(weight_grad.shape, F32),
        ),
        in_specs=[anywhere] * 3,
        out_specs=(anywhere,) * 3,
        scratch_shapes=[
            pltpu.VMEM((3,) + in_grad.shape, F32),
            pltpu.SemaphoreType.DMA((2, 3 * WRITES)),
        ],
    )(in_grad, gate_grad, weight_grad)


def on_chip_grid(inputs, values, gating, out_grad, weight, decay_rate, mode_gain):
    rows, width = inputs.shape[1:]
    channels = values.shape[2]
    modes = decay_rate.shape[0]
    block = weight.shape[0]
    tiles, half, mid = channels // LANES, channels // 2, block // 2
    scale = 1.0 / math.sqrt(rows * lax.axis_size("ctx") * lax.axis_size("dp"))
    vmem = pl.BlockSpec(memory_space=pltpu.VMEM)
    series = pltpu.VMEM((tiles, rows, LANES), F32)
    states = pltpu.VMEM((tiles, modes, RUNS, LANES), F32)
    ends = pltpu.VMEM((tiles, modes, LANES), F32)
    blocks = pltpu.VMEM((NZ, block, half), BF16)
    halves = pltpu.VMEM((NZ, mid, half), BF16)
    in_grad, gate_grad, weight_grad = pl.pallas_call(
        functools.partial(chip_kernel, scale),
        out_shape=(
            jax.ShapeDtypeStruct((rows, width), F32),
            jax.ShapeDtypeStruct((rows, channels), F32),
            jax.ShapeDtypeStruct((block, channels), F32),
        ),
        in_specs=[pl.BlockSpec(memory_space=pl.ANY)] * 5 + [vmem] * 2,
        out_specs=(pl.BlockSpec(memory_space=pl.ANY),) * 3,
        scratch_shapes=[
            pltpu.VMEM((rows, width), F32),
            pltpu.VMEM((rows, channels), F32),
            pltpu.VMEM((block, channels), F32),
            pltpu.VMEM((rows, channels), BF16),
            pltpu.VMEM((rows, channels), BF16),
            pltpu.VMEM((rows, channels), BF16),
            series, series, series, pltpu.VMEM((tiles, RUN, LANES), F32), states, states,
            ends, ends, ends, ends,
            pltpu.VMEM((2 * rows, width), BF16),
            pltpu.VMEM((2 * rows, half), BF16),
            pltpu.VMEM((rows, half), BF16),
            pltpu.VMEM((width // block, block, half), BF16),
            blocks, halves, halves, blocks, blocks, blocks, blocks, blocks, blocks,
            pltpu.VMEM((rows, width), F32),
            pltpu.VMEM((rows, width), F32),
            pltpu.VMEM((block, half), F32),
            pltpu.VMEM((block, half), F32),
            pltpu.SemaphoreType.DMA((COPIES,)),
            pltpu.SemaphoreType.DMA((COPIES,)),
            pltpu.SemaphoreType.DMA((5,)),
            pltpu.SemaphoreType.DMA((2 + NZ,)),
        ],
        compiler_params=pltpu.CompilerParams(
            collective_id=0, has_side_effects=True, vmem_limit_bytes=56 * 1024 * 1024
        ),
    )(inputs[0], values[0], gating[0], out_grad[0], weight, decay_rate, mode_gain)
    return written(in_grad, gate_grad, weight_grad)


def fits_chip_grid(mesh):
    return mesh.shape["ctx"] == 2 and mesh.shape["dp"] == 4 * NZ


def passed_along(block, axis, distance):
    devices = range(lax.axis_size(axis))
    route = [(i - distance, i) for i in devices if i - distance in devices]
    return lax.ppermute(block, axis, route)


def chain_combine(earlier, later):
    return (later[0] + later[1] * earlier[0], earlier[1] * later[1])


def power_rows(decay_rate, row_count, offset):
    steps = jnp.arange(row_count, dtype=jnp.float32) + offset
    return jnp.exp(-decay_rate[None, :, :] * steps[:, None, None])


def modal_tables(decay_rate, mode_gain, block_len):
    mode_coef = mode_gain * jnp.sqrt(-jnp.expm1(-2.0 * decay_rate))
    power_table = power_rows(decay_rate, block_len, 0.0)
    impulse = jnp.sum(mode_coef[None] * power_table, axis=1)
    sum_weights = power_table[::-1]
    inject_table = mode_coef[None] * power_rows(decay_rate, block_len, 1.0)
    step_decay = jnp.exp(-decay_rate * block_len)
    return (impulse, sum_weights, inject_table, step_decay)


def local_pass(series, tables):
    impulse, sum_weights, inject_table, step_decay = tables
    block_len = impulse.shape[0]
    mode_count = sum_weights.shape[1]
    blocked = series.reshape(-1, block_len, series.shape[-1])
    within_block = impulse[0][None, None, :] * blocked
    for lag_step in range(1, block_len):
        shifted = jnp.pad(blocked[:, : block_len - lag_step], ((0, 0), (lag_step, 0), (0, 0)))
        within_block = within_block + impulse[lag_step][None, None, :] * shifted
    block_sums = jnp.zeros((blocked.shape[0], mode_count, blocked.shape[2]), jnp.float32)
    for row_step in range(block_len):
        block_sums = block_sums + sum_weights[row_step][None] * blocked[:, row_step][:, None, :]
    block_decay = jnp.broadcast_to(step_decay, block_sums.shape)
    end_state, end_decay = lax.associative_scan(chain_combine, (block_sums, block_decay), axis=0)
    return (within_block, end_state, end_decay)


def finish_pass(within_block, end_state, end_decay, incoming, inject_table):
    total_state = end_state + end_decay * incoming[None]
    prior_state = jnp.concatenate([incoming[None], total_state[:-1]], axis=0)
    carried = within_block
    for mode_step in range(inject_table.shape[1]):
        carried = carried + inject_table[:, mode_step][None] * prior_state[:, mode_step][:, None, :]
    return carried.reshape(-1, within_block.shape[-1])


def entering(fwd_own, fwd_span, back_own, back_span):
    empty_state = jnp.zeros_like(fwd_own)
    n_ctx = lax.axis_size("ctx")

    def fwd_step(step_index, loop_state):
        received = passed_along(loop_state[1], "ctx", 1)
        return (received, fwd_own + fwd_span * received)

    def back_step(step_index, loop_state):
        received = passed_along(loop_state[1], "ctx", -1)
        return (received, back_own + back_span * received)

    fwd_in = lax.fori_loop(0, n_ctx - 1, fwd_step, (empty_state, fwd_own))[0]
    back_in = lax.fori_loop(0, n_ctx - 1, back_step, (empty_state, back_own))[0]
    return (fwd_in, back_in)


def on_device(inputs, values, gating, out_grad, weight, decay_rate, mode_gain):
    in_rows = inputs[0]
    tok_rows = in_rows.shape[0]
    n_ctx = lax.axis_size("ctx")
    n_dp = lax.axis_size("dp")
    tables = modal_tables(decay_rate, mode_gain, 16)
    fwd_within, fwd_end, fwd_decay = local_pass(values[0].astype(jnp.float32), tables)
    mix_grad = gating[0].astype(jnp.float32) * out_grad[0].astype(jnp.float32)
    back_within, back_end, back_decay = local_pass(jnp.flip(mix_grad, 0), tables)
    fwd_in, back_in = entering(fwd_end[-1], fwd_decay[-1], back_end[-1], back_decay[-1])
    val_grad = jnp.flip(
        finish_pass(back_within, back_end, back_decay, back_in, tables[2]), 0
    ).astype(jnp.bfloat16)
    mixed = finish_pass(fwd_within, fwd_end, fwd_decay, fwd_in, tables[2])
    gate_grad = out_grad[0].astype(jnp.float32) * mixed
    in_grad = lax.dot_general(
        val_grad,
        lax.all_gather(weight, "dp", axis=0, tiled=True),
        (((1,), (1,)), ((), ())),
        preferred_element_type=jnp.float32,
    )
    norm_factor = 1.0 / math.sqrt(tok_rows * n_ctx * n_dp)
    share = lax.psum_scatter(
        norm_factor
        * lax.dot_general(
            in_rows, val_grad, (((0,), (0,)), ((), ())), preferred_element_type=jnp.float32
        ),
        "dp",
        scatter_dimension=0,
        tiled=True,
    )
    weight_grad = lax.psum(share, "ctx")
    return (in_grad[None], gate_grad[None], weight_grad)


def solution(mesh):
    placed = (
        P("dp", "ctx", None),
        P("dp", "ctx", None),
        P("dp", "ctx", None),
        P("dp", "ctx", None),
        P("dp", None),
        P(),
        P(),
    )
    step = on_chip_grid if fits_chip_grid(mesh) else on_device
    return jax.shard_map(
        step,
        mesh=mesh,
        in_specs=placed,
        out_specs=(P("dp", "ctx", None), P("dp", "ctx", None), P("dp", None)),
        check_vma=False,
    )
```
